32 devices in a mesh: row: 4 (over y, x), col: 8 (over z, core).
Axes of the slice: x: 2, y: 2, z: 4, core: 2. Of those that a mesh axis runs over, the one named last changes fastest.
Arguments:
- child_rhs: bfloat16 [1536, 128, 128], P(('row', 'col')), may hold values from -6 to 6
- parent_rhs: bfloat16 [8, 128, 128], P('col'), may hold values from -6 to 6
- child_lower_inv: bfloat16 [1536, 128, 128], P(('row', 'col')), may hold values from -0.5 to 0.5
- child_lower_off: bfloat16 [1536, 128, 128], P(('row', 'col')), may hold values from -0.125 to 0.125
- child_upper_inv: bfloat16 [1536, 128, 128], P(('row', 'col')), may hold values from -0.5 to 0.5
- child_upper_off: bfloat16 [1536, 128, 128], P(('row', 'col')), may hold values from -0.25 to 0.25
- parent_lower_inv: bfloat16 [8, 128, 128], P('col'), may hold values from -0.5 to 0.5
- parent_upper_inv: bfloat16 [8, 128, 128], P('col'), may hold values from -0.5 to 0.5
- parent_of: int32 [1536], P(('row', 'col')), may hold values from 0 to 7
Outputs:
- child_solution: bfloat16 [1536, 128, 128], P(('row', 'col'))
- parent_solution: bfloat16 [8, 128, 128], P('col')
The draws below stay inside these ranges and needn't reach their ends.
Inputs may be any that keep to these rules, and one draw needn't show every extreme that they name: `parent_of`: each lower-level supernode names one upper-level parent.
All inputs are finite; a program needn't handle non-finite values.
Results may differ from the reference program's by a relative error of at most 0.0095.
Values may be sent and summed in bfloat16 or wider, within the bound.
No kernel may reach another device: no remote copies, remote signals or barrier semaphores. Data moves between devices by JAX's collectives and lax.ppermute only.
A program may use at most 64 MiB of HBM per device.

```python
import math
import jax
import jax.numpy as jnp
import numpy as np
from jax import lax

W = 128
R = 128
CH_DEV = 48
NP = 8
NC = 1536


def touch_ends(array, rng, low, high):
    longest = array.shape.index(max(array.shape))
    spots = []
    for shift in (0, 1):
        where = [jax.random.randint(jax.random.fold_in(rng, axis), (), 0, length) for axis, length in enumerate(array.shape)]
        where[longest] = (where[longest] + shift) % array.shape[longest]
        spots.append(tuple(where))
    return array.at[spots[0]].set(low).at[spots[1]].set(high)


def steps_of(rng, extent, cuts, least, top_value):
    level = 1.0
    for position, parts in cuts:
        steps = jax.random.uniform(jax.random.fold_in(jax.random.fold_in(rng, 6), position), (parts,), jnp.float32, least / len(cuts), top_value / len(cuts))
        level = level * jnp.repeat(jnp.exp(steps), extent[position] // parts).reshape((-1,) + (1,) * (len(extent) - 1 - position))
    return level


def rank_bounds(amount, slope):
    loads = [(1 << 20) // math.isqrt(grade ** slope) + 1 for grade in range(1, amount + 1)]
    scale = 1 + sum(loads) // (1 << 30)
    return np.cumsum(np.array([max(1, weight // scale) for weight in loads]))


def skewed_ids(rng, extent, count, skew):
    table = rank_bounds(count, skew)
    pick = jax.random.randint(jax.random.fold_in(rng, 1), extent, 0, int(table[count - 1]))
    grade = jnp.searchsorted(jnp.asarray(table, jnp.int32), pick, side="right")
    return jax.random.permutation(jax.random.fold_in(rng, 2), count)[grade].astype(jnp.int32)


def centred(key, extent, scale, bound, split=(), kind=jnp.bfloat16):
    factor_of = steps_of(key, extent, split, -0.22, 0.18) if split else 1.0
    result = jax.random.normal(key, extent, jnp.float32) * scale * factor_of
    return jnp.minimum(jnp.maximum(result, -bound), bound).astype(kind)


def setup_inputs(seed: int = 0) -> dict:
    splits = jax.random.split(jax.random.key(seed), 10)
    child_rhs = centred(splits[0], (NC, W, R), 1.0, 6.0, ((0, 32),))
    parent_rhs = centred(splits[1], (NP, W, R), 1.0, 6.0, ((0, 8),))
    child_lower_inv = centred(splits[2], (NC, W, W), W ** -0.5, 0.5, ((0, 32),))
    child_lower_off = centred(splits[3], (NC, W, W), (W * 16) ** -0.5, 0.125, ((0, 32),))
    child_upper_inv = centred(splits[4], (NC, W, W), W ** -0.5, 0.5, ((0, 32),))
    child_upper_off = centred(splits[5], (NC, W, W), (W * 4) ** -0.5, 0.25, ((0, 32),))
    parent_lower_inv = centred(splits[6], (NP, W, W), W ** -0.5, 0.5, ((0, 8),))
    parent_upper_inv = centred(splits[7], (NP, W, W), W ** -0.5, 0.5, ((0, 8),))
    parent_of = touch_ends(skewed_ids(splits[8], (NC,), NP, 1), jax.random.fold_in(splits[8], 3), 0, NP - 1).astype(jnp.int32)
    return {"child_rhs": child_rhs, "parent_rhs": parent_rhs, "child_lower_inv": child_lower_inv, "child_lower_off": child_lower_off, "child_upper_inv": child_upper_inv, "child_upper_off": child_upper_off, "parent_lower_inv": parent_lower_inv, "parent_upper_inv": parent_upper_inv, "parent_of": parent_of}


def bmm(a, b):
    return jnp.einsum('cij,cjr->cir', a.astype(jnp.float32), b.astype(jnp.float32))


def reference(child_rhs, parent_rhs, child_lower_inv, child_lower_off, child_upper_inv, child_upper_off, parent_lower_inv, parent_upper_inv, parent_of):
    blocks = NC // CH_DEV

    def shape_blocks(a):
        return a.reshape((blocks, CH_DEV) + a.shape[1:])

    rhs_b = shape_blocks(child_rhs)
    linv_b = shape_blocks(child_lower_inv)
    loff_b = shape_blocks(child_lower_off)
    uinv_b = shape_blocks(child_upper_inv)
    uoff_b = shape_blocks(child_upper_off)
    owner_b = shape_blocks(parent_of)
    labels = jnp.arange(NP, dtype=jnp.int32)

    def forward(total, items):
        rhs, linv, loff, owner = items
        fwd = bmm(linv, rhs).astype(jnp.bfloat16)
        contrib = bmm(loff, fwd)
        onehot = (owner[:, None] == labels[None, :]).astype(jnp.float32)
        total = total + jnp.einsum('cp,cwr->pwr', onehot, contrib, precision=lax.Precision.HIGHEST)
        return total, fwd

    update, fwd_b = lax.scan(forward, jnp.zeros((NP, W, R), jnp.float32), (rhs_b, linv_b, loff_b, owner_b))
    parent_residual = (parent_rhs.astype(jnp.float32) - update).astype(jnp.bfloat16)
    parent_forward = bmm(parent_lower_inv, parent_residual).astype(jnp.bfloat16)
    parent_solution = bmm(parent_upper_inv, parent_forward).astype(jnp.bfloat16)

    def backward(items):
        fwd, uinv, uoff, owner = items
        picked = parent_solution[owner.astype(jnp.int32)]
        resid = (fwd.astype(jnp.float32) - bmm(uoff, picked)).astype(jnp.bfloat16)
        return bmm(uinv, resid).astype(jnp.bfloat16)

    child_solution = lax.map(backward, (fwd_b, uinv_b, uoff_b, owner_b))
    return child_solution.reshape(NC, W, R), parent_solution
```

```python
import functools
import jax
import jax.numpy as jnp
from jax import lax
from jax.experimental import pallas as pl
from jax.experimental.pallas import tpu as pltpu
from jax.sharding import PartitionSpec as P

F32 = jnp.float32
BF16 = jnp.bfloat16
VMEM = pl.BlockSpec(memory_space=pltpu.VMEM)
SMEM = pl.BlockSpec(memory_space=pltpu.SMEM)
ANY = pl.BlockSpec(memory_space=pl.ANY)
MIB = 1 << 20


def target(i, k, n):
    return i ^ k if n & (n - 1) == 0 else (i + k) % n


def source(i, k, n):
    return i ^ k if n & (n - 1) == 0 else (i + n - k) % n


def shift(value, axis, k):
    n = lax.axis_size(axis)
    return lax.ppermute(value, axis, [(i, target(i, k, n)) for i in range(n)])


def chunk_of(count):
    return max(c for c in range(1, 9) if count % c == 0)


def params(mib):
    return pltpu.CompilerParams(vmem_limit_bytes=mib * MIB)


def dot(a, b):
    return jnp.dot(a, b, preferred_element_type=F32)


def dot_t(a, b):
    return lax.dot_general(a, b, (((1,), (1,)), ((), ())), preferred_element_type=F32)


def forward_kernel(n_row, owner, rhs_hbm, inv_hbm, off_hbm, fwd_hbm, *rest):
    pieces, (rhs, inv, off, fwd, acc, in_sem, out_sem) = rest[:n_row], rest[n_row:]
    count = rhs.shape[0]
    chunk = chunk_of(count)
    chunks = count // chunk
    slab = rhs.shape[2] // n_row

    def part(g):
        return pl.ds(g * chunk, chunk)

    loads = [
        [
            pltpu.make_async_copy(h.at[part(g)], v.at[part(g)], in_sem.at[s, g])
            for s, (h, v) in enumerate(((rhs_hbm, rhs), (inv_hbm, inv), (off_hbm, off)))
        ]
        for g in range(chunks)
    ]
    stores = [
        pltpu.make_async_copy(fwd.at[part(g)], fwd_hbm.at[part(g)], out_sem.at[g])
        for g in range(chunks)
    ]
    for group in loads:
        for copy in group:
            copy.start()
    acc[...] = jnp.zeros_like(acc)
    for g in range(chunks):
        for copy in loads[g]:
            copy.wait()
        for c in range(g * chunk, (g + 1) * chunk):
            fwd[c] = dot(inv[c], rhs[c]).astype(BF16)
        for c in range(g * chunk, (g + 1) * chunk):
            acc[owner[c]] += dot(off[c], fwd[c])
        stores[g].start()
    me = lax.axis_index("row")
    for p in range(acc.shape[0]):
        acc[p] = acc[p].T
    for k in range(n_row):
        rows = pl.ds(pl.multiple_of(target(me, k, n_row) * slab, slab), slab)
        pieces[k][...] = acc[:, rows, :].astype(BF16)
    for copy in stores:
        copy.wait()


def forward(parent_of, rhs, inv, off, parents, n_row):
    count, width, sides = rhs.shape
    chunks = count // chunk_of(count)
    piece = jax.ShapeDtypeStruct((parents, sides // n_row, width), BF16)
    return pl.pallas_call(
        functools.partial(forward_kernel, n_row),
        out_shape=[jax.ShapeDtypeStruct(rhs.shape, BF16)] + [piece] * n_row,
        in_specs=[SMEM, ANY, ANY, ANY],
        out_specs=[ANY] + [VMEM] * n_row,
        scratch_shapes=[
            pltpu.VMEM(rhs.shape, BF16),
            pltpu.VMEM(inv.shape, BF16),
            pltpu.VMEM(off.shape, BF16),
            pltpu.VMEM(rhs.shape, BF16),
            pltpu.VMEM((parents, sides, width), F32),
            pltpu.SemaphoreType.DMA((3, chunks)),
            pltpu.SemaphoreType.DMA((chunks,)),
        ],
        compiler_params=params(32),
        name="forward",
    )(parent_of, rhs, inv, off)


def row_sum_kernel(n_row, n_col, *rest):
    parts, outs, total = rest[:n_row], rest[n_row:-1], rest[-1]
    value = parts[0][...].astype(F32)
    for part in parts[1:]:
        value = value + part[...].astype(F32)
    total[...] = value
    me = lax.axis_index("col")
    per_col = total.shape[0] // n_col
    for k in range(n_col):
        outs[k][...] = total[pl.ds(target(me, k, n_col) * per_col, per_col)].astype(BF16)


def row_sum(parts, n_col):
    parents, slab, width = parts[0].shape
    piece = jax.ShapeDtypeStruct((parents // n_col, slab, width), BF16)
    return pl.pallas_call(
        functools.partial(row_sum_kernel, len(parts), n_col),
        out_shape=[piece] * n_col,
        in_specs=[VMEM] * len(parts),
        out_specs=[VMEM] * n_col,
        scratch_shapes=[pltpu.VMEM((parents, slab, width), F32)],
        compiler_params=params(32),
        name="row_sum",
    )(*parts)


def parent_kernel(n_row, n_col, rhs, lower, upper, *rest):
    parts, out, turned = rest[:n_col], rest[n_col], rest[n_col + 1]
    slab = out.shape[1]
    me = lax.axis_index("row")
    for p in range(out.shape[0]):
        update = parts[0][p].astype(F32)
        for part in parts[1:]:
            update = update + part[p].astype(F32)
        turned[...] = rhs[p].astype(F32).T
        mine = turned[pl.ds(pl.multiple_of(me * slab, slab), slab), :]
        residual = (mine - update).astype(BF16)
        fwd = dot_t(residual, lower[p]).astype(BF16)
        out[p] = dot_t(fwd, upper[p]).astype(BF16)


def parent_solve(rhs, lower, upper, parts, n_row):
    per_col, width, sides = rhs.shape
    return pl.pallas_call(
        functools.partial(parent_kernel, n_row, len(parts)),
        out_shape=jax.ShapeDtypeStruct((per_col, sides // n_row, width), BF16),
        in_specs=[VMEM] * (3 + len(parts)),
        out_specs=VMEM,
        scratch_shapes=[pltpu.VMEM((sides, width), F32)],
        compiler_params=params(32),
        name="parent_solve",
    )(rhs, lower, upper, *parts)


def join_kernel(n_col, *rest):
    parts, out = rest[:n_col], rest[n_col]
    me = lax.axis_index("col")
    per_col = out.shape[0] // n_col
    for k in range(n_col):
        out[pl.ds(source(me, k, n_col) * per_col, per_col)] = parts[k][...]


def join(parts):
    n_col = len(parts)
    per_col, slab, width = parts[0].shape
    return pl.pallas_call(
        functools.partial(join_kernel, n_col),
        out_shape=jax.ShapeDtypeStruct((per_col * n_col, slab, width), BF16),
        in_specs=[VMEM] * n_col,
        out_specs=VMEM,
        compiler_params=params(32),
        name="join",
    )(*parts)


def backward_kernel(n_row, n_col, owner, fwd_hbm, inv_hbm, off_hbm, *rest):
    parts, out_hbm, solved = rest[:n_row], rest[n_row], rest[n_row + 1]
    fwd, inv, off, out, turned, picked, in_sem, out_sem = rest[n_row + 2 :]
    count = fwd.shape[0]
    chunk = chunk_of(count)
    chunks = count // chunk

    def part(g):
        return pl.ds(g * chunk, chunk)

    loads = [
        [
            pltpu.make_async_copy(h.at[part(g)], v.at[part(g)], in_sem.at[s, g])
            for s, (h, v) in enumerate(((fwd_hbm, fwd), (inv_hbm, inv), (off_hbm, off)))
        ]
        for g in range(chunks)
    ]
    stores = [
        pltpu.make_async_copy(out.at[part(g)], out_hbm.at[part(g)], out_sem.at[g])
        for g in range(chunks)
    ]
    for group in loads:
        for copy in group:
            copy.start()
    me = lax.axis_index("row")
    parents, slab, _ = parts[0].shape
    for k in range(n_row):
        rows = pl.ds(pl.multiple_of(source(me, k, n_row) * slab, slab), slab)
        turned[:, rows, :] = parts[k][...].astype(F32)
    for p in range(parents):
        picked[p] = turned[p].T.astype(BF16)
    per_col = solved.shape[0]
    solved[...] = picked[pl.ds(lax.axis_index("col") * per_col, per_col)]
    for g in range(chunks):
        for copy in loads[g]:
            copy.wait()
        for c in range(g * chunk, (g + 1) * chunk):
            product = dot(off[c], picked[owner[c]])
            fwd[c] = (fwd[c].astype(F32) - product).astype(BF16)
        for c in range(g * chunk, (g + 1) * chunk):
            out[c] = dot(inv[c], fwd[c]).astype(BF16)
        stores[g].start()
    for copy in stores:
        copy.wait()


def backward(parent_of, fwd, inv, off, parts, n_col):
    count, width, sides = fwd.shape
    chunks = count // chunk_of(count)
    parents = parts[0].shape[0]
    n_row = len(parts)
    return pl.pallas_call(
        functools.partial(backward_kernel, n_row, n_col),
        out_shape=[
            jax.ShapeDtypeStruct(fwd.shape, BF16),
            jax.ShapeDtypeStruct((parents // n_col, width, sides), BF16),
        ],
        in_specs=[SMEM, ANY, ANY, ANY] + [VMEM] * n_row,
        out_specs=[ANY, VMEM],
        scratch_shapes=[
            pltpu.VMEM(fwd.shape, BF16),
            pltpu.VMEM(inv.shape, BF16),
            pltpu.VMEM(off.shape, BF16),
            pltpu.VMEM(fwd.shape, BF16),
            pltpu.VMEM((parents, sides, width), F32),
            pltpu.VMEM((parents, width, sides), BF16),
            pltpu.SemaphoreType.DMA((3, chunks)),
            pltpu.SemaphoreType.DMA((chunks,)),
        ],
        compiler_params=params(32),
        name="backward",
    )(parent_of, fwd, inv, off, *parts)


def on_device(
    child_rhs,
    parent_rhs,
    child_lower_inv,
    child_lower_off,
    child_upper_inv,
    child_upper_off,
    parent_lower_inv,
    parent_upper_inv,
    parent_of,
):
    n_row = lax.axis_size("row")
    n_col = lax.axis_size("col")
    parents = parent_rhs.shape[0] * n_col
    fwd, *pieces = forward(
        parent_of, child_rhs, child_lower_inv, child_lower_off, parents, n_row
    )
    parts = pieces[:1] + [shift(pieces[k], "row", k) for k in range(1, n_row)]
    pieces = list(row_sum(parts, n_col))
    parts = pieces[:1] + [shift(pieces[k], "col", k) for k in range(1, n_col)]
    solved = parent_solve(parent_rhs, parent_lower_inv, parent_upper_inv, parts, n_row)
    parts = [solved] + [shift(solved, "col", k) for k in range(1, n_col)]
    joined = join(parts)
    parts = [joined] + [shift(joined, "row", k) for k in range(1, n_row)]
    return tuple(
        backward(parent_of, fwd, child_upper_inv, child_upper_off, parts, n_col)
    )


def solution(mesh):
    child = P(("row", "col"), None, None)
    parent = P("col", None, None)
    return jax.shard_map(
        on_device,
        mesh=mesh,
        in_specs=(child, parent, child, child, child, child, parent, parent, P(("row", "col"))),
        out_specs=(child, parent),
        check_vma=False,
    )
```

```python
import jax
import jax.numpy as jnp
from jax import lax
from jax.experimental import pallas as pl
from jax.experimental.pallas import tpu as pltpu
from jax.sharding import PartitionSpec as P

F32 = jnp.float32
BF16 = jnp.bfloat16
VMEM = pl.BlockSpec(memory_space=pltpu.VMEM)
SMEM = pl.BlockSpec(memory_space=pltpu.SMEM)
ANY = pl.BlockSpec(memory_space=pl.ANY)
MIB = 1 << 20


def chunk_of(count):
    return max(c for c in range(1, 9) if count % c == 0)


def params(mib):
    return pltpu.CompilerParams(vmem_limit_bytes=mib * MIB)


def dot(a, b):
    return jnp.dot(a, b, preferred_element_type=F32)


def dot_t(a, b):
    return lax.dot_general(a, b, (((1,), (1,)), ((), ())), preferred_element_type=F32)


def forward_kernel(
    owner, rhs_hbm, inv_hbm, off_hbm, fwd_hbm, pieces, rhs, inv, off, fwd, acc, in_sem, out_sem
):
    n_row, _, slab, _ = pieces.shape
    count = rhs.shape[0]
    chunk = chunk_of(count)
    chunks = count // chunk

    def part(g):
        return pl.ds(g * chunk, chunk)

    loads = [
        [
            pltpu.make_async_copy(h.at[part(g)], v.at[part(g)], in_sem.at[s, g])
            for s, (h, v) in enumerate(((rhs_hbm, rhs), (inv_hbm, inv), (off_hbm, off)))
        ]
        for g in range(chunks)
    ]
    stores = [
        pltpu.make_async_copy(fwd.at[part(g)], fwd_hbm.at[part(g)], out_sem.at[g])
        for g in range(chunks)
    ]
    for group in loads:
        for copy in group:
            copy.start()
    acc[...] = jnp.zeros_like(acc)
    for g in range(chunks):
        for copy in loads[g]:
            copy.wait()
        for c in range(g * chunk, (g + 1) * chunk):
            fwd[c] = dot(inv[c], rhs[c]).astype(BF16)
        for c in range(g * chunk, (g + 1) * chunk):
            acc[owner[c]] += dot(off[c], fwd[c])
        stores[g].start()
    for p in range(acc.shape[0]):
        turned = acc[p].T.astype(BF16)
        for r in range(n_row):
            pieces[r, p] = turned[r * slab : (r + 1) * slab]
    for copy in stores:
        copy.wait()


def forward(parent_of, rhs, inv, off, parents, n_row):
    count, width, sides = rhs.shape
    chunks = count // chunk_of(count)
    return pl.pallas_call(
        forward_kernel,
        out_shape=[
            jax.ShapeDtypeStruct(rhs.shape, BF16),
            jax.ShapeDtypeStruct((n_row, parents, sides // n_row, width), BF16),
        ],
        in_specs=[SMEM, ANY, ANY, ANY],
        out_specs=[ANY, VMEM],
        scratch_shapes=[
            pltpu.VMEM(rhs.shape, BF16),
            pltpu.VMEM(inv.shape, BF16),
            pltpu.VMEM(off.shape, BF16),
            pltpu.VMEM(rhs.shape, BF16),
            pltpu.VMEM((parents, sides, width), F32),
            pltpu.SemaphoreType.DMA((3, chunks)),
            pltpu.SemaphoreType.DMA((chunks,)),
        ],
        compiler_params=params(56),
        name="forward",
    )(parent_of, rhs, inv, off)


def parent_kernel(rhs, lower, upper, parts, out, turned):
    devices, per_col, slab, _ = out.shape
    rows = pl.ds(pl.multiple_of(lax.axis_index("row") * slab, slab), slab)
    for p in range(per_col):
        update = parts[0, p].astype(F32)
        for d in range(1, parts.shape[0]):
            update = update + parts[d, p].astype(F32)
        turned[...] = rhs[p].astype(F32).T
        residual = (turned[rows, :] - update).astype(BF16)
        fwd = dot_t(residual, lower[p]).astype(BF16)
        solved = dot_t(fwd, upper[p]).astype(BF16)
        for d in range(devices):
            out[d, p] = solved


def parent_solve(rhs, lower, upper, parts):
    _, width, sides = rhs.shape
    return pl.pallas_call(
        parent_kernel,
        out_shape=jax.ShapeDtypeStruct(parts.shape, BF16),
        in_specs=[VMEM] * 4,
        out_specs=VMEM,
        scratch_shapes=[pltpu.VMEM((sides, width), F32)],
        compiler_params=params(16),
        name="parent_solve",
    )(rhs, lower, upper, parts)


def backward_kernel(owner, fwd, inv, off, parts, out_hbm, solved, res, out, picked, out_sem):
    count = fwd.shape[0]
    chunk = chunk_of(count)
    chunks = count // chunk
    n_row, parents, _, _ = parts.shape
    stores = []
    for p in range(parents):
        picked[p] = jnp.concatenate([parts[r, p] for r in range(n_row)]).astype(F32).T.astype(BF16)
    per_col = solved.shape[0]
    solved[...] = picked[pl.ds(lax.axis_index("col") * per_col, per_col)]
    for g in range(chunks):
        for c in range(g * chunk, (g + 1) * chunk):
            product = dot(off[c], picked[owner[c]])
            res[c] = (fwd[c].astype(F32) - product).astype(BF16)
        for c in range(g * chunk, (g + 1) * chunk):
            out[c] = dot(inv[c], res[c]).astype(BF16)
        part = pl.ds(g * chunk, chunk)
        copy = pltpu.make_async_copy(out.at[part], out_hbm.at[part], out_sem.at[g])
        copy.start()
        stores.append(copy)
    for copy in stores:
        copy.wait()


def backward(parent_of, fwd, inv, off, parts, per_col):
    count, width, sides = fwd.shape
    chunks = count // chunk_of(count)
    parents = parts.shape[1]
    return pl.pallas_call(
        backward_kernel,
        out_shape=[
            jax.ShapeDtypeStruct(fwd.shape, BF16),
            jax.ShapeDtypeStruct((per_col, width, sides), BF16),
        ],
        in_specs=[SMEM] + [VMEM] * 4,
        out_specs=[ANY, VMEM],
        scratch_shapes=[
            pltpu.VMEM(fwd.shape, BF16),
            pltpu.VMEM(fwd.shape, BF16),
            pltpu.VMEM((parents, width, sides), BF16),
            pltpu.SemaphoreType.DMA((chunks,)),
        ],
        compiler_params=params(32),
        name="backward",
    )(parent_of, fwd, inv, off, parts)


def on_device(
    child_rhs,
    parent_rhs,
    child_lower_inv,
    child_lower_off,
    child_upper_inv,
    child_upper_off,
    parent_lower_inv,
    parent_upper_inv,
    parent_of,
):
    n_row = lax.axis_size("row")
    n_col = lax.axis_size("col")
    parents = parent_rhs.shape[0] * n_col
    axes = ("row", "col")
    per_col = parent_rhs.shape[0]
    fwd, pieces = forward(
        parent_of, child_rhs, child_lower_inv, child_lower_off, parents, n_row
    )
    slab, width = pieces.shape[2:]
    sent = pieces.reshape(n_row * n_col, per_col, slab, width)
    parts = lax.all_to_all(sent, axes, 0, 0, tiled=True)
    solved = parent_solve(parent_rhs, parent_lower_inv, parent_upper_inv, parts)
    parts = lax.all_to_all(solved, axes, 0, 0, tiled=True)
    parts = parts.reshape(n_row, parents, slab, width)
    return tuple(
        backward(parent_of, fwd, child_upper_inv, child_upper_off, parts, per_col)
    )


def solution(mesh):
    child = P(("row", "col"), None, None)
    parent = P("col", None, None)
    return jax.shard_map(
        on_device,
        mesh=mesh,
        in_specs=(child, parent, child, child, child, child, parent, parent, P(("row", "col"))),
        out_specs=(child, parent),
        check_vma=False,
    )
```

```python
import jax
import jax.numpy as jnp
from jax import lax
from jax.experimental import pallas as pl
from jax.experimental.pallas import tpu as pltpu
from jax.sharding import PartitionSpec as P

F32 = jnp.float32
BF16 = jnp.bfloat16
VMEM = pl.BlockSpec(memory_space=pltpu.VMEM)
SMEM = pl.BlockSpec(memory_space=pltpu.SMEM)
ANY = pl.BlockSpec(memory_space=pl.ANY)
MIB = 1 << 20


def chunk_of(count):
    return max(c for c in range(1, 9) if count % c == 0)


def params(mib):
    return pltpu.CompilerParams(vmem_limit_bytes=mib * MIB)


def dot(a, b):
    return jnp.dot(a, b, preferred_element_type=F32)


def dot_t(a, b):
    return lax.dot_general(a, b, (((1,), (1,)), ((), ())), preferred_element_type=F32)


def forward_kernel(
    owner, rhs_hbm, inv_hbm, off_hbm, fwd, pieces, rhs, inv, off, acc, in_sem
):
    n_row, _, slab, _ = pieces.shape
    count = rhs.shape[0]
    chunk = chunk_of(count)
    chunks = count // chunk

    def part(g):
        return pl.ds(g * chunk, chunk)

    loads = [
        [
            pltpu.make_async_copy(h.at[part(g)], v.at[part(g)], in_sem.at[s, g])
            for s, (h, v) in enumerate(((rhs_hbm, rhs), (inv_hbm, inv), (off_hbm, off)))
        ]
        for g in range(chunks)
    ]
    for group in loads:
        for copy in group:
            copy.start()
    acc[...] = jnp.zeros_like(acc)
    for g in range(chunks):
        for copy in loads[g]:
            copy.wait()
        for c in range(g * chunk, (g + 1) * chunk):
            fwd[c] = dot(inv[c], rhs[c]).astype(BF16)
        for c in range(g * chunk, (g + 1) * chunk):
            acc[owner[c]] += dot(off[c], fwd[c])
    for p in range(acc.shape[0]):
        turned = acc[p].T.astype(BF16)
        for r in range(n_row):
            pieces[r, p] = turned[r * slab : (r + 1) * slab]


def forward(parent_of, rhs, inv, off, parents, n_row):
    count, width, sides = rhs.shape
    chunks = count // chunk_of(count)
    return pl.pallas_call(
        forward_kernel,
        out_shape=[
            pltpu.VMEM(rhs.shape, BF16),
            pltpu.VMEM((n_row, parents, sides // n_row, width), BF16),
        ],
        in_specs=[SMEM, ANY, ANY, ANY],
        out_specs=[VMEM, VMEM],
        scratch_shapes=[
            pltpu.VMEM(rhs.shape, BF16),
            pltpu.VMEM(inv.shape, BF16),
            pltpu.VMEM(off.shape, BF16),
            pltpu.VMEM((parents, sides, width), F32),
            pltpu.SemaphoreType.DMA((3, chunks)),
        ],
        compiler_params=params(24),
        name="forward",
    )(*(pltpu.with_memory_space_constraint(x, pltpu.HBM) for x in (parent_of, rhs, inv, off)))


def row_sum_kernel(parts, out):
    total = parts[0].astype(F32)
    for r in range(1, parts.shape[0]):
        total = total + parts[r].astype(F32)
    out[...] = total.astype(BF16)


def row_sum(parts):
    return pl.pallas_call(
        row_sum_kernel,
        out_shape=jax.ShapeDtypeStruct(parts.shape[1:], BF16),
        in_specs=[VMEM],
        out_specs=VMEM,
        compiler_params=params(16),
        name="row_sum",
    )(parts)


def repeat_kernel(value, out):
    for r in range(out.shape[0]):
        out[r] = value[...]


def repeat(value, times):
    return pl.pallas_call(
        repeat_kernel,
        out_shape=jax.ShapeDtypeStruct((times,) + value.shape, BF16),
        in_specs=[VMEM],
        out_specs=VMEM,
        compiler_params=params(16),
        name="repeat",
    )(value)


def parent_kernel(rhs, lower, upper, parts, out, turned):
    devices, per_col, slab, _ = out.shape
    rows = pl.ds(pl.multiple_of(lax.axis_index("row") * slab, slab), slab)
    for p in range(per_col):
        update = parts[0, p].astype(F32)
        for d in range(1, parts.shape[0]):
            update = update + parts[d, p].astype(F32)
        turned[...] = rhs[p].astype(F32).T
        residual = (turned[rows, :] - update).astype(BF16)
        fwd = dot_t(residual, lower[p]).astype(BF16)
        solved = dot_t(fwd, upper[p]).astype(BF16)
        for d in range(devices):
            out[d, p] = solved


def parent_solve(rhs, lower, upper, parts):
    _, width, sides = rhs.shape
    return pl.pallas_call(
        parent_kernel,
        out_shape=jax.ShapeDtypeStruct(parts.shape, BF16),
        in_specs=[VMEM] * 4,
        out_specs=VMEM,
        scratch_shapes=[pltpu.VMEM((sides, width), F32)],
        compiler_params=params(16),
        name="parent_solve",
    )(rhs, lower, upper, parts)


def backward_kernel(owner, fwd, inv, off, parts, out_hbm, solved, res, out, picked, out_sem):
    count = fwd.shape[0]
    chunk = chunk_of(count)
    chunks = count // chunk
    n_row, parents, _, _ = parts.shape
    stores = []
    for p in range(parents):
        picked[p] = jnp.concatenate([parts[r, p] for r in range(n_row)]).astype(F32).T.astype(BF16)
    per_col = solved.shape[0]
    solved[...] = picked[pl.ds(lax.axis_index("col") * per_col, per_col)]
    for g in range(chunks):
        for c in range(g * chunk, (g + 1) * chunk):
            product = dot(off[c], picked[owner[c]])
            res[c] = (fwd[c].astype(F32) - product).astype(BF16)
        for c in range(g * chunk, (g + 1) * chunk):
            out[c] = dot(inv[c], res[c]).astype(BF16)
        part = pl.ds(g * chunk, chunk)
        copy = pltpu.make_async_copy(out.at[part], out_hbm.at[part], out_sem.at[g])
        copy.start()
        stores.append(copy)
    for copy in stores:
        copy.wait()


def backward(parent_of, fwd, inv, off, parts, per_col):
    count, width, sides = fwd.shape
    chunks = count // chunk_of(count)
    parents = parts.shape[1]
    return pl.pallas_call(
        backward_kernel,
        out_shape=[
            jax.ShapeDtypeStruct(fwd.shape, BF16),
            jax.ShapeDtypeStruct((per_col, width, sides), BF16),
        ],
        in_specs=[SMEM] + [VMEM] * 4,
        out_specs=[ANY, VMEM],
        scratch_shapes=[
            pltpu.VMEM(fwd.shape, BF16),
            pltpu.VMEM(fwd.shape, BF16),
            pltpu.VMEM((parents, width, sides), BF16),
            pltpu.SemaphoreType.DMA((chunks,)),
        ],
        compiler_params=params(32),
        name="backward",
    )(parent_of, fwd, inv, off, parts)


def on_device(
    child_rhs,
    parent_rhs,
    child_lower_inv,
    child_lower_off,
    child_upper_inv,
    child_upper_off,
    parent_lower_inv,
    parent_upper_inv,
    parent_of,
):
    n_row = lax.axis_size("row")
    n_col = lax.axis_size("col")
    parents = parent_rhs.shape[0] * n_col
    per_col = parent_rhs.shape[0]
    fwd, pieces = forward(
        parent_of, child_rhs, child_lower_inv, child_lower_off, parents, n_row
    )
    slab, width = pieces.shape[2:]
    partial_sum = row_sum(lax.all_to_all(pieces, "row", 0, 0, tiled=True))
    sent = partial_sum.reshape(n_col, per_col, slab, width)
    parts = lax.all_to_all(sent, "col", 0, 0, tiled=True)
    solved = parent_solve(parent_rhs, parent_lower_inv, parent_upper_inv, parts)
    slabs = lax.all_to_all(solved, "col", 0, 0, tiled=True)
    slabs = repeat(slabs.reshape(parents, slab, width), n_row)
    parts = lax.all_to_all(slabs, "row", 0, 0, tiled=True)
    return tuple(
        backward(parent_of, fwd, child_upper_inv, child_upper_off, parts, per_col)
    )


def solution(mesh):
    child = P(("row", "col"), None, None)
    parent = P("col", None, None)
    return jax.shard_map(
        on_device,
        mesh=mesh,
        in_specs=(child, parent, child, child, child, child, parent, parent, P(("row", "col"))),
        out_specs=(child, parent),
        check_vma=False,
    )
```

```python
import functools
import jax
import jax.numpy as jnp
from jax import lax
from jax.experimental import pallas as pl
from jax.experimental.pallas import tpu as pltpu
from jax.sharding import Mesh, PartitionSpec as P

F32 = jnp.float32
BF16 = jnp.bfloat16
VMEM = pl.BlockSpec(memory_space=pltpu.VMEM)
SMEM = pl.BlockSpec(memory_space=pltpu.SMEM)
ANY = pl.BlockSpec(memory_space=pl.ANY)
MIB = 1 << 20


def chunk_of(count):
    return max(c for c in range(1, 9) if count % c == 0)


def params(mib):
    return pltpu.CompilerParams(vmem_limit_bytes=mib * MIB)


def dot(a, b):
    return jnp.dot(a, b, preferred_element_type=F32)


def dot_t(a, b):
    return lax.dot_general(a, b, (((1,), (1,)), ((), ())), preferred_element_type=F32)


def forward_kernel(cores, owner, rhs_hbm, inv_hbm, off_hbm, fwd, *rest):
    mine, theirs, (rhs, inv, off, acc, in_sem) = rest[0], rest[1:cores], rest[cores:]
    n_row, n_chip, per_col, slab, _ = mine.shape
    count = rhs.shape[0]
    chunk = chunk_of(count)
    chunks = count // chunk

    def part(g):
        return pl.ds(g * chunk, chunk)

    loads = [
        [
            pltpu.make_async_copy(h.at[part(g)], v.at[part(g)], in_sem.at[s, g])
            for s, (h, v) in enumerate(((rhs_hbm, rhs), (inv_hbm, inv), (off_hbm, off)))
        ]
        for g in range(chunks)
    ]
    for group in loads:
        for copy in group:
            copy.start()
    acc[...] = jnp.zeros_like(acc)
    for g in range(chunks):
        for copy in loads[g]:
            copy.wait()
        for c in range(g * chunk, (g + 1) * chunk):
            fwd[c] = dot(inv[c], rhs[c]).astype(BF16)
        for c in range(g * chunk, (g + 1) * chunk):
            acc[owner[c]] += dot(off[c], fwd[c])
    me = lax.axis_index("core")
    for k in range(cores):
        core = lax.rem(me + k, cores)
        out = theirs[k - 1] if k else mine
        for z in range(n_chip):
            for i in range(per_col):
                turned = acc[(z * cores + core) * per_col + i].T.astype(out.dtype)
                for r in range(n_row):
                    out[r, z, i] = turned[r * slab : (r + 1) * slab]


def forward(parent_of, rhs, inv, off, n_row, n_chip, cores, per_col):
    count, width, sides = rhs.shape
    chunks = count // chunk_of(count)
    parents = n_chip * cores * per_col
    piece = (n_row, n_chip, per_col, sides // n_row, width)
    return pl.pallas_call(
        functools.partial(forward_kernel, cores),
        out_shape=[pltpu.VMEM(rhs.shape, BF16), pltpu.VMEM(piece, F32)]
        + [pltpu.VMEM(piece, BF16)] * (cores - 1),
        in_specs=[SMEM, ANY, ANY, ANY],
        out_specs=[VMEM] * (1 + cores),
        scratch_shapes=[
            pltpu.VMEM(rhs.shape, BF16),
            pltpu.VMEM(inv.shape, BF16),
            pltpu.VMEM(off.shape, BF16),
            pltpu.VMEM((parents, sides, width), F32),
            pltpu.SemaphoreType.DMA((3, chunks)),
        ],
        compiler_params=params(24),
        name="forward",
    )(*(pltpu.with_memory_space_constraint(x, pltpu.HBM) for x in (parent_of, rhs, inv, off)))


def core_sum_kernel(*refs):
    total = refs[0][...]
    for part in refs[1:-1]:
        total = total + part[...].astype(F32)
    refs[-1][...] = total.astype(BF16)


def core_sum(parts):
    return pl.pallas_call(
        core_sum_kernel,
        out_shape=jax.ShapeDtypeStruct(parts[0].shape, BF16),
        in_specs=[VMEM] * len(parts),
        out_specs=VMEM,
        compiler_params=params(16),
        name="core_sum",
    )(*parts)


def parent_kernel(rhs, lower, upper, parts, out, turned):
    devices, per_col, slab, _ = out.shape
    rows = pl.ds(pl.multiple_of(lax.axis_index("row") * slab, slab), slab)
    for p in range(per_col):
        update = parts[0, p].astype(F32)
        for d in range(1, parts.shape[0]):
            update = update + parts[d, p].astype(F32)
        turned[...] = rhs[p].astype(F32).T
        residual = (turned[rows, :] - update).astype(BF16)
        fwd = dot_t(residual, lower[p]).astype(BF16)
        solved = dot_t(fwd, upper[p]).astype(BF16)
        for d in range(devices):
            out[d, p] = solved


def parent_solve(rhs, lower, upper, parts):
    _, width, sides = rhs.shape
    return pl.pallas_call(
        parent_kernel,
        out_shape=jax.ShapeDtypeStruct(parts.shape, BF16),
        in_specs=[VMEM] * 4,
        out_specs=VMEM,
        scratch_shapes=[pltpu.VMEM((sides, width), F32)],
        compiler_params=params(16),
        name="parent_solve",
    )(rhs, lower, upper, parts)


def backward_kernel(cores, owner, fwd, inv, off, *rest):
    parts, (out_hbm, solved, res, out, picked, out_sem) = rest[:cores], rest[cores:]
    count = fwd.shape[0]
    chunk = chunk_of(count)
    chunks = count // chunk
    n_row, n_chip, per_col, _, _ = parts[0].shape
    stores = []
    me = lax.axis_index("core")
    for k in range(cores):
        core = lax.rem(me + k, cores)
        for z in range(n_chip):
            for i in range(per_col):
                turned = jnp.concatenate([parts[k][r, z, i] for r in range(n_row)])
                picked[(z * cores + core) * per_col + i] = turned.astype(F32).T.astype(BF16)
    mine = (lax.axis_index("z") * cores + me) * per_col
    solved[...] = picked[pl.ds(mine, per_col)]
    for g in range(chunks):
        for c in range(g * chunk, (g + 1) * chunk):
            product = dot(off[c], picked[owner[c]])
            res[c] = (fwd[c].astype(F32) - product).astype(BF16)
        for c in range(g * chunk, (g + 1) * chunk):
            out[c] = dot(inv[c], res[c]).astype(BF16)
        part = pl.ds(g * chunk, chunk)
        copy = pltpu.make_async_copy(out.at[part], out_hbm.at[part], out_sem.at[g])
        copy.start()
        stores.append(copy)
    for copy in stores:
        copy.wait()


def backward(parent_of, fwd, inv, off, parts):
    count, width, sides = fwd.shape
    chunks = count // chunk_of(count)
    _, n_chip, per_col, _, _ = parts[0].shape
    parents = n_chip * len(parts) * per_col
    return pl.pallas_call(
        functools.partial(backward_kernel, len(parts)),
        out_shape=[
            jax.ShapeDtypeStruct(fwd.shape, BF16),
            jax.ShapeDtypeStruct((per_col, width, sides), BF16),
        ],
        in_specs=[SMEM] + [VMEM] * (3 + len(parts)),
        out_specs=[ANY, VMEM],
        scratch_shapes=[
            pltpu.VMEM(fwd.shape, BF16),
            pltpu.VMEM(fwd.shape, BF16),
            pltpu.VMEM((parents, width, sides), BF16),
            pltpu.SemaphoreType.DMA((chunks,)),
        ],
        compiler_params=params(32),
        name="backward",
    )(parent_of, fwd, inv, off, *parts)


def from_core(value, k):
    cores = lax.axis_size("core")
    return lax.ppermute(value, "core", [(i, (i + k) % cores) for i in range(cores)])


def on_device(
    child_rhs,
    parent_rhs,
    child_lower_inv,
    child_lower_off,
    child_upper_inv,
    child_upper_off,
    parent_lower_inv,
    parent_upper_inv,
    parent_of,
):
    n_row, n_chip, cores = (lax.axis_size(a) for a in ("row", "z", "core"))
    per_col = parent_rhs.shape[0]
    fwd, mine, *theirs = forward(
        parent_of, child_rhs, child_lower_inv, child_lower_off, n_row, n_chip, cores, per_col
    )
    total = core_sum([mine] + [from_core(x, k) for k, x in enumerate(theirs, 1)])
    slab, width = total.shape[3:]
    sent = total.reshape(n_row * n_chip, per_col, slab, width)
    parts = lax.all_to_all(sent, ("row", "z"), 0, 0, tiled=True)
    solved = parent_solve(parent_rhs, parent_lower_inv, parent_upper_inv, parts)
    mine = lax.all_to_all(solved, ("row", "z"), 0, 0, tiled=True).reshape(total.shape)
    parts = [mine] + [from_core(mine, cores - k) for k in range(1, cores)]
    return tuple(backward(parent_of, fwd, child_upper_inv, child_upper_off, parts))


def solution(mesh):
    n_row, n_col = (mesh.shape[a] for a in ("row", "col"))
    cores = 1 if n_col % 2 else 2
    split = Mesh(mesh.devices.reshape(n_row, n_col // cores, cores), ("row", "z", "core"))
    child = P(("row", "z", "core"), None, None)
    parent = P(("z", "core"), None, None)
    return jax.shard_map(
        on_device,
        mesh=split,
        in_specs=(child, parent, child, child, child, child, parent, parent, P(("row", "z", "core"))),
        out_specs=(child, parent),
        check_vma=False,
    )
```

```python
import functools
import jax
import jax.numpy as jnp
from jax import lax
from jax.experimental import pallas as pl
from jax.experimental.pallas import tpu as pltpu
from jax.sharding import Mesh, PartitionSpec as P

F32 = jnp.float32
BF16 = jnp.bfloat16
VMEM = pl.BlockSpec(memory_space=pltpu.VMEM)
SMEM = pl.BlockSpec(memory_space=pltpu.SMEM)
ANY = pl.BlockSpec(memory_space=pl.ANY)
MIB = 1 << 20


def ranges(count, shares):
    ends = [count * sum(shares[: i + 1]) // sum(shares) for i in range(len(shares))]
    pairs = zip([0] + ends[:-1], ends)
    return [(lo, hi) for lo, hi in pairs if hi > lo]


def params(mib):
    return pltpu.CompilerParams(vmem_limit_bytes=mib * MIB)


def dot(a, b):
    return jnp.dot(a, b, preferred_element_type=F32)


def dot_t(a, b):
    return lax.dot_general(a, b, (((1,), (1,)), ((), ())), preferred_element_type=F32)


def forward_kernel(cores, groups, owner, rhs_hbm, inv_hbm, off_hbm, fwd, *rest):
    mine, theirs, (rhs, inv, off, even, odd, in_sem) = rest[0], rest[1:cores], rest[cores:]
    n_row, n_chip, per_col, slab, _ = mine.shape
    loads = [
        [
            pltpu.make_async_copy(h.at[pl.ds(lo, hi - lo)], v.at[pl.ds(lo, hi - lo)], in_sem.at[s, g])
            for s, (h, v) in enumerate(((rhs_hbm, rhs), (inv_hbm, inv), (off_hbm, off)))
        ]
        for g, (lo, hi) in enumerate(groups)
    ]
    for group in loads:
        for copy in group:
            copy.start()
    even[...] = jnp.zeros_like(even)
    odd[...] = jnp.zeros_like(odd)

    def solve(c):
        fwd[c] = dot(inv[c], rhs[c]).astype(BF16)

    def add(c):
        acc = odd if c % 2 else even
        acc[owner[c]] += dot(off[c], fwd[c])

    late = []
    for g, (lo, hi) in enumerate(groups):
        for copy in loads[g]:
            copy.wait()
        for c in range(lo, hi):
            solve(c)
            if late:
                add(late.pop(0))
        for c in late:
            add(c)
        late = list(range(lo, hi))
    for c in late:
        add(c)
    me = lax.axis_index("core")
    for k in range(cores):
        core = lax.rem(me + k, cores)
        out = theirs[k - 1] if k else mine
        for z in range(n_chip):
            for i in range(per_col):
                p = (z * cores + core) * per_col + i
                turned = (even[p] + odd[p]).T.astype(out.dtype)
                for r in range(n_row):
                    out[r, z, i] = turned[r * slab : (r + 1) * slab]


def forward(parent_of, rhs, inv, off, n_row, n_chip, cores, per_col):
    count, width, sides = rhs.shape
    groups = ranges(count, (1, 2, 3))
    parents = n_chip * cores * per_col
    piece = (n_row, n_chip, per_col, sides // n_row, width)
    return pl.pallas_call(
        functools.partial(forward_kernel, cores, groups),
        out_shape=[pltpu.VMEM(rhs.shape, BF16), pltpu.VMEM(piece, F32)]
        + [pltpu.VMEM(piece, BF16)] * (cores - 1),
        in_specs=[SMEM, ANY, ANY, ANY],
        out_specs=[VMEM] * (1 + cores),
        scratch_shapes=[
            pltpu.VMEM(rhs.shape, BF16),
            pltpu.VMEM(inv.shape, BF16),
            pltpu.VMEM(off.shape, BF16),
            pltpu.VMEM((parents, width, sides), F32),
            pltpu.VMEM((parents, width, sides), F32),
            pltpu.SemaphoreType.DMA((3, len(groups))),
        ],
        compiler_params=params(28),
        name="forward",
    )(*(pltpu.with_memory_space_constraint(x, pltpu.HBM) for x in (parent_of, rhs, inv, off)))


def couple_kernel(inv, off, _, out):
    for c in range(out.shape[0]):
        out[c] = (-dot(inv[c], off[c])).astype(BF16)


def couple(inv, off, after):
    count, width, _ = inv.shape
    return pl.pallas_call(
        couple_kernel,
        out_shape=pltpu.VMEM(off.shape, BF16),
        in_specs=[VMEM, VMEM, ANY],
        out_specs=VMEM,
        compiler_params=params(16),
        cost_estimate=pl.CostEstimate(
            flops=2 * count * width**3, bytes_accessed=6 * count * width**2, transcendentals=0
        ),
        name="couple",
    )(inv, off, after)


def core_sum_kernel(*refs):
    total = refs[0][...]
    for part in refs[1:-2]:
        total = total + part[...].astype(F32)
    refs[-1][...] = total.astype(BF16)


def core_sum(parts, after):
    return pl.pallas_call(
        core_sum_kernel,
        out_shape=jax.ShapeDtypeStruct(parts[0].shape, BF16),
        in_specs=[VMEM] * len(parts) + [ANY],
        out_specs=VMEM,
        compiler_params=params(16),
        name="core_sum",
    )(*parts, after)


def parent_kernel(rhs, lower, upper, parts, out, turned):
    devices, per_col, slab, _ = out.shape
    rows = pl.ds(pl.multiple_of(lax.axis_index("row") * slab, slab), slab)
    for p in range(per_col):
        update = parts[0, p].astype(F32)
        for d in range(1, parts.shape[0]):
            update = update + parts[d, p].astype(F32)
        turned[...] = rhs[p].astype(F32).T
        residual = (turned[rows, :] - update).astype(BF16)
        fwd = dot_t(residual, lower[p]).astype(BF16)
        solved = dot_t(fwd, upper[p]).astype(BF16)
        for d in range(devices):
            out[d, p] = solved


def parent_solve(rhs, lower, upper, parts):
    _, width, sides = rhs.shape
    return pl.pallas_call(
        parent_kernel,
        out_shape=jax.ShapeDtypeStruct(parts.shape, BF16),
        in_specs=[VMEM] * 4,
        out_specs=VMEM,
        scratch_shapes=[pltpu.VMEM((sides, width), F32)],
        compiler_params=params(16),
        name="parent_solve",
    )(rhs, lower, upper, parts)


def backward_kernel(cores, groups, owner, fwd, inv, coupled, *rest):
    parts, (out_hbm, solved, out, picked, out_sem) = rest[:cores], rest[cores:]
    n_row, n_chip, per_col, _, _ = parts[0].shape
    me = lax.axis_index("core")
    for k in range(cores):
        core = lax.rem(me + k, cores)
        for z in range(n_chip):
            for i in range(per_col):
                turned = jnp.concatenate([parts[k][r, z, i] for r in range(n_row)])
                picked[(z * cores + core) * per_col + i] = turned.astype(F32).T.astype(BF16)
    mine = (lax.axis_index("z") * cores + me) * per_col
    solved[...] = picked[pl.ds(mine, per_col)]
    stores = []
    for g, (lo, hi) in enumerate(groups):
        for c in range(lo, hi):
            mats = jnp.concatenate([inv[c], coupled[c]], axis=1)
            out[c] = dot(mats, jnp.concatenate([fwd[c], picked[owner[c]]])).astype(BF16)
        part = pl.ds(lo, hi - lo)
        copy = pltpu.make_async_copy(out.at[part], out_hbm.at[part], out_sem.at[g])
        copy.start()
        stores.append(copy)
    for copy in stores:
        copy.wait()


def backward(parent_of, fwd, inv, coupled, parts):
    count, width, sides = fwd.shape
    groups = ranges(count, (2, 2, 1, 1))
    _, n_chip, per_col, _, _ = parts[0].shape
    parents = n_chip * len(parts) * per_col
    return pl.pallas_call(
        functools.partial(backward_kernel, len(parts), groups),
        out_shape=[
            jax.ShapeDtypeStruct(fwd.shape, BF16),
            jax.ShapeDtypeStruct((per_col, width, sides), BF16),
        ],
        in_specs=[SMEM] + [VMEM] * (3 + len(parts)),
        out_specs=[ANY, VMEM],
        scratch_shapes=[
            pltpu.VMEM(fwd.shape, BF16),
            pltpu.VMEM((parents, width, sides), BF16),
            pltpu.SemaphoreType.DMA((len(groups),)),
        ],
        compiler_params=params(32),
        name="backward",
    )(parent_of, fwd, inv, coupled, *parts)


def from_core(value, k):
    cores = lax.axis_size("core")
    return lax.ppermute(value, "core", [(i, (i + k) % cores) for i in range(cores)])


def on_device(
    child_rhs,
    parent_rhs,
    child_lower_inv,
    child_lower_off,
    child_upper_inv,
    child_upper_off,
    parent_lower_inv,
    parent_upper_inv,
    parent_of,
):
    n_row, n_chip, cores = (lax.axis_size(a) for a in ("row", "z", "core"))
    per_col = parent_rhs.shape[0]
    fwd, mine, *theirs = forward(
        parent_of, child_rhs, child_lower_inv, child_lower_off, n_row, n_chip, cores, per_col
    )
    theirs = [from_core(x, k) for k, x in enumerate(theirs, 1)]
    coupled = couple(child_upper_inv, child_upper_off, mine)
    total = core_sum([mine] + theirs, coupled)
    slab, width = total.shape[3:]
    sent = total.reshape(n_row * n_chip, per_col, slab, width)
    parts = lax.all_to_all(sent, ("row", "z"), 0, 0, tiled=True)
    solved = parent_solve(parent_rhs, parent_lower_inv, parent_upper_inv, parts)
    mine = lax.all_to_all(solved, ("row", "z"), 0, 0, tiled=True).reshape(total.shape)
    parts = [mine] + [from_core(mine, cores - k) for k in range(1, cores)]
    return tuple(backward(parent_of, fwd, child_upper_inv, coupled, parts))


def solution(mesh):
    n_row, n_col = (mesh.shape[a] for a in ("row", "col"))
    cores = 1 if n_col % 2 else 2
    split = Mesh(mesh.devices.reshape(n_row, n_col // cores, cores), ("row", "z", "core"))
    child = P(("row", "z", "core"), None, None)
    parent = P(("z", "core"), None, None)
    return jax.shard_map(
        on_device,
        mesh=split,
        in_specs=(child, parent, child, child, child, child, parent, parent, P(("row", "z", "core"))),
        out_specs=(child, parent),
        check_vma=False,
    )
```

```python
import functools
import jax
import jax.numpy as jnp
from jax import lax
from jax.experimental import pallas as pl
from jax.experimental.pallas import tpu as pltpu
from jax.sharding import Mesh, PartitionSpec as P

F32 = jnp.float32
BF16 = jnp.bfloat16
VMEM = pl.BlockSpec(memory_space=pltpu.VMEM)
SMEM = pl.BlockSpec(memory_space=pltpu.SMEM)
ANY = pl.BlockSpec(memory_space=pl.ANY)
MIB = 1 << 20


def ranges(count, shares):
    ends = [count * sum(shares[: i + 1]) // sum(shares) for i in range(len(shares))]
    pairs = zip([0] + ends[:-1], ends)
    return [(lo, hi) for lo, hi in pairs if hi > lo]


def halves(lo, hi):
    mid = (lo + hi + 1) // 2
    return (lo, mid - lo), (mid, hi - mid)


def params(mib):
    return pltpu.CompilerParams(vmem_limit_bytes=mib * MIB)


def dot(a, b):
    return jnp.dot(a, b, preferred_element_type=F32)


def dot_t(a, b):
    return lax.dot_general(a, b, (((1,), (1,)), ((), ())), preferred_element_type=F32)


def forward_kernel(cores, groups, owner, rhs_hbm, inv_hbm, off_hbm, fwd, *rest):
    mine, theirs, (rhs, inv, off, even, odd, in_sem) = rest[0], rest[1:cores], rest[cores:]
    n_row, n_chip, per_col, slab, _ = mine.shape
    loads = [
        [
            pltpu.make_async_copy(h.at[pl.ds(*part)], v.at[pl.ds(*part)], in_sem.at[s, lane, g])
            for s, (h, v) in enumerate(((rhs_hbm, rhs), (inv_hbm, inv), (off_hbm, off)))
            for lane, part in enumerate(halves(lo, hi))
        ]
        for g, (lo, hi) in enumerate(groups)
    ]
    for group in loads:
        for n, copy in enumerate(group):
            copy.start(priority=n % 2)
    even[...] = jnp.zeros_like(even)
    odd[...] = jnp.zeros_like(odd)

    def solve(c):
        fwd[c] = dot(inv[c], rhs[c]).astype(BF16)

    def add(c):
        acc = odd if c % 2 else even
        acc[owner[c]] += dot(off[c], fwd[c])

    late = []
    for g, (lo, hi) in enumerate(groups):
        for copy in loads[g]:
            copy.wait()
        for c in range(lo, hi):
            solve(c)
            if late:
                add(late.pop(0))
        for c in late:
            add(c)
        late = list(range(lo, hi))
    for c in late:
        add(c)
    me = lax.axis_index("core")
    for k in range(cores):
        core = lax.rem(me + k, cores)
        out = theirs[k - 1] if k else mine
        for z in range(n_chip):
            for i in range(per_col):
                p = (z * cores + core) * per_col + i
                turned = (even[p] + odd[p]).T.astype(out.dtype)
                for r in range(n_row):
                    out[r, z, i] = turned[r * slab : (r + 1) * slab]


def forward(parent_of, rhs, inv, off, n_row, n_chip, cores, per_col):
    count, width, sides = rhs.shape
    groups = ranges(count, (1, 2, 3))
    parents = n_chip * cores * per_col
    piece = (n_row, n_chip, per_col, sides // n_row, width)
    return pl.pallas_call(
        functools.partial(forward_kernel, cores, groups),
        out_shape=[pltpu.VMEM(rhs.shape, BF16), pltpu.VMEM(piece, F32)]
        + [pltpu.VMEM(piece, BF16)] * (cores - 1),
        in_specs=[SMEM, ANY, ANY, ANY],
        out_specs=[VMEM] * (1 + cores),
        scratch_shapes=[
            pltpu.VMEM(rhs.shape, BF16),
            pltpu.VMEM(inv.shape, BF16),
            pltpu.VMEM(off.shape, BF16),
            pltpu.VMEM((parents, width, sides), F32),
            pltpu.VMEM((parents, width, sides), F32),
            pltpu.SemaphoreType.DMA((3, 2, len(groups))),
        ],
        compiler_params=params(28),
        name="forward",
    )(*(pltpu.with_memory_space_constraint(x, pltpu.HBM) for x in (parent_of, rhs, inv, off)))


def couple_kernel(inv, off, _, out):
    for c in range(out.shape[0]):
        out[c] = (-dot(inv[c], off[c])).astype(BF16)


def couple(inv, off, after):
    count, width, _ = inv.shape
    return pl.pallas_call(
        couple_kernel,
        out_shape=pltpu.VMEM(off.shape, BF16),
        in_specs=[VMEM, VMEM, ANY],
        out_specs=VMEM,
        compiler_params=params(16),
        cost_estimate=pl.CostEstimate(
            flops=2 * count * width**3, bytes_accessed=6 * count * width**2, transcendentals=0
        ),
        name="couple",
    )(inv, off, after)


def core_sum_kernel(*refs):
    total = refs[0][...]
    for part in refs[1:-1]:
        total = total + part[...].astype(F32)
    refs[-1][...] = total.astype(BF16)


def core_sum(parts):
    return pl.pallas_call(
        core_sum_kernel,
        out_shape=jax.ShapeDtypeStruct(parts[0].shape, BF16),
        in_specs=[VMEM] * len(parts),
        out_specs=VMEM,
        compiler_params=params(16),
        name="core_sum",
    )(*parts)


def parent_kernel(rhs, lower, upper, parts, out, turned):
    devices, per_col, slab, _ = out.shape
    rows = pl.ds(pl.multiple_of(lax.axis_index("row") * slab, slab), slab)
    for p in range(per_col):
        update = parts[0, p].astype(F32)
        for d in range(1, parts.shape[0]):
            update = update + parts[d, p].astype(F32)
        turned[...] = rhs[p].astype(F32).T
        residual = (turned[rows, :] - update).astype(BF16)
        fwd = dot_t(residual, lower[p]).astype(BF16)
        solved = dot_t(fwd, upper[p]).astype(BF16)
        for d in range(devices):
            out[d, p] = solved


def parent_solve(rhs, lower, upper, parts):
    _, width, sides = rhs.shape
    return pl.pallas_call(
        parent_kernel,
        out_shape=jax.ShapeDtypeStruct(parts.shape, BF16),
        in_specs=[VMEM] * 4,
        out_specs=VMEM,
        scratch_shapes=[pltpu.VMEM((sides, width), F32)],
        compiler_params=params(16),
        name="parent_solve",
    )(rhs, lower, upper, parts)


def backward_kernel(cores, groups, owner, fwd, inv, coupled, *rest):
    parts, (out_hbm, solved, out, picked, out_sem) = rest[:cores], rest[cores:]
    n_row, n_chip, per_col, _, _ = parts[0].shape
    me = lax.axis_index("core")
    for k in range(cores):
        core = lax.rem(me + k, cores)
        for z in range(n_chip):
            for i in range(per_col):
                turned = jnp.concatenate([parts[k][r, z, i] for r in range(n_row)])
                picked[(z * cores + core) * per_col + i] = turned.astype(F32).T.astype(BF16)
    mine = (lax.axis_index("z") * cores + me) * per_col
    solved[...] = picked[pl.ds(mine, per_col)]
    stores = []
    for g, (lo, hi) in enumerate(groups):
        for c in range(lo, hi):
            mats = jnp.concatenate([inv[c], coupled[c]], axis=1)
            out[c] = dot(mats, jnp.concatenate([fwd[c], picked[owner[c]]])).astype(BF16)
        for lane, part in enumerate(halves(lo, hi)):
            part = pl.ds(*part)
            copy = pltpu.make_async_copy(out.at[part], out_hbm.at[part], out_sem.at[lane, g])
            copy.start(priority=lane)
            stores.append(copy)
    for copy in stores:
        copy.wait()


def backward(parent_of, fwd, inv, coupled, parts):
    count, width, sides = fwd.shape
    groups = ranges(count, (2, 2, 1, 1))
    _, n_chip, per_col, _, _ = parts[0].shape
    parents = n_chip * len(parts) * per_col
    return pl.pallas_call(
        functools.partial(backward_kernel, len(parts), groups),
        out_shape=[
            jax.ShapeDtypeStruct(fwd.shape, BF16),
            jax.ShapeDtypeStruct((per_col, width, sides), BF16),
        ],
        in_specs=[SMEM] + [VMEM] * (3 + len(parts)),
        out_specs=[ANY, VMEM],
        scratch_shapes=[
            pltpu.VMEM(fwd.shape, BF16),
            pltpu.VMEM((parents, width, sides), BF16),
            pltpu.SemaphoreType.DMA((2, len(groups))),
        ],
        compiler_params=params(32),
        name="backward",
    )(parent_of, fwd, inv, coupled, *parts)


def from_core(value, k):
    cores = lax.axis_size("core")
    return lax.ppermute(value, "core", [(i, (i + k) % cores) for i in range(cores)])


def on_device(
    child_rhs,
    parent_rhs,
    child_lower_inv,
    child_lower_off,
    child_upper_inv,
    child_upper_off,
    parent_lower_inv,
    parent_upper_inv,
    parent_of,
):
    n_row, n_chip, cores = (lax.axis_size(a) for a in ("row", "z", "core"))
    per_col = parent_rhs.shape[0]
    fwd, mine, *theirs = forward(
        parent_of, child_rhs, child_lower_inv, child_lower_off, n_row, n_chip, cores, per_col
    )
    theirs = [from_core(x, k) for k, x in enumerate(theirs, 1)]
    total = core_sum([mine] + theirs)
    slab, width = total.shape[3:]
    sent = total.reshape(n_row * n_chip, per_col, slab, width)
    parts = lax.all_to_all(sent, ("row", "z"), 0, 0, tiled=True)
    solved = parent_solve(parent_rhs, parent_lower_inv, parent_upper_inv, parts)
    mine = lax.all_to_all(solved, ("row", "z"), 0, 0, tiled=True).reshape(total.shape)
    parts = [mine] + [from_core(mine, cores - k) for k in range(1, cores)]
    coupled = couple(child_upper_inv, child_upper_off, mine)
    return tuple(backward(parent_of, fwd, child_upper_inv, coupled, parts))


def solution(mesh):
    n_row, n_col = (mesh.shape[a] for a in ("row", "col"))
    cores = 1 if n_col % 2 else 2
    split = Mesh(mesh.devices.reshape(n_row, n_col // cores, cores), ("row", "z", "core"))
    child = P(("row", "z", "core"), None, None)
    parent = P(("z", "core"), None, None)
    return jax.shard_map(
        on_device,
        mesh=split,
        in_specs=(child, parent, child, child, child, child, parent, parent, P(("row", "z", "core"))),
        out_specs=(child, parent),
        check_vma=False,
    )
```

```python
import functools
import math
import jax
import jax.numpy as jnp
from jax import lax
from jax.experimental import pallas as pl
from jax.experimental.pallas import tpu as pltpu
from jax.sharding import Mesh, PartitionSpec as P

F32 = jnp.float32
BF16 = jnp.bfloat16
VMEM = pl.BlockSpec(memory_space=pltpu.VMEM)
ANY = pl.BlockSpec(memory_space=pl.ANY)
MIB = 1 << 20
VMEM_BYTES = 64 * MIB
WAIT = pl.CostEstimate(flops=8 * 10**9, bytes_accessed=MIB, transcendentals=0)


def ranges(count, shares):
    ends = [count * sum(shares[: i + 1]) // sum(shares) for i in range(len(shares))]
    pairs = zip([0] + ends[:-1], ends)
    return [(lo, hi) for lo, hi in pairs if hi > lo]


def params(mib):
    return pltpu.CompilerParams(vmem_limit_bytes=mib * MIB)


def dot(a, b):
    return jnp.dot(a, b, preferred_element_type=F32)


def dot_t(a, b):
    return lax.dot_general(a, b, (((1,), (1,)), ((), ())), preferred_element_type=F32)


def forward_kernel(cores, groups, owner_hbm, rhs_hbm, inv_hbm, off_hbm, fwd, *rest):
    mine, theirs, scratch = rest[0], rest[1:cores], rest[cores:]
    rhs, inv, off, owner, even, odd, in_sem, owner_sem = scratch
    n_row, n_chip, per_col, slab, _ = mine.shape
    loads = [
        [
            pltpu.make_async_copy(h.at[pl.ds(lo, hi - lo)], v.at[pl.ds(lo, hi - lo)], in_sem.at[s, g])
            for s, (h, v) in enumerate(((rhs_hbm, rhs), (inv_hbm, inv), (off_hbm, off)))
        ]
        for g, (lo, hi) in enumerate(groups)
    ]
    names = pltpu.make_async_copy(owner_hbm, owner, owner_sem)
    for copy in loads[0]:
        copy.start()
    names.start()
    for group in loads[1:]:
        for copy in group:
            copy.start()
    even[...] = jnp.zeros_like(even)
    odd[...] = jnp.zeros_like(odd)

    def solve(c):
        fwd[c] = dot(inv[c], rhs[c]).astype(BF16)

    def add(c):
        acc = odd if c % 2 else even
        acc[owner[c]] += dot(off[c], fwd[c])

    late = []
    for g, (lo, hi) in enumerate(groups):
        for copy in loads[g]:
            copy.wait()
        for c in range(lo, hi):
            solve(c)
            if late:
                add(late.pop(0))
        if g == 0:
            names.wait()
        for c in late:
            add(c)
        late = list(range(lo, hi))
    for c in late:
        add(c)
    me = lax.axis_index("core")
    for k in range(cores):
        core = lax.rem(me + k, cores)
        out = theirs[k - 1] if k else mine
        for z in range(n_chip):
            for i in range(per_col):
                p = (z * cores + core) * per_col + i
                turned = (even[p] + odd[p]).T.astype(out.dtype)
                for r in range(n_row):
                    out[r, z, i] = turned[r * slab : (r + 1) * slab]


def forward(parent_of, rhs, inv, off, n_row, n_chip, cores, per_col):
    count, width, sides = rhs.shape
    groups = ranges(count, (2, 3, 3, 2, 1, 1))
    parents = n_chip * cores * per_col
    piece = (n_row, n_chip, per_col, sides // n_row, width)
    kept = 2 * rhs.size + (2 + 2 * cores) * math.prod(piece)
    room = (VMEM_BYTES - kept - MIB) // MIB
    return pl.pallas_call(
        functools.partial(forward_kernel, cores, groups),
        out_shape=[pltpu.VMEM(rhs.shape, BF16), pltpu.VMEM(piece, F32)]
        + [pltpu.VMEM(piece, BF16)] * (cores - 1),
        in_specs=[ANY] * 4,
        out_specs=[VMEM] * (1 + cores),
        scratch_shapes=[
            pltpu.VMEM(rhs.shape, BF16),
            pltpu.VMEM(inv.shape, BF16),
            pltpu.VMEM(off.shape, BF16),
            pltpu.SMEM(parent_of.shape, jnp.int32),
            pltpu.VMEM((parents, width, sides), F32),
            pltpu.VMEM((parents, width, sides), F32),
            pltpu.SemaphoreType.DMA((3, len(groups))),
            pltpu.SemaphoreType.DMA,
        ],
        compiler_params=params(room),
        name="forward",
    )(*(pltpu.with_memory_space_constraint(x, pltpu.HBM) for x in (parent_of, rhs, inv, off)))


def couple_kernel(inv, off, _, out):
    for c in range(out.shape[0]):
        out[c] = (-dot(inv[c], off[c])).astype(BF16)


def couple(inv, off, after):
    count, width, _ = inv.shape
    return pl.pallas_call(
        couple_kernel,
        out_shape=pltpu.VMEM(off.shape, BF16),
        in_specs=[VMEM, VMEM, ANY],
        out_specs=VMEM,
        compiler_params=params(16),
        cost_estimate=pl.CostEstimate(
            flops=2 * count * width**3, bytes_accessed=6 * count * width**2, transcendentals=0
        ),
        name="couple",
    )(inv, off, after)


def core_sum_kernel(*refs):
    total = refs[0][...]
    for part in refs[1:-1]:
        total = total + part[...].astype(F32)
    refs[-1][...] = total.astype(BF16)


def core_sum(parts):
    return pl.pallas_call(
        core_sum_kernel,
        out_shape=jax.ShapeDtypeStruct(parts[0].shape, BF16),
        in_specs=[VMEM] * len(parts),
        out_specs=VMEM,
        compiler_params=params(16),
        cost_estimate=WAIT,
        name="core_sum",
    )(*parts)


def parent_kernel(rhs, lower, upper, parts, out, turned):
    devices, per_col, slab, _ = out.shape
    rows = pl.ds(pl.multiple_of(lax.axis_index("row") * slab, slab), slab)
    for p in range(per_col):
        update = parts[0, p].astype(F32)
        for d in range(1, parts.shape[0]):
            update = update + parts[d, p].astype(F32)
        turned[...] = rhs[p].astype(F32).T
        residual = (turned[rows, :] - update).astype(BF16)
        fwd = dot_t(residual, lower[p]).astype(BF16)
        solved = dot_t(fwd, upper[p]).astype(BF16)
        for d in range(devices):
            out[d, p] = solved


def parent_solve(rhs, lower, upper, parts):
    _, width, sides = rhs.shape
    return pl.pallas_call(
        parent_kernel,
        out_shape=jax.ShapeDtypeStruct(parts.shape, BF16),
        in_specs=[VMEM] * 4,
        out_specs=VMEM,
        scratch_shapes=[pltpu.VMEM((sides, width), F32)],
        compiler_params=params(16),
        cost_estimate=WAIT,
        name="parent_solve",
    )(rhs, lower, upper, parts)


def backward_kernel(cores, groups, owner_any, fwd, inv, coupled, *rest):
    parts, scratch = rest[:cores], rest[cores:]
    out_hbm, solved_hbm, out, picked, owner, out_sem, small_sem = scratch
    n_row, n_chip, per_col, _, _ = parts[0].shape
    names = pltpu.make_async_copy(owner_any, owner, small_sem.at[0])
    names.start()
    me = lax.axis_index("core")
    for k in range(cores):
        core = lax.rem(me + k, cores)
        for z in range(n_chip):
            for i in range(per_col):
                turned = jnp.concatenate([parts[k][r, z, i] for r in range(n_row)])
                picked[(z * cores + core) * per_col + i] = turned.astype(F32).T.astype(BF16)
    mine = (lax.axis_index("z") * cores + me) * per_col
    solved = pltpu.make_async_copy(picked.at[pl.ds(mine, per_col)], solved_hbm, small_sem.at[1])
    solved.start()
    names.wait()
    stores = [solved]
    for g, (lo, hi) in enumerate(groups):
        for c in range(lo, hi):
            mats = jnp.concatenate([inv[c], coupled[c]], axis=1)
            out[c] = dot(mats, jnp.concatenate([fwd[c], picked[owner[c]]])).astype(BF16)
        part = pl.ds(lo, hi - lo)
        copy = pltpu.make_async_copy(out.at[part], out_hbm.at[part], out_sem.at[g])
        copy.start()
        stores.append(copy)
    for copy in stores:
        copy.wait()


def backward(parent_of, fwd, inv, coupled, parts):
    count, width, sides = fwd.shape
    groups = ranges(count, (2, 2, 1, 1))
    _, n_chip, per_col, _, _ = parts[0].shape
    parents = n_chip * len(parts) * per_col
    return pl.pallas_call(
        functools.partial(backward_kernel, len(parts), groups),
        out_shape=[
            jax.ShapeDtypeStruct(fwd.shape, BF16),
            jax.ShapeDtypeStruct((per_col, width, sides), BF16),
        ],
        in_specs=[ANY] + [VMEM] * (3 + len(parts)),
        out_specs=[ANY, ANY],
        scratch_shapes=[
            pltpu.VMEM(fwd.shape, BF16),
            pltpu.VMEM((parents, width, sides), BF16),
            pltpu.SMEM(parent_of.shape, jnp.int32),
            pltpu.SemaphoreType.DMA((len(groups),)),
            pltpu.SemaphoreType.DMA((2,)),
        ],
        compiler_params=params(32),
        name="backward",
    )(parent_of, fwd, inv, coupled, *parts)


def from_core(value, k):
    cores = lax.axis_size("core")
    return lax.ppermute(value, "core", [(i, (i + k) % cores) for i in range(cores)])


def on_device(
    child_rhs,
    parent_rhs,
    child_lower_inv,
    child_lower_off,
    child_upper_inv,
    child_upper_off,
    parent_lower_inv,
    parent_upper_inv,
    parent_of,
):
    n_row, n_chip, cores = (lax.axis_size(a) for a in ("row", "z", "core"))
    per_col = parent_rhs.shape[0]
    fwd, mine, *theirs = forward(
        parent_of, child_rhs, child_lower_inv, child_lower_off, n_row, n_chip, cores, per_col
    )
    theirs = [from_core(x, k) for k, x in enumerate(theirs, 1)]
    total = core_sum([mine] + theirs)
    slab, width = total.shape[3:]
    sent = total.reshape(n_row * n_chip, per_col, slab, width)
    parts = lax.all_to_all(sent, ("row", "z"), 0, 0, tiled=True)
    solved = parent_solve(parent_rhs, parent_lower_inv, parent_upper_inv, parts)
    mine = lax.all_to_all(solved, ("row", "z"), 0, 0, tiled=True).reshape(total.shape)
    parts = [mine] + [from_core(mine, cores - k) for k in range(1, cores)]
    coupled = couple(child_upper_inv, child_upper_off, mine)
    return tuple(backward(parent_of, fwd, child_upper_inv, coupled, parts))


def solution(mesh):
    n_row, n_col = (mesh.shape[a] for a in ("row", "col"))
    cores = 1 if n_col % 2 else 2
    split = Mesh(mesh.devices.reshape(n_row, n_col // cores, cores), ("row", "z", "core"))
    child = P(("row", "z", "core"), None, None)
    parent = P(("z", "core"), None, None)
    return jax.shard_map(
        on_device,
        mesh=split,
        in_specs=(child, parent, child, child, child, child, parent, parent, P(("row", "z", "core"))),
        out_specs=(child, parent),
        check_vma=False,
    )
```

```python
import functools
import math
import jax
import jax.numpy as jnp
from jax import lax
from jax.experimental import pallas as pl
from jax.experimental.pallas import tpu as pltpu
from jax.sharding import Mesh, PartitionSpec as P

F32 = jnp.float32
BF16 = jnp.bfloat16
VMEM = pl.BlockSpec(memory_space=pltpu.VMEM)
ANY = pl.BlockSpec(memory_space=pl.ANY)
MIB = 1 << 20
VMEM_BYTES = 64 * MIB
WAIT = pl.CostEstimate(flops=8 * 10**9, bytes_accessed=MIB, transcendentals=0)


def ranges(count, shares):
    ends = [count * sum(shares[: i + 1]) // sum(shares) for i in range(len(shares))]
    pairs = zip([0] + ends[:-1], ends)
    return [(lo, hi) for lo, hi in pairs if hi > lo]


def params(mib):
    return pltpu.CompilerParams(vmem_limit_bytes=mib * MIB)


def dot(a, b):
    return jnp.dot(a, b, preferred_element_type=F32)


def dot_t(a, b):
    return lax.dot_general(a, b, (((1,), (1,)), ((), ())), preferred_element_type=F32)


def forward_kernel(cores, groups, owner_hbm, rhs_hbm, inv_hbm, off_hbm, fwd, *rest):
    mine, theirs, scratch = rest[0], rest[1:cores], rest[cores:]
    rhs, inv, off, owner, even, odd, flat, in_sem, owner_sem = scratch
    n_row, _, half, _ = mine.shape
    slab = half * cores
    loads = [
        [
            pltpu.make_async_copy(h.at[pl.ds(lo, hi - lo)], v.at[pl.ds(lo, hi - lo)], in_sem.at[s, g])
            for s, (h, v) in enumerate(((rhs_hbm, rhs), (inv_hbm, inv), (off_hbm, off)))
        ]
        for g, (lo, hi) in enumerate(groups)
    ]
    names = pltpu.make_async_copy(owner_hbm, owner, owner_sem)
    for g, group in enumerate(loads):
        for lane, copy in enumerate(group):
            copy.start(priority=(3 * g + lane) % 2)
        if g == 0:
            names.start()
    even[...] = jnp.zeros_like(even)
    odd[...] = jnp.zeros_like(odd)

    def solve(c):
        fwd[c] = dot(inv[c], rhs[c]).astype(BF16)

    def add(c):
        acc = odd if c % 2 else even
        acc[owner[c]] += dot(off[c], fwd[c])

    late = []
    for g, (lo, hi) in enumerate(groups):
        for copy in loads[g]:
            copy.wait()
        for c in range(lo, hi):
            solve(c)
            if late:
                add(late.pop(0))
        if g == 0:
            names.wait()
        for c in late:
            add(c)
        late = list(range(lo, hi))
    for c in late:
        add(c)
    for p in range(flat.shape[0]):
        flat[p] = (even[p] + odd[p]).T
    me = lax.axis_index("core")
    for k in range(cores):
        out = theirs[k - 1] if k else mine
        for r in range(n_row):
            start = r * slab + lax.rem(me + k, cores) * half
            rows = pl.ds(pl.multiple_of(start, half), half)
            out[r] = flat[:, rows, :].astype(out.dtype)


def forward(parent_of, rhs, inv, off, n_row, n_chip, cores, per_col):
    count, width, sides = rhs.shape
    groups = ranges(count, (2, 3, 3, 2, 1, 1))
    parents = n_chip * cores * per_col
    piece = (n_row, parents, sides // (n_row * cores), width)
    kept = 2 * rhs.size + (2 + 2 * cores) * math.prod(piece)
    room = (VMEM_BYTES - kept - MIB) // MIB
    return pl.pallas_call(
        functools.partial(forward_kernel, cores, groups),
        out_shape=[pltpu.VMEM(rhs.shape, BF16), pltpu.VMEM(piece, F32)]
        + [pltpu.VMEM(piece, BF16)] * (cores - 1),
        in_specs=[ANY] * 4,
        out_specs=[VMEM] * (1 + cores),
        scratch_shapes=[
            pltpu.VMEM(rhs.shape, BF16),
            pltpu.VMEM(inv.shape, BF16),
            pltpu.VMEM(off.shape, BF16),
            pltpu.SMEM(parent_of.shape, jnp.int32),
            pltpu.VMEM((parents, width, sides), F32),
            pltpu.VMEM((parents, width, sides), F32),
            pltpu.VMEM((parents, sides, width), F32),
            pltpu.SemaphoreType.DMA((3, len(groups))),
            pltpu.SemaphoreType.DMA,
        ],
        compiler_params=params(room),
        name="forward",
    )(*(pltpu.with_memory_space_constraint(x, pltpu.HBM) for x in (parent_of, rhs, inv, off)))


def couple_kernel(inv, off, _, out):
    for c in range(out.shape[0]):
        out[c] = (-dot(inv[c], off[c])).astype(BF16)


def couple(inv, off, after):
    count, width, _ = inv.shape
    return pl.pallas_call(
        couple_kernel,
        out_shape=pltpu.VMEM(off.shape, BF16),
        in_specs=[VMEM, VMEM, ANY],
        out_specs=VMEM,
        compiler_params=params(16),
        cost_estimate=pl.CostEstimate(
            flops=2 * count * width**3, bytes_accessed=6 * count * width**2, transcendentals=0
        ),
        name="couple",
    )(inv, off, after)


def core_sum_kernel(*refs):
    total = refs[0][...]
    for part in refs[1:-1]:
        total = total + part[...].astype(F32)
    refs[-1][...] = total.astype(BF16)


def core_sum(parts):
    return pl.pallas_call(
        core_sum_kernel,
        out_shape=jax.ShapeDtypeStruct(parts[0].shape, BF16),
        in_specs=[VMEM] * len(parts),
        out_specs=VMEM,
        compiler_params=params(16),
        cost_estimate=WAIT,
        name="core_sum",
    )(*parts)


def parent_kernel(cores, rhs, lower, upper, parts, out, turned):
    devices, per_col, half, _ = out.shape
    slab = cores * half
    rows = pl.ds(pl.multiple_of(lax.axis_index("row") * slab, slab), slab)
    for p in range(per_col):
        updates = []
        for k in range(cores):
            update = parts[k, p].astype(F32)
            for d in range(k + cores, devices, cores):
                update = update + parts[d, p].astype(F32)
            updates.append(update)
        turned[...] = rhs[p].astype(F32).T
        residual = (turned[rows, :] - jnp.concatenate(updates)).astype(BF16)
        fwd = dot_t(residual, lower[p]).astype(BF16)
        solved = dot_t(fwd, upper[p]).astype(BF16)
        for d in range(devices):
            k = d % cores
            out[d, p] = solved[k * half : (k + 1) * half]


def parent_solve(rhs, lower, upper, parts, cores):
    _, width, sides = rhs.shape
    return pl.pallas_call(
        functools.partial(parent_kernel, cores),
        out_shape=jax.ShapeDtypeStruct(parts.shape, BF16),
        in_specs=[VMEM] * 4,
        out_specs=VMEM,
        scratch_shapes=[pltpu.VMEM((sides, width), F32)],
        compiler_params=params(16),
        cost_estimate=WAIT,
        name="parent_solve",
    )(rhs, lower, upper, parts)


def backward_kernel(cores, groups, owner_any, fwd, inv, coupled, *rest):
    parts, scratch = rest[:cores], rest[cores:]
    out_hbm, solved_hbm, out, flat, picked, owner, out_sem, small_sem = scratch
    n_row, parents, half, _ = parts[0].shape
    per_col = solved_hbm.shape[0]
    names = pltpu.make_async_copy(owner_any, owner, small_sem.at[0])
    names.start()
    me = lax.axis_index("core")
    for k in range(cores):
        for r in range(n_row):
            start = (r * cores + lax.rem(me + k, cores)) * half
            rows = pl.ds(pl.multiple_of(start, half), half)
            flat[:, rows, :] = parts[k][r].astype(F32)
    for p in range(parents):
        picked[p] = flat[p].T.astype(BF16)
    mine = (lax.axis_index("z") * cores + me) * per_col
    solved = pltpu.make_async_copy(picked.at[pl.ds(mine, per_col)], solved_hbm, small_sem.at[1])
    solved.start()
    names.wait()
    stores = [solved]
    for g, (lo, hi) in enumerate(groups):
        for c in range(lo, hi):
            mats = jnp.concatenate([inv[c], coupled[c]], axis=1)
            out[c] = dot(mats, jnp.concatenate([fwd[c], picked[owner[c]]])).astype(BF16)
        part = pl.ds(lo, hi - lo)
        copy = pltpu.make_async_copy(out.at[part], out_hbm.at[part], out_sem.at[g])
        copy.start(priority=g % 2)
        stores.append(copy)
    for copy in stores:
        copy.wait()


def backward(parent_of, fwd, inv, coupled, parts, per_col):
    count, width, sides = fwd.shape
    groups = ranges(count, (1, 2, 2, 1))
    parents = parts[0].shape[1]
    return pl.pallas_call(
        functools.partial(backward_kernel, len(parts), groups),
        out_shape=[
            jax.ShapeDtypeStruct(fwd.shape, BF16),
            jax.ShapeDtypeStruct((per_col, width, sides), BF16),
        ],
        in_specs=[ANY] + [VMEM] * (3 + len(parts)),
        out_specs=[ANY, ANY],
        scratch_shapes=[
            pltpu.VMEM(fwd.shape, BF16),
            pltpu.VMEM((parents, sides, width), F32),
            pltpu.VMEM((parents, width, sides), BF16),
            pltpu.SMEM(parent_of.shape, jnp.int32),
            pltpu.SemaphoreType.DMA((len(groups),)),
            pltpu.SemaphoreType.DMA((2,)),
        ],
        compiler_params=params(32),
        name="backward",
    )(parent_of, fwd, inv, coupled, *parts)


def from_core(value, k):
    cores = lax.axis_size("core")
    return lax.ppermute(value, "core", [(i, (i + k) % cores) for i in range(cores)])


def on_device(
    child_rhs,
    parent_rhs,
    child_lower_inv,
    child_lower_off,
    child_upper_inv,
    child_upper_off,
    parent_lower_inv,
    parent_upper_inv,
    parent_of,
):
    n_row, n_chip, cores = (lax.axis_size(a) for a in ("row", "z", "core"))
    per_col = parent_rhs.shape[0]
    fwd, mine, *theirs = forward(
        parent_of, child_rhs, child_lower_inv, child_lower_off, n_row, n_chip, cores, per_col
    )
    theirs = [from_core(x, k) for k, x in enumerate(theirs, 1)]
    total = core_sum([mine] + theirs)
    axes = ("row", "z", "core")
    sent = total.reshape(-1, per_col, *total.shape[2:])
    parts = lax.all_to_all(sent, axes, 0, 0, tiled=True)
    solved = parent_solve(parent_rhs, parent_lower_inv, parent_upper_inv, parts, cores)
    mine = lax.all_to_all(solved, axes, 0, 0, tiled=True).reshape(total.shape)
    parts = [mine] + [from_core(mine, cores - k) for k in range(1, cores)]
    coupled = couple(child_upper_inv, child_upper_off, mine)
    return tuple(backward(parent_of, fwd, child_upper_inv, coupled, parts, per_col))


def solution(mesh):
    n_row, n_col = (mesh.shape[a] for a in ("row", "col"))
    cores = 1 if n_col % 2 else 2
    split = Mesh(mesh.devices.reshape(n_row, n_col // cores, cores), ("row", "z", "core"))
    child = P(("row", "z", "core"), None, None)
    parent = P(("z", "core"), None, None)
    return jax.shard_map(
        on_device,
        mesh=split,
        in_specs=(child, parent, child, child, child, child, parent, parent, P(("row", "z", "core"))),
        out_specs=(child, parent),
        check_vma=False,
    )
```

```python
import functools
import math
import jax
import jax.numpy as jnp
from jax import lax
from jax.experimental import pallas as pl
from jax.experimental.pallas import tpu as pltpu
from jax.sharding import Mesh, PartitionSpec as P

F32 = jnp.float32
BF16 = jnp.bfloat16
VMEM = pl.BlockSpec(memory_space=pltpu.VMEM)
ANY = pl.BlockSpec(memory_space=pl.ANY)
MIB = 1 << 20
VMEM_BYTES = 64 * MIB
WAIT = pl.CostEstimate(flops=8 * 10**9, bytes_accessed=MIB, transcendentals=0)


def ranges(count, shares):
    ends = [count * sum(shares[: i + 1]) // sum(shares) for i in range(len(shares))]
    pairs = zip([0] + ends[:-1], ends)
    return [(lo, hi) for lo, hi in pairs if hi > lo]


def params(mib):
    return pltpu.CompilerParams(vmem_limit_bytes=mib * MIB)


def dot(a, b):
    return jnp.dot(a, b, preferred_element_type=F32)


def dot_t(a, b):
    return lax.dot_general(a, b, (((1,), (1,)), ((), ())), preferred_element_type=F32)


def forward_kernel(cores, groups, owner_hbm, rhs_hbm, inv_hbm, off_hbm, fwd, *rest):
    mine, theirs, scratch = rest[0], rest[1:cores], rest[cores:]
    rhs, inv, off, owner, even, odd, flat, in_sem, owner_sem = scratch
    n_row, _, half, _ = mine.shape
    slab = half * cores
    arrays = ((rhs_hbm, rhs), (inv_hbm, inv), (off_hbm, off))

    def load(s, g):
        lo, hi = groups[g]
        part = pl.ds(lo, hi - lo)
        return pltpu.make_async_copy(arrays[s][0].at[part], arrays[s][1].at[part], in_sem.at[s, g])

    names = pltpu.make_async_copy(owner_hbm, owner, owner_sem)
    last = len(groups)
    for g in range(last + 1):
        if g < last:
            load(0, g).start()
            load(1, g).start()
        if g == 0:
            names.start()
        else:
            load(2, g - 1).start()
    even[...] = jnp.zeros_like(even)
    odd[...] = jnp.zeros_like(odd)

    def solve(c):
        fwd[c] = dot(inv[c], rhs[c]).astype(BF16)

    def add(c):
        acc = odd if c % 2 else even
        acc[owner[c]] += dot(off[c], fwd[c])

    def add_turned(c):
        flat[owner[c]] += dot(off[c], fwd[c]).T

    late = []
    for g in range(last + 1):
        if g < last:
            load(0, g).wait()
            load(1, g).wait()
        if g == 1:
            names.wait()
        if g:
            load(2, g - 1).wait()
        put = add_turned if g - 1 >= last - 2 else add
        now = list(range(*groups[g])) if g < last else []
        for n in range(max(len(now), len(late))):
            if n < len(now):
                solve(now[n])
            if n < len(late):
                put(late[n])
        late = now
        if g == max(last - 2, 0):
            for p in range(flat.shape[0]):
                flat[p] = (even[p] + odd[p]).T
    me = lax.axis_index("core")
    for k in range(cores):
        out = theirs[k - 1] if k else mine
        for r in range(n_row):
            start = r * slab + lax.rem(me + k, cores) * half
            rows = pl.ds(pl.multiple_of(start, half), half)
            out[r] = flat[:, rows, :].astype(out.dtype)


def forward(parent_of, rhs, inv, off, n_row, n_chip, cores, per_col):
    count, width, sides = rhs.shape
    groups = ranges(count, (2, 3, 3, 2, 1, 1))
    parents = n_chip * cores * per_col
    piece = (n_row, parents, sides // (n_row * cores), width)
    kept = 2 * rhs.size + (2 + 2 * cores) * math.prod(piece)
    room = (VMEM_BYTES - kept - MIB) // MIB
    return pl.pallas_call(
        functools.partial(forward_kernel, cores, groups),
        out_shape=[pltpu.VMEM(rhs.shape, BF16), pltpu.VMEM(piece, F32)]
        + [pltpu.VMEM(piece, BF16)] * (cores - 1),
        in_specs=[ANY] * 4,
        out_specs=[VMEM] * (1 + cores),
        scratch_shapes=[
            pltpu.VMEM(rhs.shape, BF16),
            pltpu.VMEM(inv.shape, BF16),
            pltpu.VMEM(off.shape, BF16),
            pltpu.SMEM(parent_of.shape, jnp.int32),
            pltpu.VMEM((parents, width, sides), F32),
            pltpu.VMEM((parents, width, sides), F32),
            pltpu.VMEM((parents, sides, width), F32),
            pltpu.SemaphoreType.DMA((3, len(groups))),
            pltpu.SemaphoreType.DMA,
        ],
        compiler_params=params(room),
        name="forward",
    )(*(pltpu.with_memory_space_constraint(x, pltpu.HBM) for x in (parent_of, rhs, inv, off)))


def couple_kernel(inv, off, _, out):
    for c in range(out.shape[0]):
        out[c] = (-dot(inv[c], off[c])).astype(BF16)


def couple(inv, off, after):
    count, width, _ = inv.shape
    return pl.pallas_call(
        couple_kernel,
        out_shape=pltpu.VMEM(off.shape, BF16),
        in_specs=[VMEM, VMEM, ANY],
        out_specs=VMEM,
        compiler_params=params(16),
        cost_estimate=pl.CostEstimate(
            flops=2 * count * width**3, bytes_accessed=6 * count * width**2, transcendentals=0
        ),
        name="couple",
    )(inv, off, after)


def core_sum_kernel(*refs):
    total = refs[0][...]
    for part in refs[1:-2]:
        total = total + part[...].astype(F32)
    refs[-1][...] = total.astype(BF16)


def core_sum(parts, after):
    return pl.pallas_call(
        core_sum_kernel,
        out_shape=jax.ShapeDtypeStruct(parts[0].shape, BF16),
        in_specs=[VMEM] * len(parts) + [ANY],
        out_specs=VMEM,
        compiler_params=params(16),
        cost_estimate=WAIT,
        name="core_sum",
    )(*parts, after)


def prepare_kernel(rhs, lower, upper, _, whole, mine, turned):
    slab = mine.shape[1]
    rows = pl.ds(pl.multiple_of(lax.axis_index("row") * slab, slab), slab)
    for p in range(mine.shape[0]):
        whole[p] = dot(upper[p], lower[p]).astype(BF16)
        turned[...] = rhs[p].astype(F32).T
        mine[p] = turned[rows, :]


def prepare(rhs, lower, upper, after, n_row):
    per_col, width, sides = rhs.shape
    return pl.pallas_call(
        prepare_kernel,
        out_shape=[
            jax.ShapeDtypeStruct(lower.shape, BF16),
            jax.ShapeDtypeStruct((per_col, sides // n_row, width), F32),
        ],
        in_specs=[VMEM] * 3 + [ANY],
        out_specs=[VMEM, VMEM],
        scratch_shapes=[pltpu.VMEM((sides, width), F32)],
        compiler_params=params(16),
        name="prepare",
    )(rhs, lower, upper, after)


def parent_kernel(cores, whole, rhs, parts, out):
    devices, per_col, half, _ = out.shape
    for p in range(per_col):
        updates = []
        for k in range(cores):
            terms = [parts[d, p].astype(F32) for d in range(k, devices, cores)]
            while len(terms) > 1:
                pairs = zip(terms[::2], terms[1::2])
                terms = [x + y for x, y in pairs] + terms[len(terms) - len(terms) % 2 :]
            updates.append(terms[0])
        residual = (rhs[p] - jnp.concatenate(updates)).astype(BF16)
        solved = dot_t(residual, whole[p]).astype(BF16)
        for d in range(devices):
            k = d % cores
            out[d, p] = solved[k * half : (k + 1) * half]


def parent_solve(whole, rhs, parts, cores):
    return pl.pallas_call(
        functools.partial(parent_kernel, cores),
        out_shape=jax.ShapeDtypeStruct(parts.shape, BF16),
        in_specs=[VMEM] * 3,
        out_specs=VMEM,
        compiler_params=params(16),
        cost_estimate=WAIT,
        name="parent_solve",
    )(whole, rhs, parts)


def backward_kernel(cores, groups, owner_any, fwd, inv, coupled, *rest):
    parts, scratch = rest[:cores], rest[cores:]
    out_hbm, solved_hbm, out, flat, picked, owner, out_sem, small_sem = scratch
    n_row, parents, half, _ = parts[0].shape
    per_col = solved_hbm.shape[0]
    names = pltpu.make_async_copy(owner_any, owner, small_sem.at[0])
    names.start()
    me = lax.axis_index("core")
    for k in range(cores):
        for r in range(n_row):
            start = (r * cores + lax.rem(me + k, cores)) * half
            rows = pl.ds(pl.multiple_of(start, half), half)
            flat[:, rows, :] = parts[k][r]
    for p in range(parents):
        picked[p] = flat[p].T
    mine = (lax.axis_index("z") * cores + me) * per_col
    solved = pltpu.make_async_copy(picked.at[pl.ds(mine, per_col)], solved_hbm, small_sem.at[1])
    solved.start()
    names.wait()
    stores = [solved]
    for g, (lo, hi) in enumerate(groups):
        for c in range(lo, hi):
            mats = jnp.concatenate([inv[c], coupled[c]], axis=1)
            out[c] = dot(mats, jnp.concatenate([fwd[c], picked[owner[c]]])).astype(BF16)
        part = pl.ds(lo, hi - lo)
        copy = pltpu.make_async_copy(out.at[part], out_hbm.at[part], out_sem.at[g])
        copy.start()
        stores.append(copy)
    for copy in stores:
        copy.wait()


def backward(parent_of, fwd, inv, coupled, parts, per_col):
    count, width, sides = fwd.shape
    groups = ranges(count, (1, 2, 3, 3, 2, 1))
    parents = parts[0].shape[1]
    return pl.pallas_call(
        functools.partial(backward_kernel, len(parts), groups),
        out_shape=[
            jax.ShapeDtypeStruct(fwd.shape, BF16),
            jax.ShapeDtypeStruct((per_col, width, sides), BF16),
        ],
        in_specs=[ANY] + [VMEM] * (3 + len(parts)),
        out_specs=[ANY, ANY],
        scratch_shapes=[
            pltpu.VMEM(fwd.shape, BF16),
            pltpu.VMEM((parents, sides, width), BF16),
            pltpu.VMEM((parents, width, sides), BF16),
            pltpu.SMEM(parent_of.shape, jnp.int32),
            pltpu.SemaphoreType.DMA((len(groups),)),
            pltpu.SemaphoreType.DMA((2,)),
        ],
        compiler_params=params(32),
        name="backward",
    )(parent_of, fwd, inv, coupled, *parts)


def from_core(value, k):
    cores = lax.axis_size("core")
    return lax.ppermute(value, "core", [(i, (i + k) % cores) for i in range(cores)])


def on_device(
    child_rhs,
    parent_rhs,
    child_lower_inv,
    child_lower_off,
    child_upper_inv,
    child_upper_off,
    parent_lower_inv,
    parent_upper_inv,
    parent_of,
):
    n_row, n_chip, cores = (lax.axis_size(a) for a in ("row", "z", "core"))
    per_col = parent_rhs.shape[0]
    fwd, mine, *theirs = forward(
        parent_of, child_rhs, child_lower_inv, child_lower_off, n_row, n_chip, cores, per_col
    )
    theirs = [from_core(x, k) for k, x in enumerate(theirs, 1)]
    whole, rhs = prepare(parent_rhs, parent_lower_inv, parent_upper_inv, mine, n_row)
    total = core_sum([mine] + theirs, whole)
    axes = ("row", "z", "core")
    sent = total.reshape(-1, per_col, *total.shape[2:])
    parts = lax.all_to_all(sent, axes, 0, 0, tiled=True)
    solved = parent_solve(whole, rhs, parts, cores)
    mine = lax.all_to_all(solved, axes, 0, 0, tiled=True).reshape(total.shape)
    parts = [mine] + [from_core(mine, cores - k) for k in range(1, cores)]
    coupled = couple(child_upper_inv, child_upper_off, mine)
    return tuple(backward(parent_of, fwd, child_upper_inv, coupled, parts, per_col))


def solution(mesh):
    n_row, n_col = (mesh.shape[a] for a in ("row", "col"))
    cores = 1 if n_col % 2 else 2
    split = Mesh(mesh.devices.reshape(n_row, n_col // cores, cores), ("row", "z", "core"))
    child = P(("row", "z", "core"), None, None)
    parent = P(("z", "core"), None, None)
    return jax.shard_map(
        on_device,
        mesh=split,
        in_specs=(child, parent, child, child, child, child, parent, parent, P(("row", "z", "core"))),
        out_specs=(child, parent),
        check_vma=False,
    )
```

```python
import functools
import math
import jax
import jax.numpy as jnp
from jax import lax
from jax.experimental import pallas as pl
from jax.experimental.pallas import tpu as pltpu
from jax.sharding import Mesh, PartitionSpec as P

F32 = jnp.float32
BF16 = jnp.bfloat16
VMEM = pl.BlockSpec(memory_space=pltpu.VMEM)
ANY = pl.BlockSpec(memory_space=pl.ANY)
MIB = 1 << 20
VMEM_BYTES = 64 * MIB
WAIT = pl.CostEstimate(flops=8 * 10**9, bytes_accessed=MIB, transcendentals=0)


def ranges(count, shares):
    ends = [count * sum(shares[: i + 1]) // sum(shares) for i in range(len(shares))]
    pairs = zip([0] + ends[:-1], ends)
    return [(lo, hi) for lo, hi in pairs if hi > lo]


def params(mib):
    return pltpu.CompilerParams(vmem_limit_bytes=mib * MIB)


def dot(a, b):
    return jnp.dot(a, b, preferred_element_type=F32)


def dot_t(a, b):
    return lax.dot_general(a, b, (((1,), (1,)), ((), ())), preferred_element_type=F32)


def forward_kernel(cores, groups, owner_hbm, rhs_hbm, inv_hbm, off_hbm, fwd, *rest):
    mine, theirs, scratch = rest[0], rest[1:cores], rest[cores:]
    rhs, inv, off, owner, even, odd, in_sem, owner_sem = scratch
    n_row, _, half, _ = mine.shape
    loads = [
        [
            pltpu.make_async_copy(h.at[pl.ds(lo, hi - lo)], v.at[pl.ds(lo, hi - lo)], in_sem.at[s, g])
            for s, (h, v) in enumerate(((rhs_hbm, rhs), (inv_hbm, inv), (off_hbm, off)))
        ]
        for g, (lo, hi) in enumerate(groups)
    ]
    names = pltpu.make_async_copy(owner_hbm, owner, owner_sem)
    for g, group in enumerate(loads):
        for copy in group:
            copy.start()
        if g == 0:
            names.start()
    even[...] = jnp.zeros_like(even)
    odd[...] = jnp.zeros_like(odd)

    def solve(c):
        fwd[c] = dot(inv[c], rhs[c]).astype(BF16)

    def add(c):
        acc = odd if c % 2 else even
        acc[owner[c]] += dot(off[c], fwd[c])

    late = []
    for g, (lo, hi) in enumerate(groups):
        for copy in loads[g]:
            copy.wait()
        for c in range(lo, hi):
            solve(c)
            if late:
                add(late.pop(0))
        if g == 0:
            names.wait()
        for c in late:
            add(c)
        late = list(range(lo, hi))
    for c in late:
        add(c)
    me = lax.axis_index("core")
    for p in range(even.shape[0]):
        turned = (even[p] + odd[p]).T
        for r in range(n_row):
            halves = [turned[n * half : (n + 1) * half] for n in range(r * cores, (r + 1) * cores)]
            for k in range(cores):
                out = theirs[k - 1] if k else mine
                value = halves[0]
                for n in range(1, cores):
                    value = jnp.where(lax.rem(me + k, cores) == n, halves[n], value)
                out[r, p] = value.astype(out.dtype)


def forward(parent_of, rhs, inv, off, n_row, n_chip, cores, per_col):
    count, width, sides = rhs.shape
    groups = ranges(count, (2, 3, 3, 2, 1, 1))
    parents = n_chip * cores * per_col
    piece = (n_row, parents, sides // (n_row * cores), width)
    kept = 2 * rhs.size + (2 + 2 * cores) * math.prod(piece)
    room = (VMEM_BYTES - kept - MIB) // MIB
    return pl.pallas_call(
        functools.partial(forward_kernel, cores, groups),
        out_shape=[pltpu.VMEM(rhs.shape, BF16), pltpu.VMEM(piece, F32)]
        + [pltpu.VMEM(piece, BF16)] * (cores - 1),
        in_specs=[ANY] * 4,
        out_specs=[VMEM] * (1 + cores),
        scratch_shapes=[
            pltpu.VMEM(rhs.shape, BF16),
            pltpu.VMEM(inv.shape, BF16),
            pltpu.VMEM(off.shape, BF16),
            pltpu.SMEM(parent_of.shape, jnp.int32),
            pltpu.VMEM((parents, width, sides), F32),
            pltpu.VMEM((parents, width, sides), F32),
            pltpu.SemaphoreType.DMA((3, len(groups))),
            pltpu.SemaphoreType.DMA,
        ],
        compiler_params=params(room),
        name="forward",
    )(*(pltpu.with_memory_space_constraint(x, pltpu.HBM) for x in (parent_of, rhs, inv, off)))


def couple_kernel(inv, off, _, out):
    for c in range(out.shape[0]):
        out[c] = (-dot(inv[c], off[c])).astype(BF16)


def couple(inv, off, after):
    count, width, _ = inv.shape
    return pl.pallas_call(
        couple_kernel,
        out_shape=pltpu.VMEM(off.shape, BF16),
        in_specs=[VMEM, VMEM, ANY],
        out_specs=VMEM,
        compiler_params=params(16),
        cost_estimate=pl.CostEstimate(
            flops=2 * count * width**3, bytes_accessed=6 * count * width**2, transcendentals=0
        ),
        name="couple",
    )(inv, off, after)


def core_sum_kernel(*refs):
    total = refs[0][...]
    for part in refs[1:-2]:
        total = total + part[...].astype(F32)
    refs[-1][...] = total.astype(BF16)


def core_sum(parts, after):
    return pl.pallas_call(
        core_sum_kernel,
        out_shape=jax.ShapeDtypeStruct(parts[0].shape, BF16),
        in_specs=[VMEM] * len(parts) + [ANY],
        out_specs=VMEM,
        compiler_params=params(16),
        cost_estimate=WAIT,
        name="core_sum",
    )(*parts, after)


def prepare_kernel(rhs, lower, upper, _, whole, mine, turned):
    slab = mine.shape[1]
    rows = pl.ds(pl.multiple_of(lax.axis_index("row") * slab, slab), slab)
    for p in range(mine.shape[0]):
        whole[p] = dot(upper[p], lower[p]).astype(BF16)
        turned[...] = rhs[p].astype(F32).T
        mine[p] = turned[rows, :]


def prepare(rhs, lower, upper, after, n_row):
    per_col, width, sides = rhs.shape
    return pl.pallas_call(
        prepare_kernel,
        out_shape=[
            jax.ShapeDtypeStruct(lower.shape, BF16),
            jax.ShapeDtypeStruct((per_col, sides // n_row, width), F32),
        ],
        in_specs=[VMEM] * 3 + [ANY],
        out_specs=[VMEM, VMEM],
        scratch_shapes=[pltpu.VMEM((sides, width), F32)],
        compiler_params=params(16),
        name="prepare",
    )(rhs, lower, upper, after)


def parent_kernel(cores, whole, rhs, parts, out):
    devices, per_col, half, _ = out.shape
    for p in range(per_col):
        updates = []
        for k in range(cores):
            terms = [parts[d, p].astype(F32) for d in range(k, devices, cores)]
            while len(terms) > 1:
                pairs = zip(terms[::2], terms[1::2])
                terms = [x + y for x, y in pairs] + terms[len(terms) - len(terms) % 2 :]
            updates.append(terms[0])
        residual = (rhs[p] - jnp.concatenate(updates)).astype(BF16)
        solved = dot_t(residual, whole[p]).astype(BF16)
        for d in range(devices):
            k = d % cores
            out[d, p] = solved[k * half : (k + 1) * half]


def parent_solve(whole, rhs, parts, cores):
    return pl.pallas_call(
        functools.partial(parent_kernel, cores),
        out_shape=jax.ShapeDtypeStruct(parts.shape, BF16),
        in_specs=[VMEM] * 3,
        out_specs=VMEM,
        compiler_params=params(16),
        cost_estimate=WAIT,
        name="parent_solve",
    )(whole, rhs, parts)


def backward_kernel(cores, groups, owner, fwd, inv, coupled, *rest):
    parts, scratch = rest[:cores], rest[cores:]
    out_hbm, solved_hbm, out, flat, picked, out_sem, solved_sem = scratch
    n_row, parents, half, _ = parts[0].shape
    per_col = solved_hbm.shape[0]
    me = lax.axis_index("core")
    for k in range(cores):
        for r in range(n_row):
            start = (r * cores + lax.rem(me + k, cores)) * half
            rows = pl.ds(pl.multiple_of(start, half), half)
            flat[:, rows, :] = parts[k][r]
    for p in range(parents):
        picked[p] = flat[p].T
    mine = (lax.axis_index("z") * cores + me) * per_col
    solved = pltpu.make_async_copy(picked.at[pl.ds(mine, per_col)], solved_hbm, solved_sem)
    solved.start()
    stores = [solved]
    for g, (lo, hi) in enumerate(groups):
        for c in range(lo, hi):
            mats = jnp.concatenate([inv[c], coupled[c]], axis=1)
            out[c] = dot(mats, jnp.concatenate([fwd[c], picked[owner[c]]])).astype(BF16)
        part = pl.ds(lo, hi - lo)
        copy = pltpu.make_async_copy(out.at[part], out_hbm.at[part], out_sem.at[g])
        copy.start()
        stores.append(copy)
    for copy in stores:
        copy.wait()


def backward(parent_of, fwd, inv, coupled, parts, per_col):
    count, width, sides = fwd.shape
    groups = ranges(count, (1, 2, 3, 3, 2, 1))
    parents = parts[0].shape[1]
    return pl.pallas_call(
        functools.partial(backward_kernel, len(parts), groups),
        out_shape=[
            jax.ShapeDtypeStruct(fwd.shape, BF16),
            jax.ShapeDtypeStruct((per_col, width, sides), BF16),
        ],
        in_specs=[VMEM] * (4 + len(parts)),
        out_specs=[ANY, ANY],
        scratch_shapes=[
            pltpu.VMEM(fwd.shape, BF16),
            pltpu.VMEM((parents, sides, width), BF16),
            pltpu.VMEM((parents, width, sides), BF16),
            pltpu.SemaphoreType.DMA((len(groups),)),
            pltpu.SemaphoreType.DMA,
        ],
        compiler_params=params(32),
        name="backward",
    )(parent_of, fwd, inv, coupled, *parts)


def from_core(value, k):
    cores = lax.axis_size("core")
    return lax.ppermute(value, "core", [(i, (i + k) % cores) for i in range(cores)])


def on_device(
    child_rhs,
    parent_rhs,
    child_lower_inv,
    child_lower_off,
    child_upper_inv,
    child_upper_off,
    parent_lower_inv,
    parent_upper_inv,
    parent_of,
):
    n_row, n_chip, cores = (lax.axis_size(a) for a in ("row", "z", "core"))
    per_col = parent_rhs.shape[0]
    fwd, mine, *theirs = forward(
        parent_of, child_rhs, child_lower_inv, child_lower_off, n_row, n_chip, cores, per_col
    )
    theirs = [from_core(x, k) for k, x in enumerate(theirs, 1)]
    whole, rhs = prepare(parent_rhs, parent_lower_inv, parent_upper_inv, mine, n_row)
    total = core_sum([mine] + theirs, whole)
    axes = ("row", "z", "core")
    sent = total.reshape(-1, per_col, *total.shape[2:])
    parts = lax.all_to_all(sent, axes, 0, 0, tiled=True)
    solved = parent_solve(whole, rhs, parts, cores)
    mine = lax.all_to_all(solved, axes, 0, 0, tiled=True).reshape(total.shape)
    parts = [mine] + [from_core(mine, cores - k) for k in range(1, cores)]
    coupled = couple(child_upper_inv, child_upper_off, mine)
    return tuple(backward(parent_of, fwd, child_upper_inv, coupled, parts, per_col))


def solution(mesh):
    n_row, n_col = (mesh.shape[a] for a in ("row", "col"))
    cores = 1 if n_col % 2 else 2
    split = Mesh(mesh.devices.reshape(n_row, n_col // cores, cores), ("row", "z", "core"))
    child = P(("row", "z", "core"), None, None)
    parent = P(("z", "core"), None, None)
    return jax.shard_map(
        on_device,
        mesh=split,
        in_specs=(child, parent, child, child, child, child, parent, parent, P(("row", "z", "core"))),
        out_specs=(child, parent),
        check_vma=False,
    )
```

```python
import functools
import math
import jax
import jax.numpy as jnp
from jax import lax
from jax.experimental import pallas as pl
from jax.experimental.pallas import tpu as pltpu
from jax.sharding import Mesh, PartitionSpec as P

F32 = jnp.float32
BF16 = jnp.bfloat16
VMEM = pl.BlockSpec(memory_space=pltpu.VMEM)
ANY = pl.BlockSpec(memory_space=pl.ANY)
MIB = 1 << 20
VMEM_BYTES = 64 * MIB
WAIT = pl.CostEstimate(flops=8 * 10**9, bytes_accessed=MIB, transcendentals=0)


def ranges(count, shares):
    ends = [count * sum(shares[: i + 1]) // sum(shares) for i in range(len(shares))]
    pairs = zip([0] + ends[:-1], ends)
    return [(lo, hi) for lo, hi in pairs if hi > lo]


def params(mib):
    return pltpu.CompilerParams(vmem_limit_bytes=mib * MIB)


def dot(a, b):
    return jnp.dot(a, b, preferred_element_type=F32)


def dot_t(a, b):
    return lax.dot_general(a, b, (((1,), (1,)), ((), ())), preferred_element_type=F32)


def forward_kernel(cores, groups, owner_hbm, rhs_hbm, inv_hbm, off_hbm, fwd, *rest):
    mine, theirs, scratch = rest[0], rest[1:cores], rest[cores:]
    rhs, inv, off, owner, even, odd, in_sem, owner_sem = scratch
    n_chip, n_row, span, half, _ = mine.shape
    loads = [
        [
            pltpu.make_async_copy(h.at[pl.ds(lo, hi - lo)], v.at[pl.ds(lo, hi - lo)], in_sem.at[s, g])
            for s, (h, v) in enumerate(((rhs_hbm, rhs), (inv_hbm, inv), (off_hbm, off)))
        ]
        for g, (lo, hi) in enumerate(groups)
    ]
    names = pltpu.make_async_copy(owner_hbm, owner, owner_sem)
    for g, group in enumerate(loads):
        for copy in group:
            copy.start()
        if g == 0:
            names.start()
    even[...] = jnp.zeros_like(even)
    odd[...] = jnp.zeros_like(odd)

    def solve(c):
        fwd[c] = dot(inv[c], rhs[c]).astype(BF16)

    def add(c):
        acc = odd if c % 2 else even
        acc[owner[c]] += dot(off[c], fwd[c])

    late = []
    for g, (lo, hi) in enumerate(groups):
        for copy in loads[g]:
            copy.wait()
        for c in range(lo, hi):
            solve(c)
            if late:
                add(late.pop(0))
        if g == 0:
            names.wait()
        for c in late:
            add(c)
        late = list(range(lo, hi))
    for c in late:
        add(c)
    me = lax.axis_index("core")
    for p in range(even.shape[0]):
        turned = (even[p] + odd[p]).astype(BF16).T
        for r in range(n_row):
            halves = [turned[n * half : (n + 1) * half] for n in range(r * cores, (r + 1) * cores)]
            for k in range(cores):
                out = theirs[k - 1] if k else mine
                value = halves[0]
                for n in range(1, cores):
                    value = jnp.where(lax.rem(me + k, cores) == n, halves[n], value)
                out[p // span, r, p % span] = value


def forward(parent_of, rhs, inv, off, n_row, n_chip, cores, per_col):
    count, width, sides = rhs.shape
    groups = ranges(count, (4, 6, 6, 4, 2, 1, 1))
    parents = n_chip * cores * per_col
    piece = (n_chip, n_row, cores * per_col, sides // (n_row * cores), width)
    kept = 2 * rhs.size + 2 * cores * math.prod(piece)
    room = (VMEM_BYTES - kept - MIB) // MIB
    return pl.pallas_call(
        functools.partial(forward_kernel, cores, groups),
        out_shape=[pltpu.VMEM(rhs.shape, BF16)] + [pltpu.VMEM(piece, BF16)] * cores,
        in_specs=[ANY] * 4,
        out_specs=[VMEM] * (1 + cores),
        scratch_shapes=[
            pltpu.VMEM(rhs.shape, BF16),
            pltpu.VMEM(inv.shape, BF16),
            pltpu.VMEM(off.shape, BF16),
            pltpu.SMEM(parent_of.shape, jnp.int32),
            pltpu.VMEM((parents, width, sides), F32),
            pltpu.VMEM((parents, width, sides), F32),
            pltpu.SemaphoreType.DMA((3, len(groups))),
            pltpu.SemaphoreType.DMA,
        ],
        compiler_params=params(room),
        name="forward",
    )(*(pltpu.with_memory_space_constraint(x, pltpu.HBM) for x in (parent_of, rhs, inv, off)))


def couple_kernel(inv, off, _, out):
    for c in range(out.shape[0]):
        out[c] = (-dot(inv[c], off[c])).astype(BF16)


def couple(inv, off, after):
    count, width, _ = inv.shape
    return pl.pallas_call(
        couple_kernel,
        out_shape=pltpu.VMEM(off.shape, BF16),
        in_specs=[VMEM, VMEM, ANY],
        out_specs=VMEM,
        compiler_params=params(16),
        cost_estimate=pl.CostEstimate(
            flops=2 * count * width**3, bytes_accessed=6 * count * width**2, transcendentals=0
        ),
        name="couple",
    )(inv, off, after)


def core_sum_kernel(*refs):
    total = refs[0][...].astype(F32)
    for part in refs[1:-2]:
        total = total + part[...].astype(F32)
    refs[-1][...] = total.astype(BF16)


def core_sum(parts, after):
    return pl.pallas_call(
        core_sum_kernel,
        out_shape=jax.ShapeDtypeStruct(parts[0].shape, BF16),
        in_specs=[VMEM] * len(parts) + [ANY],
        out_specs=VMEM,
        compiler_params=params(16),
        cost_estimate=WAIT,
        name="core_sum",
    )(*parts, after)


def prepare_kernel(rhs, lower, upper, _, whole, mine, turned):
    slab = mine.shape[1]
    rows = pl.ds(pl.multiple_of(lax.axis_index("row") * slab, slab), slab)
    for p in range(mine.shape[0]):
        whole[p] = dot(upper[p], lower[p]).astype(BF16)
        turned[...] = rhs[p].astype(F32).T
        mine[p] = turned[rows, :]


def prepare(rhs, lower, upper, after, n_row):
    per_col, width, sides = rhs.shape
    return pl.pallas_call(
        prepare_kernel,
        out_shape=[
            jax.ShapeDtypeStruct(lower.shape, BF16),
            jax.ShapeDtypeStruct((per_col, sides // n_row, width), F32),
        ],
        in_specs=[VMEM] * 3 + [ANY],
        out_specs=[VMEM, VMEM],
        scratch_shapes=[pltpu.VMEM((sides, width), F32)],
        compiler_params=params(16),
        name="prepare",
    )(rhs, lower, upper, after)


def parent_kernel(cores, whole, rhs, parts, out):
    devices, per_col, half, _ = out.shape
    for p in range(per_col):
        updates = []
        for k in range(cores):
            terms = [parts[d, p].astype(F32) for d in range(k, devices, cores)]
            while len(terms) > 1:
                pairs = zip(terms[::2], terms[1::2])
                terms = [x + y for x, y in pairs] + terms[len(terms) - len(terms) % 2 :]
            updates.append(terms[0])
        residual = (rhs[p] - jnp.concatenate(updates)).astype(BF16)
        solved = dot_t(residual, whole[p]).astype(BF16)
        for d in range(devices):
            k = d % cores
            out[d, p] = solved[k * half : (k + 1) * half]


def parent_solve(whole, rhs, parts, cores):
    return pl.pallas_call(
        functools.partial(parent_kernel, cores),
        out_shape=jax.ShapeDtypeStruct(parts.shape, BF16),
        in_specs=[VMEM] * 3,
        out_specs=VMEM,
        compiler_params=params(16),
        cost_estimate=WAIT,
        name="parent_solve",
    )(whole, rhs, parts)


def backward_kernel(cores, groups, owner, fwd, inv, coupled, *rest):
    parts, scratch = rest[:cores], rest[cores:]
    out_hbm, solved_hbm, out, flat, picked, out_sem, solved_sem = scratch
    n_chip, n_row, group, half, _ = parts[0].shape
    per_col = solved_hbm.shape[0]
    me = lax.axis_index("core")
    for k in range(cores):
        for r in range(n_row):
            start = (r * cores + lax.rem(me + k, cores)) * half
            rows = pl.ds(pl.multiple_of(start, half), half)
            for z in range(n_chip):
                flat[z * group : (z + 1) * group, rows, :] = parts[k][z, r]
    for p in range(n_chip * group):
        picked[p] = flat[p].T
    mine = (lax.axis_index("z") * cores + me) * per_col
    solved = pltpu.make_async_copy(picked.at[pl.ds(mine, per_col)], solved_hbm, solved_sem)
    solved.start()
    stores = [solved]
    for g, (lo, hi) in enumerate(groups):
        for c in range(lo, hi):
            mats = jnp.concatenate([inv[c], coupled[c]], axis=1)
            out[c] = dot(mats, jnp.concatenate([fwd[c], picked[owner[c]]])).astype(BF16)
        part = pl.ds(lo, hi - lo)
        copy = pltpu.make_async_copy(out.at[part], out_hbm.at[part], out_sem.at[g])
        copy.start()
        stores.append(copy)
    for copy in stores:
        copy.wait()


def backward(parent_of, fwd, inv, coupled, parts, per_col):
    count, width, sides = fwd.shape
    groups = ranges(count, (1, 2, 3, 3, 2, 1))
    parents = parts[0].shape[0] * parts[0].shape[2]
    return pl.pallas_call(
        functools.partial(backward_kernel, len(parts), groups),
        out_shape=[
            jax.ShapeDtypeStruct(fwd.shape, BF16),
            jax.ShapeDtypeStruct((per_col, width, sides), BF16),
        ],
        in_specs=[VMEM] * (4 + len(parts)),
        out_specs=[ANY, ANY],
        scratch_shapes=[
            pltpu.VMEM(fwd.shape, BF16),
            pltpu.VMEM((parents, sides, width), BF16),
            pltpu.VMEM((parents, width, sides), BF16),
            pltpu.SemaphoreType.DMA((len(groups),)),
            pltpu.SemaphoreType.DMA,
        ],
        compiler_params=params(32),
        name="backward",
    )(parent_of, fwd, inv, coupled, *parts)


def from_core(value, k):
    cores = lax.axis_size("core")
    return lax.ppermute(value, "core", [(i, (i + k) % cores) for i in range(cores)])


def on_device(
    child_rhs,
    parent_rhs,
    child_lower_inv,
    child_lower_off,
    child_upper_inv,
    child_upper_off,
    parent_lower_inv,
    parent_upper_inv,
    parent_of,
):
    n_row, n_chip, cores = (lax.axis_size(a) for a in ("row", "z", "core"))
    per_col = parent_rhs.shape[0]
    fwd, mine, *theirs = forward(
        parent_of, child_rhs, child_lower_inv, child_lower_off, n_row, n_chip, cores, per_col
    )
    theirs = [from_core(x, k) for k, x in enumerate(theirs, 1)]
    whole, rhs = prepare(parent_rhs, parent_lower_inv, parent_upper_inv, mine, n_row)
    total = core_sum([mine] + theirs, whole)
    axes = ("z", "row", "core")
    sent = total.reshape(-1, per_col, *total.shape[3:])
    parts = lax.all_to_all(sent, axes, 0, 0, tiled=True)
    solved = parent_solve(whole, rhs, parts, cores)
    mine = lax.all_to_all(solved, axes, 0, 0, tiled=True).reshape(total.shape)
    parts = [mine] + [from_core(mine, cores - k) for k in range(1, cores)]
    coupled = couple(child_upper_inv, child_upper_off, mine)
    return tuple(backward(parent_of, fwd, child_upper_inv, coupled, parts, per_col))


def solution(mesh):
    n_row, n_col = (mesh.shape[a] for a in ("row", "col"))
    cores = 1 if n_col % 2 else 2
    split = Mesh(mesh.devices.reshape(n_row, n_col // cores, cores), ("row", "z", "core"))
    child = P(("row", "z", "core"), None, None)
    parent = P(("z", "core"), None, None)
    return jax.shard_map(
        on_device,
        mesh=split,
        in_specs=(child, parent, child, child, child, child, parent, parent, P(("row", "z", "core"))),
        out_specs=(child, parent),
        check_vma=False,
    )
```

```python
import functools
import math
import jax
import jax.numpy as jnp
from jax import lax
from jax.experimental import pallas as pl
from jax.experimental.pallas import tpu as pltpu
from jax.sharding import Mesh, PartitionSpec as P

F32 = jnp.float32
BF16 = jnp.bfloat16
VMEM = pl.BlockSpec(memory_space=pltpu.VMEM)
ANY = pl.BlockSpec(memory_space=pl.ANY)
MIB = 1 << 20
VMEM_BYTES = 64 * MIB
WAIT = pl.CostEstimate(flops=8 * 10**9, bytes_accessed=MIB, transcendentals=0)


def ranges(count, shares):
    ends = [count * sum(shares[: i + 1]) // sum(shares) for i in range(len(shares))]
    pairs = zip([0] + ends[:-1], ends)
    return [(lo, hi) for lo, hi in pairs if hi > lo]


def params(mib):
    return pltpu.CompilerParams(vmem_limit_bytes=mib * MIB)


def dot(a, b):
    return jnp.dot(a, b, preferred_element_type=F32)


def dot_t(a, b):
    return lax.dot_general(a, b, (((1,), (1,)), ((), ())), preferred_element_type=F32)


def forward_kernel(cores, groups, owner_hbm, rhs_hbm, inv_hbm, off_hbm, fwd, *rest):
    mine, theirs, scratch = rest[0], rest[1:cores], rest[cores:]
    rhs, inv, off, owner, even, odd, in_sem, owner_sem = scratch
    n_row, _, half, _ = mine.shape
    loads = [
        [
            pltpu.make_async_copy(h.at[pl.ds(lo, hi - lo)], v.at[pl.ds(lo, hi - lo)], in_sem.at[s, g])
            for s, (h, v) in enumerate(((rhs_hbm, rhs), (inv_hbm, inv), (off_hbm, off)))
        ]
        for g, (lo, hi) in enumerate(groups)
    ]
    names = pltpu.make_async_copy(owner_hbm, owner, owner_sem)
    for g, group in enumerate(loads):
        for copy in group:
            copy.start()
        if g == 0:
            names.start()
    even[...] = jnp.zeros_like(even)
    odd[...] = jnp.zeros_like(odd)

    def solve(c):
        fwd[c] = dot(inv[c], rhs[c]).astype(BF16)

    def add(c):
        acc = odd if c % 2 else even
        acc[owner[c]] += dot(off[c], fwd[c])

    lag = 4
    for g, (lo, hi) in enumerate(groups):
        for copy in loads[g]:
            copy.wait()
        if g == 0:
            names.wait()
        for c in range(lo, hi + lag):
            if c < hi:
                solve(c)
            if c >= lo + lag:
                add(c - lag)
    me = lax.axis_index("core")
    for p in range(even.shape[0]):
        turned = (even[p] + odd[p]).T
        for r in range(n_row):
            halves = [turned[n * half : (n + 1) * half] for n in range(r * cores, (r + 1) * cores)]
            for k in range(cores):
                out = theirs[k - 1] if k else mine
                value = halves[0]
                for n in range(1, cores):
                    value = jnp.where(lax.rem(me + k, cores) == n, halves[n], value)
                out[r, p] = value.astype(out.dtype)


def forward(parent_of, rhs, inv, off, n_row, n_chip, cores, per_col):
    count, width, sides = rhs.shape
    groups = ranges(count, (5, 4, 2, 1))
    parents = n_chip * cores * per_col
    piece = (n_row, parents, sides // (n_row * cores), width)
    kept = 2 * rhs.size + (2 + 2 * cores) * math.prod(piece)
    room = (VMEM_BYTES - kept - MIB) // MIB
    return pl.pallas_call(
        functools.partial(forward_kernel, cores, groups),
        out_shape=[pltpu.VMEM(rhs.shape, BF16), pltpu.VMEM(piece, F32)]
        + [pltpu.VMEM(piece, BF16)] * (cores - 1),
        in_specs=[ANY] * 4,
        out_specs=[VMEM] * (1 + cores),
        scratch_shapes=[
            pltpu.VMEM(rhs.shape, BF16),
            pltpu.VMEM(inv.shape, BF16),
            pltpu.VMEM(off.shape, BF16),
            pltpu.SMEM(parent_of.shape, jnp.int32),
            pltpu.VMEM((parents, width, sides), F32),
            pltpu.VMEM((parents, width, sides), F32),
            pltpu.SemaphoreType.DMA((3, len(groups))),
            pltpu.SemaphoreType.DMA,
        ],
        compiler_params=params(room),
        name="forward",
    )(*(pltpu.with_memory_space_constraint(x, pltpu.HBM) for x in (parent_of, rhs, inv, off)))


def couple_kernel(inv, off, _, out):
    for c in range(out.shape[0]):
        out[c] = (-dot(inv[c], off[c])).astype(BF16)


def couple(inv, off, after):
    count, width, _ = inv.shape
    return pl.pallas_call(
        couple_kernel,
        out_shape=pltpu.VMEM(off.shape, BF16),
        in_specs=[VMEM, VMEM, ANY],
        out_specs=VMEM,
        compiler_params=params(16),
        cost_estimate=pl.CostEstimate(
            flops=2 * count * width**3, bytes_accessed=6 * count * width**2, transcendentals=0
        ),
        name="couple",
    )(inv, off, after)


def core_sum_kernel(*refs):
    total = refs[0][...]
    for part in refs[1:-2]:
        total = total + part[...].astype(F32)
    refs[-1][...] = total.astype(BF16)


def core_sum(parts, after):
    return pl.pallas_call(
        core_sum_kernel,
        out_shape=jax.ShapeDtypeStruct(parts[0].shape, BF16),
        in_specs=[VMEM] * len(parts) + [ANY],
        out_specs=VMEM,
        compiler_params=params(16),
        cost_estimate=WAIT,
        name="core_sum",
    )(*parts, after)


def prepare_kernel(rhs, lower, upper, _, whole, mine, turned):
    slab = mine.shape[1]
    rows = pl.ds(pl.multiple_of(lax.axis_index("row") * slab, slab), slab)
    for p in range(mine.shape[0]):
        whole[p] = dot(upper[p], lower[p]).astype(BF16)
        turned[...] = rhs[p].astype(F32).T
        mine[p] = turned[rows, :]


def prepare(rhs, lower, upper, after, n_row):
    per_col, width, sides = rhs.shape
    return pl.pallas_call(
        prepare_kernel,
        out_shape=[
            jax.ShapeDtypeStruct(lower.shape, BF16),
            jax.ShapeDtypeStruct((per_col, sides // n_row, width), F32),
        ],
        in_specs=[VMEM] * 3 + [ANY],
        out_specs=[VMEM, VMEM],
        scratch_shapes=[pltpu.VMEM((sides, width), F32)],
        compiler_params=params(16),
        name="prepare",
    )(rhs, lower, upper, after)


def parent_kernel(cores, whole, rhs, parts, out):
    devices, per_col, half, _ = out.shape
    for p in range(per_col):
        updates = []
        for k in range(cores):
            terms = [parts[d, p].astype(F32) for d in range(k, devices, cores)]
            while len(terms) > 1:
                pairs = zip(terms[::2], terms[1::2])
                terms = [x + y for x, y in pairs] + terms[len(terms) - len(terms) % 2 :]
            updates.append(terms[0])
        residual = (rhs[p] - jnp.concatenate(updates)).astype(BF16)
        solved = dot_t(residual, whole[p]).astype(BF16)
        for d in range(devices):
            k = d % cores
            out[d, p] = solved[k * half : (k + 1) * half]


def parent_solve(whole, rhs, parts, cores):
    return pl.pallas_call(
        functools.partial(parent_kernel, cores),
        out_shape=jax.ShapeDtypeStruct(parts.shape, BF16),
        in_specs=[VMEM] * 3,
        out_specs=VMEM,
        compiler_params=params(16),
        cost_estimate=WAIT,
        name="parent_solve",
    )(whole, rhs, parts)


def backward_kernel(cores, groups, owner, fwd, inv, coupled, *rest):
    parts, scratch = rest[:cores], rest[cores:]
    out_hbm, solved_hbm, out, flat, picked, out_sem, solved_sem = scratch
    n_row, parents, half, _ = parts[0].shape
    per_col = solved_hbm.shape[0]
    me = lax.axis_index("core")
    for k in range(cores):
        for r in range(n_row):
            start = (r * cores + lax.rem(me + k, cores)) * half
            rows = pl.ds(pl.multiple_of(start, half), half)
            flat[:, rows, :] = parts[k][r]
    for p in range(parents):
        picked[p] = flat[p].T
    mine = (lax.axis_index("z") * cores + me) * per_col
    solved = pltpu.make_async_copy(picked.at[pl.ds(mine, per_col)], solved_hbm, solved_sem)
    solved.start()
    stores = [solved]
    for g, (lo, hi) in enumerate(groups):
        for c in range(lo, hi):
            mats = jnp.concatenate([inv[c], coupled[c]], axis=1)
            out[c] = dot(mats, jnp.concatenate([fwd[c], picked[owner[c]]])).astype(BF16)
        part = pl.ds(lo, hi - lo)
        copy = pltpu.make_async_copy(out.at[part], out_hbm.at[part], out_sem.at[g])
        copy.start()
        stores.append(copy)
    for copy in stores:
        copy.wait()


def backward(parent_of, fwd, inv, coupled, parts, per_col):
    count, width, sides = fwd.shape
    groups = ranges(count, (1, 2, 3, 3, 2, 1))
    parents = parts[0].shape[1]
    return pl.pallas_call(
        functools.partial(backward_kernel, len(parts), groups),
        out_shape=[
            jax.ShapeDtypeStruct(fwd.shape, BF16),
            jax.ShapeDtypeStruct((per_col, width, sides), BF16),
        ],
        in_specs=[VMEM] * (4 + len(parts)),
        out_specs=[ANY, ANY],
        scratch_shapes=[
            pltpu.VMEM(fwd.shape, BF16),
            pltpu.VMEM((parents, sides, width), BF16),
            pltpu.VMEM((parents, width, sides), BF16),
            pltpu.SemaphoreType.DMA((len(groups),)),
            pltpu.SemaphoreType.DMA,
        ],
        compiler_params=params(32),
        name="backward",
    )(parent_of, fwd, inv, coupled, *parts)


def from_core(value, k):
    cores = lax.axis_size("core")
    return lax.ppermute(value, "core", [(i, (i + k) % cores) for i in range(cores)])


def on_device(
    child_rhs,
    parent_rhs,
    child_lower_inv,
    child_lower_off,
    child_upper_inv,
    child_upper_off,
    parent_lower_inv,
    parent_upper_inv,
    parent_of,
):
    n_row, n_chip, cores = (lax.axis_size(a) for a in ("row", "z", "core"))
    per_col = parent_rhs.shape[0]
    fwd, mine, *theirs = forward(
        parent_of, child_rhs, child_lower_inv, child_lower_off, n_row, n_chip, cores, per_col
    )
    theirs = [from_core(x, k) for k, x in enumerate(theirs, 1)]
    whole, rhs = prepare(parent_rhs, parent_lower_inv, parent_upper_inv, mine, n_row)
    total = core_sum([mine] + theirs, whole)
    axes = ("row", "z", "core")
    sent = total.reshape(-1, per_col, *total.shape[2:])
    parts = lax.all_to_all(sent, axes, 0, 0, tiled=True)
    solved = parent_solve(whole, rhs, parts, cores)
    mine = lax.all_to_all(solved, axes, 0, 0, tiled=True).reshape(total.shape)
    parts = [mine] + [from_core(mine, cores - k) for k in range(1, cores)]
    coupled = couple(child_upper_inv, child_upper_off, mine)
    return tuple(backward(parent_of, fwd, child_upper_inv, coupled, parts, per_col))


def solution(mesh):
    n_row, n_col = (mesh.shape[a] for a in ("row", "col"))
    cores = 1 if n_col % 2 else 2
    split = Mesh(mesh.devices.reshape(n_row, n_col // cores, cores), ("row", "z", "core"))
    child = P(("row", "z", "core"), None, None)
    parent = P(("z", "core"), None, None)
    return jax.shard_map(
        on_device,
        mesh=split,
        in_specs=(child, parent, child, child, child, child, parent, parent, P(("row", "z", "core"))),
        out_specs=(child, parent),
        check_vma=False,
    )
```

```python
import functools
import math
import jax
import jax.numpy as jnp
from jax import lax
from jax.experimental import pallas as pl
from jax.experimental.pallas import tpu as pltpu
from jax.sharding import Mesh, PartitionSpec as P

F32 = jnp.float32
BF16 = jnp.bfloat16
VMEM = pl.BlockSpec(memory_space=pltpu.VMEM)
ANY = pl.BlockSpec(memory_space=pl.ANY)
MIB = 1 << 20
VMEM_BYTES = 64 * MIB
WAIT = pl.CostEstimate(flops=8 * 10**9, bytes_accessed=MIB, transcendentals=0)


def ranges(count, shares):
    ends = [count * sum(shares[: i + 1]) // sum(shares) for i in range(len(shares))]
    pairs = zip([0] + ends[:-1], ends)
    return [(lo, hi) for lo, hi in pairs if hi > lo]


def params(mib):
    return pltpu.CompilerParams(vmem_limit_bytes=mib * MIB)


def dot(a, b):
    return jnp.dot(a, b, preferred_element_type=F32)


def dot_t(a, b):
    return lax.dot_general(a, b, (((1,), (1,)), ((), ())), preferred_element_type=F32)


def forward_kernel(cores, chunk, owner_hbm, rhs_hbm, inv_hbm, off_hbm, fwd, *rest):
    mine, theirs, scratch = rest[0], rest[1:cores], rest[cores:]
    rhs, inv, off, owner, even, odd, in_sem, owner_sem = scratch
    n_row, _, half, _ = mine.shape
    groups = fwd.shape[0] // chunk
    arrays = ((rhs_hbm, rhs), (inv_hbm, inv), (off_hbm, off))

    def loads(g):
        part = pl.ds(g * chunk, chunk)
        return [
            pltpu.make_async_copy(h.at[part], v.at[part], in_sem.at[s, g])
            for s, (h, v) in enumerate(arrays)
        ]

    names = pltpu.make_async_copy(owner_hbm, owner, owner_sem)
    names.start()

    @pl.loop(0, groups)
    def _(g):
        for copy in loads(g):
            copy.start()

    even[...] = jnp.zeros_like(even)
    odd[...] = jnp.zeros_like(odd)

    def solve(c):
        fwd[c] = dot(inv[c], rhs[c]).astype(BF16)

    def add(c, acc):
        acc[owner[c]] += dot(off[c], fwd[c])

    for copy in loads(0):
        copy.wait()
    for n in range(chunk):
        solve(n)
    names.wait()

    @pl.loop(1, groups)
    def _(g):
        for copy in loads(g):
            copy.wait()
        for n in range(chunk):
            solve(g * chunk + n)
            add((g - 1) * chunk + n, odd if n % 2 else even)

    for n in range(chunk):
        add((groups - 1) * chunk + n, odd if n % 2 else even)
    me = lax.axis_index("core")
    for p in range(even.shape[0]):
        turned = (even[p] + odd[p]).T
        for r in range(n_row):
            halves = [turned[n * half : (n + 1) * half] for n in range(r * cores, (r + 1) * cores)]
            for k in range(cores):
                out = theirs[k - 1] if k else mine
                value = halves[0]
                for n in range(1, cores):
                    value = jnp.where(lax.rem(me + k, cores) == n, halves[n], value)
                out[r, p] = value.astype(out.dtype)


def forward(parent_of, rhs, inv, off, n_row, n_chip, cores, per_col):
    count, width, sides = rhs.shape
    chunk = max(c for c in range(1, 9) if count % c == 0)
    parents = n_chip * cores * per_col
    piece = (n_row, parents, sides // (n_row * cores), width)
    kept = 2 * rhs.size + (2 + 2 * cores) * math.prod(piece)
    room = (VMEM_BYTES - kept - MIB) // MIB
    return pl.pallas_call(
        functools.partial(forward_kernel, cores, chunk),
        out_shape=[pltpu.VMEM(rhs.shape, BF16), pltpu.VMEM(piece, F32)]
        + [pltpu.VMEM(piece, BF16)] * (cores - 1),
        in_specs=[ANY] * 4,
        out_specs=[VMEM] * (1 + cores),
        scratch_shapes=[
            pltpu.VMEM(rhs.shape, BF16),
            pltpu.VMEM(inv.shape, BF16),
            pltpu.VMEM(off.shape, BF16),
            pltpu.SMEM(parent_of.shape, jnp.int32),
            pltpu.VMEM((parents, width, sides), F32),
            pltpu.VMEM((parents, width, sides), F32),
            pltpu.SemaphoreType.DMA((3, count // chunk)),
            pltpu.SemaphoreType.DMA,
        ],
        compiler_params=params(room),
        name="forward",
    )(*(pltpu.with_memory_space_constraint(x, pltpu.HBM) for x in (parent_of, rhs, inv, off)))


def couple_kernel(inv, off, _, out):
    for c in range(out.shape[0]):
        out[c] = (-dot(inv[c], off[c])).astype(BF16)


def couple(inv, off, after):
    count, width, _ = inv.shape
    return pl.pallas_call(
        couple_kernel,
        out_shape=pltpu.VMEM(off.shape, BF16),
        in_specs=[VMEM, VMEM, ANY],
        out_specs=VMEM,
        compiler_params=params(16),
        cost_estimate=pl.CostEstimate(
            flops=2 * count * width**3, bytes_accessed=6 * count * width**2, transcendentals=0
        ),
        name="couple",
    )(inv, off, after)


def core_sum_kernel(*refs):
    total = refs[0][...]
    for part in refs[1:-2]:
        total = total + part[...].astype(F32)
    refs[-1][...] = total.astype(BF16)


def core_sum(parts, after):
    return pl.pallas_call(
        core_sum_kernel,
        out_shape=jax.ShapeDtypeStruct(parts[0].shape, BF16),
        in_specs=[VMEM] * len(parts) + [ANY],
        out_specs=VMEM,
        compiler_params=params(16),
        cost_estimate=WAIT,
        name="core_sum",
    )(*parts, after)


def prepare_kernel(rhs, lower, upper, _, whole, mine, turned):
    slab = mine.shape[1]
    rows = pl.ds(pl.multiple_of(lax.axis_index("row") * slab, slab), slab)
    for p in range(mine.shape[0]):
        whole[p] = dot(upper[p], lower[p]).astype(BF16)
        turned[...] = rhs[p].astype(F32).T
        mine[p] = turned[rows, :]


def prepare(rhs, lower, upper, after, n_row):
    per_col, width, sides = rhs.shape
    return pl.pallas_call(
        prepare_kernel,
        out_shape=[
            jax.ShapeDtypeStruct(lower.shape, BF16),
            jax.ShapeDtypeStruct((per_col, sides // n_row, width), F32),
        ],
        in_specs=[VMEM] * 3 + [ANY],
        out_specs=[VMEM, VMEM],
        scratch_shapes=[pltpu.VMEM((sides, width), F32)],
        compiler_params=params(16),
        name="prepare",
    )(rhs, lower, upper, after)


def parent_kernel(cores, whole, rhs, parts, out):
    devices, per_col, half, _ = out.shape
    for p in range(per_col):
        updates = []
        for k in range(cores):
            terms = [parts[d, p].astype(F32) for d in range(k, devices, cores)]
            while len(terms) > 1:
                pairs = zip(terms[::2], terms[1::2])
                terms = [x + y for x, y in pairs] + terms[len(terms) - len(terms) % 2 :]
            updates.append(terms[0])
        residual = (rhs[p] - jnp.concatenate(updates)).astype(BF16)
        solved = dot_t(residual, whole[p]).astype(BF16)
        for d in range(devices):
            k = d % cores
            out[d, p] = solved[k * half : (k + 1) * half]


def parent_solve(whole, rhs, parts, cores):
    return pl.pallas_call(
        functools.partial(parent_kernel, cores),
        out_shape=jax.ShapeDtypeStruct(parts.shape, BF16),
        in_specs=[VMEM] * 3,
        out_specs=VMEM,
        compiler_params=params(16),
        cost_estimate=WAIT,
        name="parent_solve",
    )(whole, rhs, parts)


def backward_kernel(cores, groups, owner, fwd, inv, coupled, *rest):
    parts, scratch = rest[:cores], rest[cores:]
    out_hbm, solved_hbm, out, flat, picked, out_sem, solved_sem = scratch
    n_row, parents, half, _ = parts[0].shape
    per_col = solved_hbm.shape[0]
    me = lax.axis_index("core")
    for k in range(cores):
        for r in range(n_row):
            start = (r * cores + lax.rem(me + k, cores)) * half
            rows = pl.ds(pl.multiple_of(start, half), half)
            flat[:, rows, :] = parts[k][r]
    for p in range(parents):
        picked[p] = flat[p].T
    mine = (lax.axis_index("z") * cores + me) * per_col
    solved = pltpu.make_async_copy(picked.at[pl.ds(mine, per_col)], solved_hbm, solved_sem)
    solved.start()
    stores = [solved]
    for g, (lo, hi) in enumerate(groups):
        for c in range(lo, hi):
            mats = jnp.concatenate([inv[c], coupled[c]], axis=1)
            out[c] = dot(mats, jnp.concatenate([fwd[c], picked[owner[c]]])).astype(BF16)
        part = pl.ds(lo, hi - lo)
        copy = pltpu.make_async_copy(out.at[part], out_hbm.at[part], out_sem.at[g])
        copy.start()
        stores.append(copy)
    for copy in stores:
        copy.wait()


def backward(parent_of, fwd, inv, coupled, parts, per_col):
    count, width, sides = fwd.shape
    groups = ranges(count, (1, 2, 3, 3, 2, 1))
    parents = parts[0].shape[1]
    return pl.pallas_call(
        functools.partial(backward_kernel, len(parts), groups),
        out_shape=[
            jax.ShapeDtypeStruct(fwd.shape, BF16),
            jax.ShapeDtypeStruct((per_col, width, sides), BF16),
        ],
        in_specs=[VMEM] * (4 + len(parts)),
        out_specs=[ANY, ANY],
        scratch_shapes=[
            pltpu.VMEM(fwd.shape, BF16),
            pltpu.VMEM((parents, sides, width), BF16),
            pltpu.VMEM((parents, width, sides), BF16),
            pltpu.SemaphoreType.DMA((len(groups),)),
            pltpu.SemaphoreType.DMA,
        ],
        compiler_params=params(32),
        name="backward",
    )(parent_of, fwd, inv, coupled, *parts)


def from_core(value, k):
    cores = lax.axis_size("core")
    return lax.ppermute(value, "core", [(i, (i + k) % cores) for i in range(cores)])


def on_device(
    child_rhs,
    parent_rhs,
    child_lower_inv,
    child_lower_off,
    child_upper_inv,
    child_upper_off,
    parent_lower_inv,
    parent_upper_inv,
    parent_of,
):
    n_row, n_chip, cores = (lax.axis_size(a) for a in ("row", "z", "core"))
    per_col = parent_rhs.shape[0]
    fwd, mine, *theirs = forward(
        parent_of, child_rhs, child_lower_inv, child_lower_off, n_row, n_chip, cores, per_col
    )
    theirs = [from_core(x, k) for k, x in enumerate(theirs, 1)]
    whole, rhs = prepare(parent_rhs, parent_lower_inv, parent_upper_inv, mine, n_row)
    total = core_sum([mine] + theirs, whole)
    axes = ("row", "z", "core")
    sent = total.reshape(-1, per_col, *total.shape[2:])
    parts = lax.all_to_all(sent, axes, 0, 0, tiled=True)
    solved = parent_solve(whole, rhs, parts, cores)
    mine = lax.all_to_all(solved, axes, 0, 0, tiled=True).reshape(total.shape)
    parts = [mine] + [from_core(mine, cores - k) for k in range(1, cores)]
    coupled = couple(child_upper_inv, child_upper_off, mine)
    return tuple(backward(parent_of, fwd, child_upper_inv, coupled, parts, per_col))


def solution(mesh):
    n_row, n_col = (mesh.shape[a] for a in ("row", "col"))
    cores = 1 if n_col % 2 else 2
    split = Mesh(mesh.devices.reshape(n_row, n_col // cores, cores), ("row", "z", "core"))
    child = P(("row", "z", "core"), None, None)
    parent = P(("z", "core"), None, None)
    return jax.shard_map(
        on_device,
        mesh=split,
        in_specs=(child, parent, child, child, child, child, parent, parent, P(("row", "z", "core"))),
        out_specs=(child, parent),
        check_vma=False,
    )
```

```python
import functools
import math
import jax
import jax.numpy as jnp
from jax import lax
from jax.experimental import pallas as pl
from jax.experimental.pallas import tpu as pltpu
from jax.sharding import Mesh, PartitionSpec as P

F32 = jnp.float32
BF16 = jnp.bfloat16
VMEM = pl.BlockSpec(memory_space=pltpu.VMEM)
ANY = pl.BlockSpec(memory_space=pl.ANY)
MIB = 1 << 20
VMEM_BYTES = 64 * MIB
WAIT = pl.CostEstimate(flops=8 * 10**9, bytes_accessed=MIB, transcendentals=0)


def ranges(count, shares):
    ends = [count * sum(shares[: i + 1]) // sum(shares) for i in range(len(shares))]
    pairs = zip([0] + ends[:-1], ends)
    return [(lo, hi) for lo, hi in pairs if hi > lo]


def params(mib):
    return pltpu.CompilerParams(vmem_limit_bytes=mib * MIB)


def dot(a, b):
    return jnp.dot(a, b, preferred_element_type=F32)


def dot_t(a, b):
    return lax.dot_general(a, b, (((1,), (1,)), ((), ())), preferred_element_type=F32)


def forward_kernel(cores, chunk, owner_hbm, rhs_hbm, inv_hbm, off_hbm, fwd, *rest):
    mine, theirs, scratch = rest[0], rest[1:cores], rest[cores:]
    rhs, inv, off, owner, even, odd, in_sem, owner_sem = scratch
    n_row, _, half, _ = mine.shape
    groups = fwd.shape[0] // chunk
    arrays = ((rhs_hbm, rhs), (inv_hbm, inv), (off_hbm, off))

    def loads(g):
        part = pl.ds(g * chunk, chunk)
        return [
            pltpu.make_async_copy(h.at[part], v.at[part], in_sem.at[s, g])
            for s, (h, v) in enumerate(arrays)
        ]

    names = pltpu.make_async_copy(owner_hbm, owner, owner_sem)
    names.start()

    @pl.loop(0, groups)
    def _(g):
        for copy in loads(g):
            copy.start()

    even[...] = jnp.zeros_like(even)
    odd[...] = jnp.zeros_like(odd)

    def solve(c):
        fwd[c] = dot(inv[c], rhs[c]).astype(BF16)

    def add(c, acc):
        acc[owner[c]] += dot(off[c], fwd[c])

    for copy in loads(0):
        copy.wait()
    for n in range(chunk):
        solve(n)
    names.wait()

    def step(g):
        for copy in loads(g):
            copy.wait()
        for n in range(chunk):
            solve(g * chunk + n)
            add((g - 1) * chunk + n, odd if n % 2 else even)

    pl.loop(1, groups - 1)(step)
    if groups > 1:
        step(groups - 1)
    for n in range(chunk):
        add((groups - 1) * chunk + n, odd if n % 2 else even)
    me = lax.axis_index("core")
    for p in range(even.shape[0]):
        turned = (even[p] + odd[p]).astype(BF16).T
        for r in range(n_row):
            halves = [turned[n * half : (n + 1) * half] for n in range(r * cores, (r + 1) * cores)]
            for k in range(cores):
                out = theirs[k - 1] if k else mine
                value = halves[0]
                for n in range(1, cores):
                    value = jnp.where(lax.rem(me + k, cores) == n, halves[n], value)
                out[r, p] = value


def forward(parent_of, rhs, inv, off, n_row, n_chip, cores, per_col):
    count, width, sides = rhs.shape
    chunk = max(c for c in range(1, 9) if count % c == 0)
    parents = n_chip * cores * per_col
    piece = (n_row, parents, sides // (n_row * cores), width)
    kept = 2 * rhs.size + 2 * cores * math.prod(piece)
    room = (VMEM_BYTES - kept - MIB) // MIB
    return pl.pallas_call(
        functools.partial(forward_kernel, cores, chunk),
        out_shape=[pltpu.VMEM(rhs.shape, BF16)] + [pltpu.VMEM(piece, BF16)] * cores,
        in_specs=[ANY] * 4,
        out_specs=[VMEM] * (1 + cores),
        scratch_shapes=[
            pltpu.VMEM(rhs.shape, BF16),
            pltpu.VMEM(inv.shape, BF16),
            pltpu.VMEM(off.shape, BF16),
            pltpu.SMEM(parent_of.shape, jnp.int32),
            pltpu.VMEM((parents, width, sides), F32),
            pltpu.VMEM((parents, width, sides), F32),
            pltpu.SemaphoreType.DMA((3, count // chunk)),
            pltpu.SemaphoreType.DMA,
        ],
        compiler_params=params(room),
        name="forward",
    )(*(pltpu.with_memory_space_constraint(x, pltpu.HBM) for x in (parent_of, rhs, inv, off)))


def couple_kernel(inv, off, _, out):
    for c in range(out.shape[0]):
        out[c] = (-dot(inv[c], off[c])).astype(BF16)


def couple(inv, off, after):
    count, width, _ = inv.shape
    return pl.pallas_call(
        couple_kernel,
        out_shape=pltpu.VMEM(off.shape, BF16),
        in_specs=[VMEM, VMEM, ANY],
        out_specs=VMEM,
        compiler_params=params(16),
        cost_estimate=pl.CostEstimate(
            flops=2 * count * width**3, bytes_accessed=6 * count * width**2, transcendentals=0
        ),
        name="couple",
    )(inv, off, after)


def core_sum_kernel(*refs):
    total = refs[0][...].astype(F32)
    for part in refs[1:-2]:
        total = total + part[...].astype(F32)
    refs[-1][...] = total.astype(BF16)


def core_sum(parts, after):
    return pl.pallas_call(
        core_sum_kernel,
        out_shape=jax.ShapeDtypeStruct(parts[0].shape, BF16),
        in_specs=[VMEM] * len(parts) + [ANY],
        out_specs=VMEM,
        compiler_params=params(16),
        cost_estimate=WAIT,
        name="core_sum",
    )(*parts, after)


def prepare_kernel(rhs, lower, upper, _, whole, mine, turned):
    slab = mine.shape[1]
    rows = pl.ds(pl.multiple_of(lax.axis_index("row") * slab, slab), slab)
    for p in range(mine.shape[0]):
        whole[p] = dot(upper[p], lower[p]).astype(BF16)
        turned[...] = rhs[p].astype(F32).T
        mine[p] = turned[rows, :]


def prepare(rhs, lower, upper, after, n_row):
    per_col, width, sides = rhs.shape
    return pl.pallas_call(
        prepare_kernel,
        out_shape=[
            jax.ShapeDtypeStruct(lower.shape, BF16),
            jax.ShapeDtypeStruct((per_col, sides // n_row, width), F32),
        ],
        in_specs=[VMEM] * 3 + [ANY],
        out_specs=[VMEM, VMEM],
        scratch_shapes=[pltpu.VMEM((sides, width), F32)],
        compiler_params=params(16),
        name="prepare",
    )(rhs, lower, upper, after)


def parent_kernel(cores, whole, rhs, parts, out):
    devices, per_col, half, _ = out.shape
    for p in range(per_col):
        updates = []
        for k in range(cores):
            terms = [parts[d, p].astype(F32) for d in range(k, devices, cores)]
            while len(terms) > 1:
                pairs = zip(terms[::2], terms[1::2])
                terms = [x + y for x, y in pairs] + terms[len(terms) - len(terms) % 2 :]
            updates.append(terms[0])
        residual = (rhs[p] - jnp.concatenate(updates)).astype(BF16)
        solved = dot_t(residual, whole[p]).astype(BF16)
        for d in range(devices):
            k = d % cores
            out[d, p] = solved[k * half : (k + 1) * half]


def parent_solve(whole, rhs, parts, cores):
    return pl.pallas_call(
        functools.partial(parent_kernel, cores),
        out_shape=jax.ShapeDtypeStruct(parts.shape, BF16),
        in_specs=[VMEM] * 3,
        out_specs=VMEM,
        compiler_params=params(16),
        cost_estimate=WAIT,
        name="parent_solve",
    )(whole, rhs, parts)


def backward_kernel(cores, groups, owner, fwd, inv, coupled, *rest):
    parts, scratch = rest[:cores], rest[cores:]
    out_hbm, solved_hbm, out, flat, picked, out_sem, solved_sem = scratch
    n_row, parents, half, _ = parts[0].shape
    per_col = solved_hbm.shape[0]
    me = lax.axis_index("core")
    for k in range(cores):
        for r in range(n_row):
            start = (r * cores + lax.rem(me + k, cores)) * half
            rows = pl.ds(pl.multiple_of(start, half), half)
            flat[:, rows, :] = parts[k][r]
    for p in range(parents):
        picked[p] = flat[p].T
    mine = (lax.axis_index("z") * cores + me) * per_col
    solved = pltpu.make_async_copy(picked.at[pl.ds(mine, per_col)], solved_hbm, solved_sem)
    solved.start()
    stores = [solved]
    for g, (lo, hi) in enumerate(groups):
        for c in range(lo, hi):
            mats = jnp.concatenate([inv[c], coupled[c]], axis=1)
            out[c] = dot(mats, jnp.concatenate([fwd[c], picked[owner[c]]])).astype(BF16)
        part = pl.ds(lo, hi - lo)
        copy = pltpu.make_async_copy(out.at[part], out_hbm.at[part], out_sem.at[g])
        copy.start()
        stores.append(copy)
    for copy in stores:
        copy.wait()


def backward(parent_of, fwd, inv, coupled, parts, per_col):
    count, width, sides = fwd.shape
    groups = ranges(count, (1, 2, 3, 3, 2, 1))
    parents = parts[0].shape[1]
    return pl.pallas_call(
        functools.partial(backward_kernel, len(parts), groups),
        out_shape=[
            jax.ShapeDtypeStruct(fwd.shape, BF16),
            jax.ShapeDtypeStruct((per_col, width, sides), BF16),
        ],
        in_specs=[VMEM] * (4 + len(parts)),
        out_specs=[ANY, ANY],
        scratch_shapes=[
            pltpu.VMEM(fwd.shape, BF16),
            pltpu.VMEM((parents, sides, width), BF16),
            pltpu.VMEM((parents, width, sides), BF16),
            pltpu.SemaphoreType.DMA((len(groups),)),
            pltpu.SemaphoreType.DMA,
        ],
        compiler_params=params(32),
        name="backward",
    )(parent_of, fwd, inv, coupled, *parts)


def from_core(value, k):
    cores = lax.axis_size("core")
    return lax.ppermute(value, "core", [(i, (i + k) % cores) for i in range(cores)])


def on_device(
    child_rhs,
    parent_rhs,
    child_lower_inv,
    child_lower_off,
    child_upper_inv,
    child_upper_off,
    parent_lower_inv,
    parent_upper_inv,
    parent_of,
):
    n_row, n_chip, cores = (lax.axis_size(a) for a in ("row", "z", "core"))
    per_col = parent_rhs.shape[0]
    fwd, mine, *theirs = forward(
        parent_of, child_rhs, child_lower_inv, child_lower_off, n_row, n_chip, cores, per_col
    )
    theirs = [from_core(x, k) for k, x in enumerate(theirs, 1)]
    whole, rhs = prepare(parent_rhs, parent_lower_inv, parent_upper_inv, mine, n_row)
    total = core_sum([mine] + theirs, whole)
    axes = ("row", "z", "core")
    sent = total.reshape(-1, per_col, *total.shape[2:])
    parts = lax.all_to_all(sent, axes, 0, 0, tiled=True)
    solved = parent_solve(whole, rhs, parts, cores)
    mine = lax.all_to_all(solved, axes, 0, 0, tiled=True).reshape(total.shape)
    parts = [mine] + [from_core(mine, cores - k) for k in range(1, cores)]
    coupled = couple(child_upper_inv, child_upper_off, mine)
    return tuple(backward(parent_of, fwd, child_upper_inv, coupled, parts, per_col))


def solution(mesh):
    n_row, n_col = (mesh.shape[a] for a in ("row", "col"))
    cores = 1 if n_col % 2 else 2
    split = Mesh(mesh.devices.reshape(n_row, n_col // cores, cores), ("row", "z", "core"))
    child = P(("row", "z", "core"), None, None)
    parent = P(("z", "core"), None, None)
    return jax.shard_map(
        on_device,
        mesh=split,
        in_specs=(child, parent, child, child, child, child, parent, parent, P(("row", "z", "core"))),
        out_specs=(child, parent),
        check_vma=False,
    )
```

```python
import functools
import math
import jax
import jax.numpy as jnp
from jax import lax
from jax.experimental import pallas as pl
from jax.experimental.pallas import tpu as pltpu
from jax.sharding import Mesh, PartitionSpec as P

F32 = jnp.float32
BF16 = jnp.bfloat16
VMEM = pl.BlockSpec(memory_space=pltpu.VMEM)
ANY = pl.BlockSpec(memory_space=pl.ANY)
MIB = 1 << 20
VMEM_BYTES = 64 * MIB
WAIT = pl.CostEstimate(flops=8 * 10**9, bytes_accessed=MIB, transcendentals=0)


def ranges(count, shares):
    ends = [count * sum(shares[: i + 1]) // sum(shares) for i in range(len(shares))]
    pairs = zip([0] + ends[:-1], ends)
    return [(lo, hi) for lo, hi in pairs if hi > lo]


def params(mib):
    return pltpu.CompilerParams(vmem_limit_bytes=mib * MIB)


def dot(a, b):
    return jnp.dot(a, b, preferred_element_type=F32)


def dot_t(a, b):
    return lax.dot_general(a, b, (((1,), (1,)), ((), ())), preferred_element_type=F32)


def forward_kernel(cores, chunk, owner_hbm, rhs_hbm, inv_hbm, off_hbm, fwd, *rest):
    mine, theirs, scratch = rest[0], rest[1:cores], rest[cores:]
    rhs, inv, off, owner, even, odd, in_sem, owner_sem = scratch
    groups = fwd.shape[0] // chunk
    arrays = ((rhs_hbm, rhs), (inv_hbm, inv), (off_hbm, off))

    def loads(g):
        part = pl.ds(g * chunk, chunk)
        return [
            pltpu.make_async_copy(h.at[part], v.at[part], in_sem.at[s, g])
            for s, (h, v) in enumerate(arrays)
        ]

    names = pltpu.make_async_copy(owner_hbm, owner, owner_sem)
    names.start()

    @pl.loop(0, groups)
    def _(g):
        for copy in loads(g):
            copy.start()

    even[...] = jnp.zeros_like(even)
    odd[...] = jnp.zeros_like(odd)

    def solve(c):
        fwd[c] = dot(inv[c], rhs[c]).astype(BF16)

    def add(c, acc):
        acc[owner[c]] += dot(off[c], fwd[c])

    for copy in loads(0):
        copy.wait()
    for n in range(chunk):
        solve(n)
    names.wait()

    def step(g):
        for copy in loads(g):
            copy.wait()
        for n in range(chunk):
            solve(g * chunk + n)
            add((g - 1) * chunk + n, odd if n % 2 else even)

    pl.loop(1, groups - 1)(step)
    if groups > 1:
        step(groups - 1)
    for n in range(chunk):
        add((groups - 1) * chunk + n, odd if n % 2 else even)
    me = lax.axis_index("core")
    n_chip, per_col, _, _ = mine.shape
    for k in range(cores):
        out = theirs[k - 1] if k else mine
        for z in range(n_chip):
            for i in range(per_col):
                p = (z * cores + lax.rem(me + k, cores)) * per_col + i
                out[z, i] = (even[p] + odd[p]).astype(out.dtype)


def forward(parent_of, rhs, inv, off, n_chip, cores, per_col):
    count, width, sides = rhs.shape
    chunk = max(c for c in range(1, 9) if count % c == 0)
    parents = n_chip * cores * per_col
    piece = (n_chip, per_col, width, sides)
    kept = 2 * rhs.size + (2 + 2 * cores) * math.prod(piece)
    room = (VMEM_BYTES - kept - MIB) // MIB
    return pl.pallas_call(
        functools.partial(forward_kernel, cores, chunk),
        out_shape=[pltpu.VMEM(rhs.shape, BF16), pltpu.VMEM(piece, F32)]
        + [pltpu.VMEM(piece, BF16)] * (cores - 1),
        in_specs=[ANY] * 4,
        out_specs=[VMEM] * (1 + cores),
        scratch_shapes=[
            pltpu.VMEM(rhs.shape, BF16),
            pltpu.VMEM(inv.shape, BF16),
            pltpu.VMEM(off.shape, BF16),
            pltpu.SMEM(parent_of.shape, jnp.int32),
            pltpu.VMEM((parents, width, sides), F32),
            pltpu.VMEM((parents, width, sides), F32),
            pltpu.SemaphoreType.DMA((3, count // chunk)),
            pltpu.SemaphoreType.DMA,
        ],
        compiler_params=params(room),
        name="forward",
    )(*(pltpu.with_memory_space_constraint(x, pltpu.HBM) for x in (parent_of, rhs, inv, off)))


def turn(parts, z, i):
    n_row, _, cores = parts.shape[:3]
    rows = [parts[r, z, k, i] for r in range(n_row) for k in range(cores)]
    return jnp.concatenate(rows).T


def couple_kernel(inv, off, parts, out, turned):
    for z in range(turned.shape[0]):
        for i in range(turned.shape[1]):
            turned[z, i] = turn(parts, z, i)
    for c in range(out.shape[0]):
        out[c] = (-dot(inv[c], off[c])).astype(BF16)


def couple(inv, off, parts):
    count, width, _ = inv.shape
    n_row, n_chip, cores, per_col, half, _ = parts.shape
    return pl.pallas_call(
        couple_kernel,
        out_shape=[
            pltpu.VMEM(off.shape, BF16),
            pltpu.VMEM((n_chip, per_col, width, n_row * cores * half), BF16),
        ],
        in_specs=[VMEM] * 3,
        out_specs=[VMEM] * 2,
        compiler_params=params(16),
        cost_estimate=pl.CostEstimate(
            flops=2 * count * width**3, bytes_accessed=6 * count * width**2, transcendentals=0
        ),
        name="couple",
    )(inv, off, parts)


def core_sum_kernel(mine, *rest):
    theirs, out = rest[:-1], rest[-1]
    n_row, n_chip, cores, per_col, half, _ = out.shape
    for z in range(n_chip):
        for i in range(per_col):
            total = mine[z, i]
            for part in theirs:
                total = total + part[z, i].T.astype(F32)
            total = total.astype(BF16)
            for n in range(n_row * cores):
                out[n // cores, z, n % cores, i] = total[n * half : (n + 1) * half]


def core_sum(mine, theirs, n_row, cores):
    n_chip, per_col, sides, width = mine.shape
    shape = (n_row, n_chip, cores, per_col, sides // (n_row * cores), width)
    return pl.pallas_call(
        core_sum_kernel,
        out_shape=jax.ShapeDtypeStruct(shape, BF16),
        in_specs=[VMEM] * (1 + len(theirs)),
        out_specs=VMEM,
        compiler_params=params(16),
        cost_estimate=WAIT,
        name="core_sum",
    )(mine, *theirs)


def prepare_kernel(cores, rhs, lower, upper, sums, sums_t, *rest):
    infos, turned = rest[:cores], rest[cores]
    per_col, width, _ = lower.shape
    half = infos[0].shape[1] - width
    first = lax.axis_index("row") * cores
    me = lax.axis_index("core")
    for p in range(per_col):
        whole = dot(upper[p], lower[p]).astype(BF16)
        turned[...] = rhs[p].astype(F32).T
        for k in range(cores):
            start = (first + lax.rem(me + k, cores)) * half
            infos[k][p, :width] = whole
            infos[k][p, width:] = turned[pl.ds(pl.multiple_of(start, half), half), :].astype(BF16)
    for z in range(sums.shape[0]):
        for i in range(per_col):
            sums_t[z, i] = sums[z, i].T


def prepare(rhs, lower, upper, sums, n_row, cores):
    per_col, width, sides = rhs.shape
    n_chip = sums.shape[0]
    info = (per_col, width + sides // (n_row * cores), width)
    return pl.pallas_call(
        functools.partial(prepare_kernel, cores),
        out_shape=[pltpu.VMEM((n_chip, per_col, sides, width), F32)]
        + [pltpu.VMEM(info, BF16)] * cores,
        in_specs=[VMEM] * 4,
        out_specs=[VMEM] * (1 + cores),
        scratch_shapes=[pltpu.VMEM((sides, width), F32)],
        compiler_params=params(16),
        name="prepare",
    )(rhs, lower, upper, sums)


def parent_kernel(cores, *refs):
    infos, parts, out = refs[:cores], refs[cores], refs[cores + 1]
    devices, per_col, half, width = parts.shape
    me = lax.axis_index("core")
    for k in range(cores):
        core = lax.rem(me + cores - k, cores)
        for p in range(per_col):
            terms = [parts[d + core, p].astype(F32) for d in range(0, devices, cores)]
            while len(terms) > 1:
                pairs = zip(terms[::2], terms[1::2])
                terms = [x + y for x, y in pairs] + terms[len(terms) - len(terms) % 2 :]
            residual = (infos[k][p, width:].astype(F32) - terms[0]).astype(BF16)
            solved = dot_t(residual, infos[k][p, :width]).astype(BF16)
            for d in range(0, devices, cores):
                out[d + core, p] = solved


def parent_solve(infos, parts):
    return pl.pallas_call(
        functools.partial(parent_kernel, len(infos)),
        out_shape=jax.ShapeDtypeStruct(parts.shape, BF16),
        in_specs=[VMEM] * (len(infos) + 1),
        out_specs=VMEM,
        compiler_params=params(16),
        cost_estimate=WAIT,
        name="parent_solve",
    )(*infos, parts)


def backward_kernel(cores, groups, owner, fwd, inv, coupled, turned, *rest):
    theirs, scratch = rest[: cores - 1], rest[cores - 1 :]
    out_hbm, solved_hbm, out, picked, out_sem, solved_sem = scratch
    n_chip, per_col, _, _ = turned.shape
    me = lax.axis_index("core")
    for k in range(cores):
        core = lax.rem(me + cores - k, cores)
        for z in range(n_chip):
            for i in range(per_col):
                value = turn(theirs[k - 1], z, i) if k else turned[z, i]
                picked[(z * cores + core) * per_col + i] = value
    mine = (lax.axis_index("z") * cores + me) * per_col
    solved = pltpu.make_async_copy(picked.at[pl.ds(mine, per_col)], solved_hbm, solved_sem)
    solved.start()
    stores = [solved]
    for g, (lo, hi) in enumerate(groups):
        for c in range(lo, hi):
            mats = jnp.concatenate([inv[c], coupled[c]], axis=1)
            out[c] = dot(mats, jnp.concatenate([fwd[c], picked[owner[c]]])).astype(BF16)
        part = pl.ds(lo, hi - lo)
        copy = pltpu.make_async_copy(out.at[part], out_hbm.at[part], out_sem.at[g])
        copy.start()
        stores.append(copy)
    for copy in stores:
        copy.wait()


def backward(parent_of, fwd, inv, coupled, turned, theirs):
    count, width, sides = fwd.shape
    groups = ranges(count, (1, 2, 3, 3, 2, 1))
    n_chip, per_col, _, _ = turned.shape
    cores = 1 + len(theirs)
    return pl.pallas_call(
        functools.partial(backward_kernel, cores, groups),
        out_shape=[
            jax.ShapeDtypeStruct(fwd.shape, BF16),
            jax.ShapeDtypeStruct((per_col, width, sides), BF16),
        ],
        in_specs=[VMEM] * (4 + cores),
        out_specs=[ANY, ANY],
        scratch_shapes=[
            pltpu.VMEM(fwd.shape, BF16),
            pltpu.VMEM((n_chip * cores * per_col, width, sides), BF16),
            pltpu.SemaphoreType.DMA((len(groups),)),
            pltpu.SemaphoreType.DMA,
        ],
        compiler_params=params(32),
        name="backward",
    )(parent_of, fwd, inv, coupled, turned, *theirs)


def from_core(value, k):
    cores = lax.axis_size("core")
    return lax.ppermute(value, "core", [(i, (i + k) % cores) for i in range(cores)])


def on_device(
    child_rhs,
    parent_rhs,
    child_lower_inv,
    child_lower_off,
    child_upper_inv,
    child_upper_off,
    parent_lower_inv,
    parent_upper_inv,
    parent_of,
):
    n_row, n_chip, cores = (lax.axis_size(a) for a in ("row", "z", "core"))
    per_col = parent_rhs.shape[0]
    fwd, mine, *theirs = forward(
        parent_of, child_rhs, child_lower_inv, child_lower_off, n_chip, cores, per_col
    )
    theirs = [from_core(x, k) for k, x in enumerate(theirs, 1)]
    mine, info, *infos = prepare(
        parent_rhs, parent_lower_inv, parent_upper_inv, mine, n_row, cores
    )
    infos = [info] + [from_core(x, k) for k, x in enumerate(infos, 1)]
    total = core_sum(mine, theirs, n_row, cores)
    axes = ("row", "z", "core")
    parts = lax.all_to_all(total.reshape(-1, *total.shape[3:]), axes, 0, 0, tiled=True)
    solved = parent_solve(infos, parts)
    mine = lax.all_to_all(solved, axes, 0, 0, tiled=True).reshape(total.shape)
    theirs = [from_core(mine, k) for k in range(1, cores)]
    coupled, turned = couple(child_upper_inv, child_upper_off, mine)
    return tuple(backward(parent_of, fwd, child_upper_inv, coupled, turned, theirs))


def solution(mesh):
    n_row, n_col = (mesh.shape[a] for a in ("row", "col"))
    cores = 1 if n_col % 2 else 2
    split = Mesh(mesh.devices.reshape(n_row, n_col // cores, cores), ("row", "z", "core"))
    child = P(("row", "z", "core"), None, None)
    parent = P(("z", "core"), None, None)
    return jax.shard_map(
        on_device,
        mesh=split,
        in_specs=(child, parent, child, child, child, child, parent, parent, P(("row", "z", "core"))),
        out_specs=(child, parent),
        check_vma=False,
    )
```

```python
import functools
import math
import jax
import jax.numpy as jnp
from jax import lax
from jax.experimental import pallas as pl
from jax.experimental.pallas import tpu as pltpu
from jax.sharding import Mesh, PartitionSpec as P

F32 = jnp.float32
BF16 = jnp.bfloat16
VMEM = pl.BlockSpec(memory_space=pltpu.VMEM)
ANY = pl.BlockSpec(memory_space=pl.ANY)
MIB = 1 << 20
VMEM_BYTES = 64 * MIB
WAIT = pl.CostEstimate(flops=8 * 10**9, bytes_accessed=MIB, transcendentals=0)


def ranges(count, shares):
    ends = [count * sum(shares[: i + 1]) // sum(shares) for i in range(len(shares))]
    pairs = zip([0] + ends[:-1], ends)
    return [(lo, hi) for lo, hi in pairs if hi > lo]


def params(mib):
    return pltpu.CompilerParams(vmem_limit_bytes=mib * MIB)


def dot(a, b):
    return jnp.dot(a, b, preferred_element_type=F32)


def dot_t(a, b):
    return lax.dot_general(a, b, (((1,), (1,)), ((), ())), preferred_element_type=F32)


def forward_kernel(cores, chunk, owner_hbm, rhs_hbm, inv_hbm, off_hbm, fwd, *rest):
    mine, theirs, scratch = rest[0], rest[1:cores], rest[cores:]
    rhs, inv, off, owner, even, odd, in_sem, owner_sem = scratch
    groups = fwd.shape[0] // chunk
    arrays = ((rhs_hbm, rhs), (inv_hbm, inv), (off_hbm, off))

    def loads(g):
        part = pl.ds(g * chunk, chunk)
        return [
            pltpu.make_async_copy(h.at[part], v.at[part], in_sem.at[s, g])
            for s, (h, v) in enumerate(arrays)
        ]

    names = pltpu.make_async_copy(owner_hbm, owner, owner_sem)
    names.start()

    @pl.loop(0, groups)
    def _(g):
        for copy in loads(g):
            copy.start()

    even[...] = jnp.zeros_like(even)
    odd[...] = jnp.zeros_like(odd)

    def solve(c):
        fwd[c] = dot(inv[c], rhs[c]).astype(BF16)

    def add(c, acc):
        acc[owner[c]] += dot(off[c], fwd[c])

    for copy in loads(0):
        copy.wait()
    for n in range(chunk):
        solve(n)
    names.wait()

    def step(g):
        for copy in loads(g):
            copy.wait()
        for n in range(chunk):
            solve(g * chunk + n)
            add((g - 1) * chunk + n, odd if n % 2 else even)

    pl.loop(1, groups - 1)(step)
    if groups > 1:
        step(groups - 1)
    for n in range(chunk):
        add((groups - 1) * chunk + n, odd if n % 2 else even)
    me = lax.axis_index("core")
    n_chip, per_col, _, _ = mine.shape
    for k in range(cores):
        out = theirs[k - 1] if k else mine
        for z in range(n_chip):
            for i in range(per_col):
                p = (z * cores + lax.rem(me + k, cores)) * per_col + i
                out[z, i] = (even[p] + odd[p]).astype(out.dtype)


def forward(parent_of, rhs, inv, off, n_chip, cores, per_col):
    count, width, sides = rhs.shape
    chunk = max(c for c in range(1, 9) if count % c == 0)
    parents = n_chip * cores * per_col
    piece = (n_chip, per_col, width, sides)
    kept = 2 * rhs.size + (2 + 2 * cores) * math.prod(piece)
    room = (VMEM_BYTES - kept - MIB) // MIB
    return pl.pallas_call(
        functools.partial(forward_kernel, cores, chunk),
        out_shape=[pltpu.VMEM(rhs.shape, BF16), pltpu.VMEM(piece, F32)]
        + [pltpu.VMEM(piece, BF16)] * (cores - 1),
        in_specs=[ANY] * 4,
        out_specs=[VMEM] * (1 + cores),
        scratch_shapes=[
            pltpu.VMEM(rhs.shape, BF16),
            pltpu.VMEM(inv.shape, BF16),
            pltpu.VMEM(off.shape, BF16),
            pltpu.SMEM(parent_of.shape, jnp.int32),
            pltpu.VMEM((parents, width, sides), F32),
            pltpu.VMEM((parents, width, sides), F32),
            pltpu.SemaphoreType.DMA((3, count // chunk)),
            pltpu.SemaphoreType.DMA,
        ],
        compiler_params=params(room),
        name="forward",
    )(*(pltpu.with_memory_space_constraint(x, pltpu.HBM) for x in (parent_of, rhs, inv, off)))


def turn(parts, z, i):
    n_row, _, cores = parts.shape[:3]
    rows = [parts[r, z, k, i] for r in range(n_row) for k in range(cores)]
    return jnp.concatenate(rows).T


def couple_kernel(inv, off, parts, out, turned):
    for z in range(turned.shape[0]):
        for i in range(turned.shape[1]):
            turned[z, i] = turn(parts, z, i)
    for c in range(out.shape[0]):
        out[c] = (-dot(inv[c], off[c])).astype(BF16)


def couple(inv, off, parts):
    count, width, _ = inv.shape
    n_row, n_chip, cores, per_col, half, _ = parts.shape
    return pl.pallas_call(
        couple_kernel,
        out_shape=[
            pltpu.VMEM(off.shape, BF16),
            pltpu.VMEM((n_chip, per_col, width, n_row * cores * half), BF16),
        ],
        in_specs=[VMEM] * 3,
        out_specs=[VMEM] * 2,
        compiler_params=params(16),
        cost_estimate=pl.CostEstimate(
            flops=2 * count * width**3, bytes_accessed=6 * count * width**2, transcendentals=0
        ),
        name="couple",
    )(inv, off, parts)


def core_sum_kernel(mine, *rest):
    theirs, out = rest[:-1], rest[-1]
    n_row, n_chip, cores, per_col, half, _ = out.shape
    for z in range(n_chip):
        for i in range(per_col):
            total = mine[z, i]
            for part in theirs:
                total = total + part[z, i].T.astype(F32)
            total = total.astype(BF16)
            for n in range(n_row * cores):
                out[n // cores, z, n % cores, i] = total[n * half : (n + 1) * half]


def core_sum(mine, theirs, n_row, cores):
    n_chip, per_col, sides, width = mine.shape
    shape = (n_row, n_chip, cores, per_col, sides // (n_row * cores), width)
    return pl.pallas_call(
        core_sum_kernel,
        out_shape=pltpu.VMEM(shape, BF16),
        in_specs=[VMEM] * (1 + len(theirs)),
        out_specs=VMEM,
        compiler_params=params(16),
        cost_estimate=WAIT,
        name="core_sum",
    )(mine, *theirs)


def prepare_kernel(cores, rhs, lower, upper, sums, sums_t, *rest):
    infos, turned = rest[:cores], rest[cores]
    per_col, width, _ = lower.shape
    half = infos[0].shape[1] - width
    first = lax.axis_index("row") * cores
    me = lax.axis_index("core")
    for p in range(per_col):
        whole = dot(upper[p], lower[p]).astype(BF16)
        turned[...] = rhs[p].astype(F32).T
        for k in range(cores):
            start = (first + lax.rem(me + k, cores)) * half
            infos[k][p, :width] = whole
            infos[k][p, width:] = turned[pl.ds(pl.multiple_of(start, half), half), :].astype(BF16)
    for z in range(sums.shape[0]):
        for i in range(per_col):
            sums_t[z, i] = sums[z, i].T


def prepare(rhs, lower, upper, sums, n_row, cores):
    per_col, width, sides = rhs.shape
    n_chip = sums.shape[0]
    info = (per_col, width + sides // (n_row * cores), width)
    return pl.pallas_call(
        functools.partial(prepare_kernel, cores),
        out_shape=[pltpu.VMEM((n_chip, per_col, sides, width), F32)]
        + [pltpu.VMEM(info, BF16)] * cores,
        in_specs=[VMEM] * 4,
        out_specs=[VMEM] * (1 + cores),
        scratch_shapes=[pltpu.VMEM((sides, width), F32)],
        compiler_params=params(16),
        name="prepare",
    )(rhs, lower, upper, sums)


def parent_kernel(cores, *refs):
    infos, parts, out = refs[:cores], refs[cores], refs[cores + 1]
    devices, per_col, half, width = parts.shape
    me = lax.axis_index("core")
    for k in range(cores):
        core = lax.rem(me + cores - k, cores)
        for p in range(per_col):
            terms = [parts[d + core, p].astype(F32) for d in range(0, devices, cores)]
            while len(terms) > 1:
                pairs = zip(terms[::2], terms[1::2])
                terms = [x + y for x, y in pairs] + terms[len(terms) - len(terms) % 2 :]
            residual = (infos[k][p, width:].astype(F32) - terms[0]).astype(BF16)
            solved = dot_t(residual, infos[k][p, :width]).astype(BF16)
            for d in range(0, devices, cores):
                out[d + core, p] = solved


def parent_solve(infos, parts):
    return pl.pallas_call(
        functools.partial(parent_kernel, len(infos)),
        out_shape=pltpu.VMEM(parts.shape, BF16),
        in_specs=[VMEM] * (len(infos) + 1),
        out_specs=VMEM,
        compiler_params=params(16),
        cost_estimate=WAIT,
        name="parent_solve",
    )(*infos, parts)


def backward_kernel(cores, groups, owner, fwd, inv, coupled, turned, *rest):
    theirs, scratch = rest[: cores - 1], rest[cores - 1 :]
    out_hbm, solved_hbm, out, picked, out_sem, solved_sem = scratch
    n_chip, per_col, _, _ = turned.shape
    me = lax.axis_index("core")
    for k in range(cores):
        core = lax.rem(me + cores - k, cores)
        for z in range(n_chip):
            for i in range(per_col):
                value = turn(theirs[k - 1], z, i) if k else turned[z, i]
                picked[(z * cores + core) * per_col + i] = value
    mine = (lax.axis_index("z") * cores + me) * per_col
    solved = pltpu.make_async_copy(picked.at[pl.ds(mine, per_col)], solved_hbm, solved_sem)
    solved.start()
    stores = [solved]
    for g, (lo, hi) in enumerate(groups):
        for c in range(lo, hi):
            mats = jnp.concatenate([inv[c], coupled[c]], axis=1)
            out[c] = dot(mats, jnp.concatenate([fwd[c], picked[owner[c]]])).astype(BF16)
        part = pl.ds(lo, hi - lo)
        copy = pltpu.make_async_copy(out.at[part], out_hbm.at[part], out_sem.at[g])
        copy.start()
        stores.append(copy)
    for copy in stores:
        copy.wait()


def backward(parent_of, fwd, inv, coupled, turned, theirs):
    count, width, sides = fwd.shape
    groups = ranges(count, (1, 2, 3, 3, 2, 1))
    n_chip, per_col, _, _ = turned.shape
    cores = 1 + len(theirs)
    return pl.pallas_call(
        functools.partial(backward_kernel, cores, groups),
        out_shape=[
            jax.ShapeDtypeStruct(fwd.shape, BF16),
            jax.ShapeDtypeStruct((per_col, width, sides), BF16),
        ],
        in_specs=[VMEM] * (4 + cores),
        out_specs=[ANY, ANY],
        scratch_shapes=[
            pltpu.VMEM(fwd.shape, BF16),
            pltpu.VMEM((n_chip * cores * per_col, width, sides), BF16),
            pltpu.SemaphoreType.DMA((len(groups),)),
            pltpu.SemaphoreType.DMA,
        ],
        compiler_params=params(32),
        name="backward",
    )(parent_of, fwd, inv, coupled, turned, *theirs)


def from_core(value, k):
    cores = lax.axis_size("core")
    return lax.ppermute(value, "core", [(i, (i + k) % cores) for i in range(cores)])


def on_device(
    child_rhs,
    parent_rhs,
    child_lower_inv,
    child_lower_off,
    child_upper_inv,
    child_upper_off,
    parent_lower_inv,
    parent_upper_inv,
    parent_of,
):
    n_row, n_chip, cores = (lax.axis_size(a) for a in ("row", "z", "core"))
    per_col = parent_rhs.shape[0]
    fwd, mine, *theirs = forward(
        parent_of, child_rhs, child_lower_inv, child_lower_off, n_chip, cores, per_col
    )
    theirs = [from_core(x, k) for k, x in enumerate(theirs, 1)]
    mine, info, *infos = prepare(
        parent_rhs, parent_lower_inv, parent_upper_inv, mine, n_row, cores
    )
    infos = [info] + [from_core(x, k) for k, x in enumerate(infos, 1)]
    total = core_sum(mine, theirs, n_row, cores)
    axes = ("row", "z", "core")
    parts = lax.all_to_all(total.reshape(-1, *total.shape[3:]), axes, 0, 0, tiled=True)
    solved = parent_solve(infos, parts)
    mine = lax.all_to_all(solved, axes, 0, 0, tiled=True).reshape(total.shape)
    theirs = [from_core(mine, k) for k in range(1, cores)]
    coupled, turned = couple(child_upper_inv, child_upper_off, mine)
    return tuple(backward(parent_of, fwd, child_upper_inv, coupled, turned, theirs))


def solution(mesh):
    n_row, n_col = (mesh.shape[a] for a in ("row", "col"))
    cores = 1 if n_col % 2 else 2
    split = Mesh(mesh.devices.reshape(n_row, n_col // cores, cores), ("row", "z", "core"))
    child = P(("row", "z", "core"), None, None)
    parent = P(("z", "core"), None, None)
    return jax.shard_map(
        on_device,
        mesh=split,
        in_specs=(child, parent, child, child, child, child, parent, parent, P(("row", "z", "core"))),
        out_specs=(child, parent),
        check_vma=False,
    )
```

```python
import functools
import math
import jax
import jax.numpy as jnp
from jax import lax
from jax.experimental import pallas as pl
from jax.experimental.pallas import tpu as pltpu
from jax.sharding import Mesh, PartitionSpec as P

F32 = jnp.float32
BF16 = jnp.bfloat16
VMEM = pl.BlockSpec(memory_space=pltpu.VMEM)
ANY = pl.BlockSpec(memory_space=pl.ANY)
MIB = 1 << 20
VMEM_BYTES = 64 * MIB
WAIT = pl.CostEstimate(flops=8 * 10**9, bytes_accessed=MIB, transcendentals=0)


def ranges(count, shares):
    ends = [count * sum(shares[: i + 1]) // sum(shares) for i in range(len(shares))]
    pairs = zip([0] + ends[:-1], ends)
    return [(lo, hi) for lo, hi in pairs if hi > lo]


def params(mib):
    return pltpu.CompilerParams(vmem_limit_bytes=mib * MIB)


def dot(a, b):
    return jnp.dot(a, b, preferred_element_type=F32)


def dot_t(a, b):
    return lax.dot_general(a, b, (((1,), (1,)), ((), ())), preferred_element_type=F32)


def forward_kernel(cores, chunk, owner_hbm, rhs_hbm, inv_hbm, off_hbm, fwd, *rest):
    mine, theirs, scratch = rest[0], rest[1:cores], rest[cores:]
    rhs, inv, off, owner, even, odd, in_sem, owner_sem = scratch
    n_row, _, half, _ = mine.shape
    groups = fwd.shape[0] // chunk
    arrays = ((rhs_hbm, rhs), (inv_hbm, inv), (off_hbm, off))

    def loads(g):
        part = pl.ds(g * chunk, chunk)
        return [
            pltpu.make_async_copy(h.at[part], v.at[part], in_sem.at[s, g])
            for s, (h, v) in enumerate(arrays)
        ]

    names = pltpu.make_async_copy(owner_hbm, owner, owner_sem)
    names.start()

    @pl.loop(0, groups)
    def _(g):
        for copy in loads(g):
            copy.start()

    even[...] = jnp.zeros_like(even)
    odd[...] = jnp.zeros_like(odd)

    def solve(c):
        fwd[c] = dot(inv[c], rhs[c]).astype(BF16)

    def add(c, acc):
        acc[owner[c]] += dot(off[c], fwd[c])

    for copy in loads(0):
        copy.wait()
    for n in range(chunk):
        solve(n)
    names.wait()

    def step(g):
        for copy in loads(g):
            copy.wait()
        for n in range(chunk):
            solve(g * chunk + n)
            add((g - 1) * chunk + n, odd if n % 2 else even)

    pl.loop(1, groups - 1)(step)
    if groups > 1:
        step(groups - 1)
    for n in range(chunk):
        add((groups - 1) * chunk + n, odd if n % 2 else even)
    me = lax.axis_index("core")
    for p in range(even.shape[0]):
        turned = (even[p] + odd[p]).astype(BF16).T
        for r in range(n_row):
            halves = [turned[n * half : (n + 1) * half] for n in range(r * cores, (r + 1) * cores)]
            for k in range(cores):
                out = theirs[k - 1] if k else mine
                value = halves[0]
                for n in range(1, cores):
                    value = jnp.where(lax.rem(me + k, cores) == n, halves[n], value)
                out[r, p] = value


def forward(parent_of, rhs, inv, off, n_row, n_chip, cores, per_col):
    count, width, sides = rhs.shape
    chunk = max(c for c in range(1, 7) if count % c == 0)
    parents = n_chip * cores * per_col
    piece = (n_row, parents, sides // (n_row * cores), width)
    kept = 2 * rhs.size + 2 * cores * math.prod(piece)
    room = (VMEM_BYTES - kept - MIB) // MIB
    return pl.pallas_call(
        functools.partial(forward_kernel, cores, chunk),
        out_shape=[pltpu.VMEM(rhs.shape, BF16)] + [pltpu.VMEM(piece, BF16)] * cores,
        in_specs=[ANY] * 4,
        out_specs=[VMEM] * (1 + cores),
        scratch_shapes=[
            pltpu.VMEM(rhs.shape, BF16),
            pltpu.VMEM(inv.shape, BF16),
            pltpu.VMEM(off.shape, BF16),
            pltpu.SMEM(parent_of.shape, jnp.int32),
            pltpu.VMEM((parents, width, sides), F32),
            pltpu.VMEM((parents, width, sides), F32),
            pltpu.SemaphoreType.DMA((3, count // chunk)),
            pltpu.SemaphoreType.DMA,
        ],
        compiler_params=params(room),
        name="forward",
    )(*(pltpu.with_memory_space_constraint(x, pltpu.HBM) for x in (parent_of, rhs, inv, off)))


def couple_kernel(inv, off, _, out):
    for c in range(out.shape[0]):
        out[c] = (-dot(inv[c], off[c])).astype(BF16)


def couple(inv, off, after):
    count, width, _ = inv.shape
    return pl.pallas_call(
        couple_kernel,
        out_shape=pltpu.VMEM(off.shape, BF16),
        in_specs=[VMEM, VMEM, ANY],
        out_specs=VMEM,
        compiler_params=params(16),
        cost_estimate=pl.CostEstimate(
            flops=2 * count * width**3, bytes_accessed=6 * count * width**2, transcendentals=0
        ),
        name="couple",
    )(inv, off, after)


def core_sum_kernel(*refs):
    total = refs[0][...].astype(F32)
    for part in refs[1:-2]:
        total = total + part[...].astype(F32)
    refs[-1][...] = total.astype(BF16)


def core_sum(parts, after):
    return pl.pallas_call(
        core_sum_kernel,
        out_shape=jax.ShapeDtypeStruct(parts[0].shape, BF16),
        in_specs=[VMEM] * len(parts) + [ANY],
        out_specs=VMEM,
        compiler_params=params(16),
        cost_estimate=WAIT,
        name="core_sum",
    )(*parts, after)


def prepare_kernel(rhs, lower, upper, _, whole, mine, turned):
    slab = mine.shape[1]
    rows = pl.ds(pl.multiple_of(lax.axis_index("row") * slab, slab), slab)
    for p in range(mine.shape[0]):
        whole[p] = dot(upper[p], lower[p]).astype(BF16)
        turned[...] = rhs[p].astype(F32).T
        mine[p] = turned[rows, :]


def prepare(rhs, lower, upper, after, n_row):
    per_col, width, sides = rhs.shape
    return pl.pallas_call(
        prepare_kernel,
        out_shape=[
            jax.ShapeDtypeStruct(lower.shape, BF16),
            jax.ShapeDtypeStruct((per_col, sides // n_row, width), F32),
        ],
        in_specs=[VMEM] * 3 + [ANY],
        out_specs=[VMEM, VMEM],
        scratch_shapes=[pltpu.VMEM((sides, width), F32)],
        compiler_params=params(16),
        name="prepare",
    )(rhs, lower, upper, after)


def parent_kernel(cores, whole, rhs, parts, out):
    devices, per_col, half, _ = out.shape
    for p in range(per_col):
        updates = []
        for k in range(cores):
            terms = [parts[d, p].astype(F32) for d in range(k, devices, cores)]
            while len(terms) > 1:
                pairs = zip(terms[::2], terms[1::2])
                terms = [x + y for x, y in pairs] + terms[len(terms) - len(terms) % 2 :]
            updates.append(terms[0])
        residual = (rhs[p] - jnp.concatenate(updates)).astype(BF16)
        solved = dot_t(residual, whole[p]).astype(BF16)
        for d in range(devices):
            k = d % cores
            out[d, p] = solved[k * half : (k + 1) * half]


def parent_solve(whole, rhs, parts, cores):
    return pl.pallas_call(
        functools.partial(parent_kernel, cores),
        out_shape=jax.ShapeDtypeStruct(parts.shape, BF16),
        in_specs=[VMEM] * 3,
        out_specs=VMEM,
        compiler_params=params(16),
        cost_estimate=WAIT,
        name="parent_solve",
    )(whole, rhs, parts)


def backward_kernel(cores, groups, owner, fwd, inv, coupled, *rest):
    parts, scratch = rest[:cores], rest[cores:]
    out_hbm, solved_hbm, out, flat, picked, out_sem, solved_sem = scratch
    n_row, parents, half, _ = parts[0].shape
    per_col = solved_hbm.shape[0]
    me = lax.axis_index("core")
    for k in range(cores):
        for r in range(n_row):
            start = (r * cores + lax.rem(me + k, cores)) * half
            rows = pl.ds(pl.multiple_of(start, half), half)
            flat[:, rows, :] = parts[k][r]
    for p in range(parents):
        picked[p] = flat[p].T
    mine = (lax.axis_index("z") * cores + me) * per_col
    solved = pltpu.make_async_copy(picked.at[pl.ds(mine, per_col)], solved_hbm, solved_sem)
    solved.start()
    stores = [solved]
    for g, (lo, hi) in enumerate(groups):
        for c in range(lo, hi):
            mats = jnp.concatenate([inv[c], coupled[c]], axis=1)
            out[c] = dot(mats, jnp.concatenate([fwd[c], picked[owner[c]]])).astype(BF16)
        part = pl.ds(lo, hi - lo)
        copy = pltpu.make_async_copy(out.at[part], out_hbm.at[part], out_sem.at[g])
        copy.start()
        stores.append(copy)
    for copy in stores:
        copy.wait()


def backward(parent_of, fwd, inv, coupled, parts, per_col):
    count, width, sides = fwd.shape
    groups = ranges(count, (1, 2, 3, 3, 2, 1))
    parents = parts[0].shape[1]
    return pl.pallas_call(
        functools.partial(backward_kernel, len(parts), groups),
        out_shape=[
            jax.ShapeDtypeStruct(fwd.shape, BF16),
            jax.ShapeDtypeStruct((per_col, width, sides), BF16),
        ],
        in_specs=[VMEM] * (4 + len(parts)),
        out_specs=[ANY, ANY],
        scratch_shapes=[
            pltpu.VMEM(fwd.shape, BF16),
            pltpu.VMEM((parents, sides, width), BF16),
            pltpu.VMEM((parents, width, sides), BF16),
            pltpu.SemaphoreType.DMA((len(groups),)),
            pltpu.SemaphoreType.DMA,
        ],
        compiler_params=params(32),
        name="backward",
    )(parent_of, fwd, inv, coupled, *parts)


def from_core(value, k):
    cores = lax.axis_size("core")
    return lax.ppermute(value, "core", [(i, (i + k) % cores) for i in range(cores)])


def on_device(
    child_rhs,
    parent_rhs,
    child_lower_inv,
    child_lower_off,
    child_upper_inv,
    child_upper_off,
    parent_lower_inv,
    parent_upper_inv,
    parent_of,
):
    n_row, n_chip, cores = (lax.axis_size(a) for a in ("row", "z", "core"))
    per_col = parent_rhs.shape[0]
    fwd, mine, *theirs = forward(
        parent_of, child_rhs, child_lower_inv, child_lower_off, n_row, n_chip, cores, per_col
    )
    theirs = [from_core(x, k) for k, x in enumerate(theirs, 1)]
    whole, rhs = prepare(parent_rhs, parent_lower_inv, parent_upper_inv, mine, n_row)
    total = core_sum([mine] + theirs, whole)
    axes = ("row", "z", "core")
    sent = total.reshape(-1, per_col, *total.shape[2:])
    parts = lax.all_to_all(sent, axes, 0, 0, tiled=True)
    solved = parent_solve(whole, rhs, parts, cores)
    mine = lax.all_to_all(solved, axes, 0, 0, tiled=True).reshape(total.shape)
    parts = [mine] + [from_core(mine, cores - k) for k in range(1, cores)]
    coupled = couple(child_upper_inv, child_upper_off, mine)
    return tuple(backward(parent_of, fwd, child_upper_inv, coupled, parts, per_col))


def solution(mesh):
    n_row, n_col = (mesh.shape[a] for a in ("row", "col"))
    cores = 1 if n_col % 2 else 2
    split = Mesh(mesh.devices.reshape(n_row, n_col // cores, cores), ("row", "z", "core"))
    child = P(("row", "z", "core"), None, None)
    parent = P(("z", "core"), None, None)
    return jax.shard_map(
        on_device,
        mesh=split,
        in_specs=(child, parent, child, child, child, child, parent, parent, P(("row", "z", "core"))),
        out_specs=(child, parent),
        check_vma=False,
    )
```

```python
import functools
import math
import jax
import jax.numpy as jnp
from jax import lax
from jax.experimental import pallas as pl
from jax.experimental.pallas import tpu as pltpu
from jax.sharding import Mesh, PartitionSpec as P

F32 = jnp.float32
BF16 = jnp.bfloat16
VMEM = pl.BlockSpec(memory_space=pltpu.VMEM)
ANY = pl.BlockSpec(memory_space=pl.ANY)
MIB = 1 << 20
VMEM_BYTES = 64 * MIB
WAIT = pl.CostEstimate(flops=8 * 10**9, bytes_accessed=MIB, transcendentals=0)


def ranges(count, shares):
    ends = [count * sum(shares[: i + 1]) // sum(shares) for i in range(len(shares))]
    pairs = zip([0] + ends[:-1], ends)
    return [(lo, hi) for lo, hi in pairs if hi > lo]


def params(mib):
    return pltpu.CompilerParams(vmem_limit_bytes=mib * MIB)


def dot(a, b):
    return jnp.dot(a, b, preferred_element_type=F32)


def dot_t(a, b):
    return lax.dot_general(a, b, (((1,), (1,)), ((), ())), preferred_element_type=F32)


def forward_kernel(cores, chunk, owner_hbm, rhs_hbm, inv_hbm, off_hbm, fwd, *rest):
    mine, theirs, scratch = rest[0], rest[1:cores], rest[cores:]
    rhs, inv, off, owner, even, odd, in_sem, owner_sem = scratch
    n_row, _, half, _ = mine.shape
    groups = fwd.shape[0] // chunk
    arrays = ((rhs_hbm, rhs), (inv_hbm, inv), (off_hbm, off))

    def loads(g):
        part = pl.ds(g * chunk, chunk)
        return [
            pltpu.make_async_copy(h.at[part], v.at[part], in_sem.at[s, g])
            for s, (h, v) in enumerate(arrays)
        ]

    names = pltpu.make_async_copy(owner_hbm, owner, owner_sem)
    names.start()

    @pl.loop(0, groups)
    def _(g):
        for copy in loads(g):
            copy.start()

    even[...] = jnp.zeros_like(even)
    odd[...] = jnp.zeros_like(odd)

    def solve(c):
        fwd[c] = dot(inv[c], rhs[c]).astype(BF16)

    def add(c, acc):
        acc[owner[c]] += dot(off[c], fwd[c])

    for copy in loads(0):
        copy.wait()
    for n in range(chunk):
        solve(n)
    names.wait()

    def step(g):
        for copy in loads(g):
            copy.wait()
        for n in range(chunk):
            solve(g * chunk + n)
            add((g - 1) * chunk + n, odd if n % 2 else even)

    pl.loop(1, groups - 1)(step)
    if groups > 1:
        step(groups - 1)
    for n in range(chunk):
        add((groups - 1) * chunk + n, odd if n % 2 else even)
    me = lax.axis_index("core")
    for p in range(even.shape[0]):
        turned = (even[p] + odd[p]).astype(BF16).T
        for r in range(n_row):
            halves = [turned[n * half : (n + 1) * half] for n in range(r * cores, (r + 1) * cores)]
            for k in range(cores):
                out = theirs[k - 1] if k else mine
                value = halves[0]
                for n in range(1, cores):
                    value = jnp.where(lax.rem(me + k, cores) == n, halves[n], value)
                out[r, p] = value


def forward(parent_of, rhs, inv, off, n_row, n_chip, cores, per_col):
    count, width, sides = rhs.shape
    chunk = max(c for c in range(1, 13) if count % c == 0)
    parents = n_chip * cores * per_col
    piece = (n_row, parents, sides // (n_row * cores), width)
    kept = 2 * rhs.size + 2 * cores * math.prod(piece)
    room = (VMEM_BYTES - kept - MIB) // MIB
    return pl.pallas_call(
        functools.partial(forward_kernel, cores, chunk),
        out_shape=[pltpu.VMEM(rhs.shape, BF16)] + [pltpu.VMEM(piece, BF16)] * cores,
        in_specs=[ANY] * 4,
        out_specs=[VMEM] * (1 + cores),
        scratch_shapes=[
            pltpu.VMEM(rhs.shape, BF16),
            pltpu.VMEM(inv.shape, BF16),
            pltpu.VMEM(off.shape, BF16),
            pltpu.SMEM(parent_of.shape, jnp.int32),
            pltpu.VMEM((parents, width, sides), F32),
            pltpu.VMEM((parents, width, sides), F32),
            pltpu.SemaphoreType.DMA((3, count // chunk)),
            pltpu.SemaphoreType.DMA,
        ],
        compiler_params=params(room),
        name="forward",
    )(*(pltpu.with_memory_space_constraint(x, pltpu.HBM) for x in (parent_of, rhs, inv, off)))


def couple_kernel(inv, off, _, out):
    for c in range(out.shape[0]):
        out[c] = (-dot(inv[c], off[c])).astype(BF16)


def couple(inv, off, after):
    count, width, _ = inv.shape
    return pl.pallas_call(
        couple_kernel,
        out_shape=pltpu.VMEM(off.shape, BF16),
        in_specs=[VMEM, VMEM, ANY],
        out_specs=VMEM,
        compiler_params=params(16),
        cost_estimate=pl.CostEstimate(
            flops=2 * count * width**3, bytes_accessed=6 * count * width**2, transcendentals=0
        ),
        name="couple",
    )(inv, off, after)


def core_sum_kernel(*refs):
    total = refs[0][...].astype(F32)
    for part in refs[1:-2]:
        total = total + part[...].astype(F32)
    refs[-1][...] = total.astype(BF16)


def core_sum(parts, after):
    return pl.pallas_call(
        core_sum_kernel,
        out_shape=jax.ShapeDtypeStruct(parts[0].shape, BF16),
        in_specs=[VMEM] * len(parts) + [ANY],
        out_specs=VMEM,
        compiler_params=params(16),
        cost_estimate=WAIT,
        name="core_sum",
    )(*parts, after)


def prepare_kernel(rhs, lower, upper, _, whole, mine, turned):
    slab = mine.shape[1]
    rows = pl.ds(pl.multiple_of(lax.axis_index("row") * slab, slab), slab)
    for p in range(mine.shape[0]):
        whole[p] = dot(upper[p], lower[p]).astype(BF16)
        turned[...] = rhs[p].astype(F32).T
        mine[p] = turned[rows, :]


def prepare(rhs, lower, upper, after, n_row):
    per_col, width, sides = rhs.shape
    return pl.pallas_call(
        prepare_kernel,
        out_shape=[
            jax.ShapeDtypeStruct(lower.shape, BF16),
            jax.ShapeDtypeStruct((per_col, sides // n_row, width), F32),
        ],
        in_specs=[VMEM] * 3 + [ANY],
        out_specs=[VMEM, VMEM],
        scratch_shapes=[pltpu.VMEM((sides, width), F32)],
        compiler_params=params(16),
        name="prepare",
    )(rhs, lower, upper, after)


def parent_kernel(cores, whole, rhs, parts, out):
    devices, per_col, half, _ = out.shape
    for p in range(per_col):
        updates = []
        for k in range(cores):
            terms = [parts[d, p].astype(F32) for d in range(k, devices, cores)]
            while len(terms) > 1:
                pairs = zip(terms[::2], terms[1::2])
                terms = [x + y for x, y in pairs] + terms[len(terms) - len(terms) % 2 :]
            updates.append(terms[0])
        residual = (rhs[p] - jnp.concatenate(updates)).astype(BF16)
        solved = dot_t(residual, whole[p]).astype(BF16)
        for d in range(devices):
            k = d % cores
            out[d, p] = solved[k * half : (k + 1) * half]


def parent_solve(whole, rhs, parts, cores):
    return pl.pallas_call(
        functools.partial(parent_kernel, cores),
        out_shape=jax.ShapeDtypeStruct(parts.shape, BF16),
        in_specs=[VMEM] * 3,
        out_specs=VMEM,
        compiler_params=params(16),
        cost_estimate=WAIT,
        name="parent_solve",
    )(whole, rhs, parts)


def backward_kernel(cores, groups, owner, fwd, inv, coupled, *rest):
    parts, scratch = rest[:cores], rest[cores:]
    out_hbm, solved_hbm, out, flat, picked, out_sem, solved_sem = scratch
    n_row, parents, half, _ = parts[0].shape
    per_col = solved_hbm.shape[0]
    me = lax.axis_index("core")
    for k in range(cores):
        for r in range(n_row):
            start = (r * cores + lax.rem(me + k, cores)) * half
            rows = pl.ds(pl.multiple_of(start, half), half)
            flat[:, rows, :] = parts[k][r]
    for p in range(parents):
        picked[p] = flat[p].T
    mine = (lax.axis_index("z") * cores + me) * per_col
    solved = pltpu.make_async_copy(picked.at[pl.ds(mine, per_col)], solved_hbm, solved_sem)
    solved.start()
    stores = [solved]
    for g, (lo, hi) in enumerate(groups):
        for c in range(lo, hi):
            mats = jnp.concatenate([inv[c], coupled[c]], axis=1)
            out[c] = dot(mats, jnp.concatenate([fwd[c], picked[owner[c]]])).astype(BF16)
        part = pl.ds(lo, hi - lo)
        copy = pltpu.make_async_copy(out.at[part], out_hbm.at[part], out_sem.at[g])
        copy.start()
        stores.append(copy)
    for copy in stores:
        copy.wait()


def backward(parent_of, fwd, inv, coupled, parts, per_col):
    count, width, sides = fwd.shape
    groups = ranges(count, (1, 2, 3, 3, 2, 1))
    parents = parts[0].shape[1]
    return pl.pallas_call(
        functools.partial(backward_kernel, len(parts), groups),
        out_shape=[
            jax.ShapeDtypeStruct(fwd.shape, BF16),
            jax.ShapeDtypeStruct((per_col, width, sides), BF16),
        ],
        in_specs=[VMEM] * (4 + len(parts)),
        out_specs=[ANY, ANY],
        scratch_shapes=[
            pltpu.VMEM(fwd.shape, BF16),
            pltpu.VMEM((parents, sides, width), BF16),
            pltpu.VMEM((parents, width, sides), BF16),
            pltpu.SemaphoreType.DMA((len(groups),)),
            pltpu.SemaphoreType.DMA,
        ],
        compiler_params=params(32),
        name="backward",
    )(parent_of, fwd, inv, coupled, *parts)


def from_core(value, k):
    cores = lax.axis_size("core")
    return lax.ppermute(value, "core", [(i, (i + k) % cores) for i in range(cores)])


def on_device(
    child_rhs,
    parent_rhs,
    child_lower_inv,
    child_lower_off,
    child_upper_inv,
    child_upper_off,
    parent_lower_inv,
    parent_upper_inv,
    parent_of,
):
    n_row, n_chip, cores = (lax.axis_size(a) for a in ("row", "z", "core"))
    per_col = parent_rhs.shape[0]
    fwd, mine, *theirs = forward(
        parent_of, child_rhs, child_lower_inv, child_lower_off, n_row, n_chip, cores, per_col
    )
    theirs = [from_core(x, k) for k, x in enumerate(theirs, 1)]
    whole, rhs = prepare(parent_rhs, parent_lower_inv, parent_upper_inv, mine, n_row)
    total = core_sum([mine] + theirs, whole)
    axes = ("row", "z", "core")
    sent = total.reshape(-1, per_col, *total.shape[2:])
    parts = lax.all_to_all(sent, axes, 0, 0, tiled=True)
    solved = parent_solve(whole, rhs, parts, cores)
    mine = lax.all_to_all(solved, axes, 0, 0, tiled=True).reshape(total.shape)
    parts = [mine] + [from_core(mine, cores - k) for k in range(1, cores)]
    coupled = couple(child_upper_inv, child_upper_off, mine)
    return tuple(backward(parent_of, fwd, child_upper_inv, coupled, parts, per_col))


def solution(mesh):
    n_row, n_col = (mesh.shape[a] for a in ("row", "col"))
    cores = 1 if n_col % 2 else 2
    split = Mesh(mesh.devices.reshape(n_row, n_col // cores, cores), ("row", "z", "core"))
    child = P(("row", "z", "core"), None, None)
    parent = P(("z", "core"), None, None)
    return jax.shard_map(
        on_device,
        mesh=split,
        in_specs=(child, parent, child, child, child, child, parent, parent, P(("row", "z", "core"))),
        out_specs=(child, parent),
        check_vma=False,
    )
```

```python
import functools
import math
import jax
import jax.numpy as jnp
from jax import lax
from jax.experimental import pallas as pl
from jax.experimental.pallas import tpu as pltpu
from jax.sharding import Mesh, PartitionSpec as P

F32 = jnp.float32
BF16 = jnp.bfloat16
VMEM = pl.BlockSpec(memory_space=pltpu.VMEM)
ANY = pl.BlockSpec(memory_space=pl.ANY)
MIB = 1 << 20
VMEM_BYTES = 64 * MIB
WAIT = pl.CostEstimate(flops=8 * 10**9, bytes_accessed=MIB, transcendentals=0)


def ranges(count, shares):
    ends = [count * sum(shares[: i + 1]) // sum(shares) for i in range(len(shares))]
    pairs = zip([0] + ends[:-1], ends)
    return [(lo, hi) for lo, hi in pairs if hi > lo]


def params(mib):
    return pltpu.CompilerParams(vmem_limit_bytes=mib * MIB)


def dot(a, b):
    return jnp.dot(a, b, preferred_element_type=F32)


def dot_t(a, b):
    return lax.dot_general(a, b, (((1,), (1,)), ((), ())), preferred_element_type=F32)


def forward_kernel(cores, chunk, owner_hbm, rhs_hbm, inv_hbm, off_hbm, fwd, *rest):
    mine, theirs, scratch = rest[0], rest[1:cores], rest[cores:]
    rhs, inv, off, owner, even, odd, in_sem, owner_sem = scratch
    n_row, _, half, _ = mine.shape
    groups = fwd.shape[0] // chunk
    arrays = ((rhs_hbm, rhs), (inv_hbm, inv), (off_hbm, off))

    def loads(g):
        part = pl.ds(g * chunk, chunk)
        return [
            pltpu.make_async_copy(h.at[part], v.at[part], in_sem.at[s, g])
            for s, (h, v) in enumerate(arrays)
        ]

    names = pltpu.make_async_copy(owner_hbm, owner, owner_sem)
    names.start()

    @pl.loop(0, groups)
    def _(g):
        for copy in loads(g):
            copy.start()

    even[...] = jnp.zeros_like(even)
    odd[...] = jnp.zeros_like(odd)

    def solve(c):
        fwd[c] = dot(inv[c], rhs[c]).astype(BF16)

    def add(c, acc):
        acc[owner[c]] += dot(off[c], fwd[c])

    for copy in loads(0):
        copy.wait()
    for n in range(chunk):
        solve(n)
    names.wait()

    def step(g):
        for copy in loads(g):
            copy.wait()
        for n in range(chunk):
            solve(g * chunk + n)
            add((g - 1) * chunk + n, odd if n % 2 else even)

    pl.loop(1, groups - 1)(step)
    if groups > 1:
        step(groups - 1)
    for n in range(chunk):
        add((groups - 1) * chunk + n, odd if n % 2 else even)
    me = lax.axis_index("core")
    for p in range(even.shape[0]):
        turned = (even[p] + odd[p]).astype(BF16).T
        for r in range(n_row):
            halves = [turned[n * half : (n + 1) * half] for n in range(r * cores, (r + 1) * cores)]
            for k in range(cores):
                out = theirs[k - 1] if k else mine
                value = halves[0]
                for n in range(1, cores):
                    value = jnp.where(lax.rem(me + k, cores) == n, halves[n], value)
                out[r, p] = value


def forward(parent_of, rhs, inv, off, n_row, n_chip, cores, per_col):
    count, width, sides = rhs.shape
    chunk = max(c for c in range(1, 17) if count % c == 0)
    parents = n_chip * cores * per_col
    piece = (n_row, parents, sides // (n_row * cores), width)
    kept = 2 * rhs.size + 2 * cores * math.prod(piece)
    room = (VMEM_BYTES - kept - MIB) // MIB
    return pl.pallas_call(
        functools.partial(forward_kernel, cores, chunk),
        out_shape=[pltpu.VMEM(rhs.shape, BF16)] + [pltpu.VMEM(piece, BF16)] * cores,
        in_specs=[ANY] * 4,
        out_specs=[VMEM] * (1 + cores),
        scratch_shapes=[
            pltpu.VMEM(rhs.shape, BF16),
            pltpu.VMEM(inv.shape, BF16),
            pltpu.VMEM(off.shape, BF16),
            pltpu.SMEM(parent_of.shape, jnp.int32),
            pltpu.VMEM((parents, width, sides), F32),
            pltpu.VMEM((parents, width, sides), F32),
            pltpu.SemaphoreType.DMA((3, count // chunk)),
            pltpu.SemaphoreType.DMA,
        ],
        compiler_params=params(room),
        name="forward",
    )(*(pltpu.with_memory_space_constraint(x, pltpu.HBM) for x in (parent_of, rhs, inv, off)))


def couple_kernel(inv, off, _, out):
    for c in range(out.shape[0]):
        out[c] = (-dot(inv[c], off[c])).astype(BF16)


def couple(inv, off, after):
    count, width, _ = inv.shape
    return pl.pallas_call(
        couple_kernel,
        out_shape=pltpu.VMEM(off.shape, BF16),
        in_specs=[VMEM, VMEM, ANY],
        out_specs=VMEM,
        compiler_params=params(16),
        cost_estimate=pl.CostEstimate(
            flops=2 * count * width**3, bytes_accessed=6 * count * width**2, transcendentals=0
        ),
        name="couple",
    )(inv, off, after)


def core_sum_kernel(*refs):
    total = refs[0][...].astype(F32)
    for part in refs[1:-2]:
        total = total + part[...].astype(F32)
    refs[-1][...] = total.astype(BF16)


def core_sum(parts, after):
    return pl.pallas_call(
        core_sum_kernel,
        out_shape=jax.ShapeDtypeStruct(parts[0].shape, BF16),
        in_specs=[VMEM] * len(parts) + [ANY],
        out_specs=VMEM,
        compiler_params=params(16),
        cost_estimate=WAIT,
        name="core_sum",
    )(*parts, after)


def prepare_kernel(rhs, lower, upper, _, whole, mine, turned):
    slab = mine.shape[1]
    rows = pl.ds(pl.multiple_of(lax.axis_index("row") * slab, slab), slab)
    for p in range(mine.shape[0]):
        whole[p] = dot(upper[p], lower[p]).astype(BF16)
        turned[...] = rhs[p].astype(F32).T
        mine[p] = turned[rows, :]


def prepare(rhs, lower, upper, after, n_row):
    per_col, width, sides = rhs.shape
    return pl.pallas_call(
        prepare_kernel,
        out_shape=[
            jax.ShapeDtypeStruct(lower.shape, BF16),
            jax.ShapeDtypeStruct((per_col, sides // n_row, width), F32),
        ],
        in_specs=[VMEM] * 3 + [ANY],
        out_specs=[VMEM, VMEM],
        scratch_shapes=[pltpu.VMEM((sides, width), F32)],
        compiler_params=params(16),
        name="prepare",
    )(rhs, lower, upper, after)


def parent_kernel(cores, whole, rhs, parts, out):
    devices, per_col, half, _ = out.shape
    for p in range(per_col):
        updates = []
        for k in range(cores):
            terms = [parts[d, p].astype(F32) for d in range(k, devices, cores)]
            while len(terms) > 1:
                pairs = zip(terms[::2], terms[1::2])
                terms = [x + y for x, y in pairs] + terms[len(terms) - len(terms) % 2 :]
            updates.append(terms[0])
        residual = (rhs[p] - jnp.concatenate(updates)).astype(BF16)
        solved = dot_t(residual, whole[p]).astype(BF16)
        for d in range(devices):
            k = d % cores
            out[d, p] = solved[k * half : (k + 1) * half]


def parent_solve(whole, rhs, parts, cores):
    return pl.pallas_call(
        functools.partial(parent_kernel, cores),
        out_shape=jax.ShapeDtypeStruct(parts.shape, BF16),
        in_specs=[VMEM] * 3,
        out_specs=VMEM,
        compiler_params=params(16),
        cost_estimate=WAIT,
        name="parent_solve",
    )(whole, rhs, parts)


def backward_kernel(cores, groups, owner, fwd, inv, coupled, *rest):
    parts, scratch = rest[:cores], rest[cores:]
    out_hbm, solved_hbm, out, flat, picked, out_sem, solved_sem = scratch
    n_row, parents, half, _ = parts[0].shape
    per_col = solved_hbm.shape[0]
    me = lax.axis_index("core")
    for k in range(cores):
        for r in range(n_row):
            start = (r * cores + lax.rem(me + k, cores)) * half
            rows = pl.ds(pl.multiple_of(start, half), half)
            flat[:, rows, :] = parts[k][r]
    for p in range(parents):
        picked[p] = flat[p].T
    mine = (lax.axis_index("z") * cores + me) * per_col
    solved = pltpu.make_async_copy(picked.at[pl.ds(mine, per_col)], solved_hbm, solved_sem)
    solved.start()
    stores = [solved]
    for g, (lo, hi) in enumerate(groups):
        for c in range(lo, hi):
            mats = jnp.concatenate([inv[c], coupled[c]], axis=1)
            out[c] = dot(mats, jnp.concatenate([fwd[c], picked[owner[c]]])).astype(BF16)
        part = pl.ds(lo, hi - lo)
        copy = pltpu.make_async_copy(out.at[part], out_hbm.at[part], out_sem.at[g])
        copy.start()
        stores.append(copy)
    for copy in stores:
        copy.wait()


def backward(parent_of, fwd, inv, coupled, parts, per_col):
    count, width, sides = fwd.shape
    groups = ranges(count, (1, 2, 3))
    parents = parts[0].shape[1]
    return pl.pallas_call(
        functools.partial(backward_kernel, len(parts), groups),
        out_shape=[
            jax.ShapeDtypeStruct(fwd.shape, BF16),
            jax.ShapeDtypeStruct((per_col, width, sides), BF16),
        ],
        in_specs=[VMEM] * (4 + len(parts)),
        out_specs=[ANY, ANY],
        scratch_shapes=[
            pltpu.VMEM(fwd.shape, BF16),
            pltpu.VMEM((parents, sides, width), BF16),
            pltpu.VMEM((parents, width, sides), BF16),
            pltpu.SemaphoreType.DMA((len(groups),)),
            pltpu.SemaphoreType.DMA,
        ],
        compiler_params=params(32),
        name="backward",
    )(parent_of, fwd, inv, coupled, *parts)


def from_core(value, k):
    cores = lax.axis_size("core")
    return lax.ppermute(value, "core", [(i, (i + k) % cores) for i in range(cores)])


def on_device(
    child_rhs,
    parent_rhs,
    child_lower_inv,
    child_lower_off,
    child_upper_inv,
    child_upper_off,
    parent_lower_inv,
    parent_upper_inv,
    parent_of,
):
    n_row, n_chip, cores = (lax.axis_size(a) for a in ("row", "z", "core"))
    per_col = parent_rhs.shape[0]
    fwd, mine, *theirs = forward(
        parent_of, child_rhs, child_lower_inv, child_lower_off, n_row, n_chip, cores, per_col
    )
    theirs = [from_core(x, k) for k, x in enumerate(theirs, 1)]
    whole, rhs = prepare(parent_rhs, parent_lower_inv, parent_upper_inv, mine, n_row)
    total = core_sum([mine] + theirs, whole)
    axes = ("row", "z", "core")
    sent = total.reshape(-1, per_col, *total.shape[2:])
    parts = lax.all_to_all(sent, axes, 0, 0, tiled=True)
    solved = parent_solve(whole, rhs, parts, cores)
    mine = lax.all_to_all(solved, axes, 0, 0, tiled=True).reshape(total.shape)
    parts = [mine] + [from_core(mine, cores - k) for k in range(1, cores)]
    coupled = couple(child_upper_inv, child_upper_off, mine)
    return tuple(backward(parent_of, fwd, child_upper_inv, coupled, parts, per_col))


def solution(mesh):
    n_row, n_col = (mesh.shape[a] for a in ("row", "col"))
    cores = 1 if n_col % 2 else 2
    split = Mesh(mesh.devices.reshape(n_row, n_col // cores, cores), ("row", "z", "core"))
    child = P(("row", "z", "core"), None, None)
    parent = P(("z", "core"), None, None)
    return jax.shard_map(
        on_device,
        mesh=split,
        in_specs=(child, parent, child, child, child, child, parent, parent, P(("row", "z", "core"))),
        out_specs=(child, parent),
        check_vma=False,
    )
```

```python
import functools
import math
import jax
import jax.numpy as jnp
from jax import lax
from jax.experimental import pallas as pl
from jax.experimental.pallas import tpu as pltpu
from jax.sharding import Mesh, PartitionSpec as P

F32 = jnp.float32
BF16 = jnp.bfloat16
VMEM = pl.BlockSpec(memory_space=pltpu.VMEM)
ANY = pl.BlockSpec(memory_space=pl.ANY)
MIB = 1 << 20
VMEM_BYTES = 64 * MIB
WAIT = pl.CostEstimate(flops=8 * 10**9, bytes_accessed=MIB, transcendentals=0)


def ranges(count, shares):
    ends = [count * sum(shares[: i + 1]) // sum(shares) for i in range(len(shares))]
    pairs = zip([0] + ends[:-1], ends)
    return [(lo, hi) for lo, hi in pairs if hi > lo]


def params(mib):
    return pltpu.CompilerParams(vmem_limit_bytes=mib * MIB)


def dot(a, b):
    return jnp.dot(a, b, preferred_element_type=F32)


def dot_t(a, b):
    return lax.dot_general(a, b, (((1,), (1,)), ((), ())), preferred_element_type=F32)


def forward_kernel(cores, chunk, owner_hbm, rhs_hbm, inv_hbm, off_hbm, fwd, *rest):
    mine, theirs, scratch = rest[0], rest[1:cores], rest[cores:]
    rhs, inv, off, owner, even, odd, in_sem, owner_sem = scratch
    n_row, _, half, _ = mine.shape
    groups = fwd.shape[0] // chunk
    arrays = ((rhs_hbm, rhs), (inv_hbm, inv), (off_hbm, off))

    def loads(g):
        part = pl.ds(g * chunk, chunk)
        return [
            pltpu.make_async_copy(h.at[part], v.at[part], in_sem.at[s, g])
            for s, (h, v) in enumerate(arrays)
        ]

    names = pltpu.make_async_copy(owner_hbm, owner, owner_sem)
    names.start()

    @pl.loop(0, groups)
    def _(g):
        for copy in loads(g):
            copy.start()

    even[...] = jnp.zeros_like(even)
    odd[...] = jnp.zeros_like(odd)

    def solve(c):
        fwd[c] = dot(inv[c], rhs[c]).astype(BF16)

    def add(c, acc):
        acc[owner[c]] += dot(off[c], fwd[c])

    for copy in loads(0):
        copy.wait()
    for n in range(chunk):
        solve(n)
    names.wait()

    def step(g):
        for copy in loads(g):
            copy.wait()
        for n in range(chunk):
            solve(g * chunk + n)
            add((g - 1) * chunk + n, odd if n % 2 else even)

    pl.loop(1, groups - 1)(step)
    if groups > 1:
        step(groups - 1)
    for n in range(chunk):
        add((groups - 1) * chunk + n, odd if n % 2 else even)
    me = lax.axis_index("core")
    for p in range(even.shape[0]):
        turned = (even[p] + odd[p]).astype(BF16).T
        for r in range(n_row):
            halves = [turned[n * half : (n + 1) * half] for n in range(r * cores, (r + 1) * cores)]
            for k in range(cores):
                out = theirs[k - 1] if k else mine
                value = halves[0]
                for n in range(1, cores):
                    value = jnp.where(lax.rem(me + k, cores) == n, halves[n], value)
                out[r, p] = value


def forward(parent_of, rhs, inv, off, n_row, n_chip, cores, per_col):
    count, width, sides = rhs.shape
    chunk = max(c for c in range(1, 13) if count % c == 0)
    parents = n_chip * cores * per_col
    piece = (n_row, parents, sides // (n_row * cores), width)
    kept = 2 * rhs.size + 2 * cores * math.prod(piece)
    room = (VMEM_BYTES - kept - MIB) // MIB
    return pl.pallas_call(
        functools.partial(forward_kernel, cores, chunk),
        out_shape=[pltpu.VMEM(rhs.shape, BF16)] + [pltpu.VMEM(piece, BF16)] * cores,
        in_specs=[ANY] * 4,
        out_specs=[VMEM] * (1 + cores),
        scratch_shapes=[
            pltpu.VMEM(rhs.shape, BF16),
            pltpu.VMEM(inv.shape, BF16),
            pltpu.VMEM(off.shape, BF16),
            pltpu.SMEM(parent_of.shape, jnp.int32),
            pltpu.VMEM((parents, width, sides), F32),
            pltpu.VMEM((parents, width, sides), F32),
            pltpu.SemaphoreType.DMA((3, count // chunk)),
            pltpu.SemaphoreType.DMA,
        ],
        compiler_params=params(room),
        name="forward",
    )(*(pltpu.with_memory_space_constraint(x, pltpu.HBM) for x in (parent_of, rhs, inv, off)))


def couple_kernel(inv, off, _, out):
    for c in range(out.shape[0]):
        out[c] = (-dot(inv[c], off[c])).astype(BF16)


def couple(inv, off, after):
    count, width, _ = inv.shape
    return pl.pallas_call(
        couple_kernel,
        out_shape=pltpu.VMEM(off.shape, BF16),
        in_specs=[VMEM, VMEM, ANY],
        out_specs=VMEM,
        compiler_params=params(16),
        cost_estimate=pl.CostEstimate(
            flops=2 * count * width**3, bytes_accessed=6 * count * width**2, transcendentals=0
        ),
        name="couple",
    )(inv, off, after)


def core_sum_kernel(*refs):
    total = refs[0][...].astype(F32)
    for part in refs[1:-2]:
        total = total + part[...].astype(F32)
    refs[-1][...] = total.astype(BF16)


def core_sum(parts, after):
    return pl.pallas_call(
        core_sum_kernel,
        out_shape=jax.ShapeDtypeStruct(parts[0].shape, BF16),
        in_specs=[VMEM] * len(parts) + [ANY],
        out_specs=VMEM,
        compiler_params=params(16),
        cost_estimate=WAIT,
        name="core_sum",
    )(*parts, after)


def prepare_kernel(rhs, lower, upper, _, whole, mine, turned):
    slab = mine.shape[1]
    rows = pl.ds(pl.multiple_of(lax.axis_index("row") * slab, slab), slab)
    for p in range(mine.shape[0]):
        whole[p] = dot(upper[p], lower[p]).astype(BF16)
        turned[...] = rhs[p].astype(F32).T
        mine[p] = turned[rows, :]


def prepare(rhs, lower, upper, after, n_row):
    per_col, width, sides = rhs.shape
    return pl.pallas_call(
        prepare_kernel,
        out_shape=[
            jax.ShapeDtypeStruct(lower.shape, BF16),
            jax.ShapeDtypeStruct((per_col, sides // n_row, width), F32),
        ],
        in_specs=[VMEM] * 3 + [ANY],
        out_specs=[VMEM, VMEM],
        scratch_shapes=[pltpu.VMEM((sides, width), F32)],
        compiler_params=params(16),
        name="prepare",
    )(rhs, lower, upper, after)


def parent_kernel(cores, whole, rhs, parts, out):
    devices, per_col, half, _ = out.shape
    for p in range(per_col):
        updates = []
        for k in range(cores):
            terms = [parts[d, p].astype(F32) for d in range(k, devices, cores)]
            while len(terms) > 1:
                pairs = zip(terms[::2], terms[1::2])
                terms = [x + y for x, y in pairs] + terms[len(terms) - len(terms) % 2 :]
            updates.append(terms[0])
        residual = (rhs[p] - jnp.concatenate(updates)).astype(BF16)
        solved = dot_t(residual, whole[p]).astype(BF16)
        for d in range(devices):
            k = d % cores
            out[d, p] = solved[k * half : (k + 1) * half]


def parent_solve(whole, rhs, parts, cores):
    return pl.pallas_call(
        functools.partial(parent_kernel, cores),
        out_shape=jax.ShapeDtypeStruct(parts.shape, BF16),
        in_specs=[VMEM] * 3,
        out_specs=VMEM,
        compiler_params=params(16),
        cost_estimate=WAIT,
        name="parent_solve",
    )(whole, rhs, parts)


def backward_kernel(cores, groups, owner, fwd, inv, coupled, *rest):
    parts, scratch = rest[:cores], rest[cores:]
    out_hbm, solved_hbm, out, picked, out_sem, solved_sem = scratch
    n_row, parents, half, _ = parts[0].shape
    per_col = solved_hbm.shape[0]
    me = lax.axis_index("core")
    for p in range(parents):
        rows = []
        for r in range(n_row):
            for n in range(cores):
                value = parts[0][r, p]
                for k in range(1, cores):
                    value = jnp.where(lax.rem(me + k, cores) == n, parts[k][r, p], value)
                rows.append(value)
        picked[p] = jnp.concatenate(rows).T
    mine = (lax.axis_index("z") * cores + me) * per_col
    solved = pltpu.make_async_copy(picked.at[pl.ds(mine, per_col)], solved_hbm, solved_sem)
    solved.start()
    stores = [solved]
    for g, (lo, hi) in enumerate(groups):
        for c in range(lo, hi):
            mats = jnp.concatenate([inv[c], coupled[c]], axis=1)
            out[c] = dot(mats, jnp.concatenate([fwd[c], picked[owner[c]]])).astype(BF16)
        part = pl.ds(lo, hi - lo)
        copy = pltpu.make_async_copy(out.at[part], out_hbm.at[part], out_sem.at[g])
        copy.start()
        stores.append(copy)
    for copy in stores:
        copy.wait()


def backward(parent_of, fwd, inv, coupled, parts, per_col):
    count, width, sides = fwd.shape
    groups = ranges(count, (1, 2, 3, 4, 5, 4, 3, 2))
    parents = parts[0].shape[1]
    return pl.pallas_call(
        functools.partial(backward_kernel, len(parts), groups),
        out_shape=[
            jax.ShapeDtypeStruct(fwd.shape, BF16),
            jax.ShapeDtypeStruct((per_col, width, sides), BF16),
        ],
        in_specs=[VMEM] * (4 + len(parts)),
        out_specs=[ANY, ANY],
        scratch_shapes=[
            pltpu.VMEM(fwd.shape, BF16),
            pltpu.VMEM((parents, width, sides), BF16),
            pltpu.SemaphoreType.DMA((len(groups),)),
            pltpu.SemaphoreType.DMA,
        ],
        compiler_params=params(32),
        name="backward",
    )(parent_of, fwd, inv, coupled, *parts)


def from_core(value, k):
    cores = lax.axis_size("core")
    return lax.ppermute(value, "core", [(i, (i + k) % cores) for i in range(cores)])


def on_device(
    child_rhs,
    parent_rhs,
    child_lower_inv,
    child_lower_off,
    child_upper_inv,
    child_upper_off,
    parent_lower_inv,
    parent_upper_inv,
    parent_of,
):
    n_row, n_chip, cores = (lax.axis_size(a) for a in ("row", "z", "core"))
    per_col = parent_rhs.shape[0]
    fwd, mine, *theirs = forward(
        parent_of, child_rhs, child_lower_inv, child_lower_off, n_row, n_chip, cores, per_col
    )
    theirs = [from_core(x, k) for k, x in enumerate(theirs, 1)]
    whole, rhs = prepare(parent_rhs, parent_lower_inv, parent_upper_inv, mine, n_row)
    total = core_sum([mine] + theirs, whole)
    axes = ("row", "z", "core")
    sent = total.reshape(-1, per_col, *total.shape[2:])
    parts = lax.all_to_all(sent, axes, 0, 0, tiled=True)
    solved = parent_solve(whole, rhs, parts, cores)
    mine = lax.all_to_all(solved, axes, 0, 0, tiled=True).reshape(total.shape)
    parts = [mine] + [from_core(mine, cores - k) for k in range(1, cores)]
    coupled = couple(child_upper_inv, child_upper_off, mine)
    return tuple(backward(parent_of, fwd, child_upper_inv, coupled, parts, per_col))


def solution(mesh):
    n_row, n_col = (mesh.shape[a] for a in ("row", "col"))
    cores = 1 if n_col % 2 else 2
    split = Mesh(mesh.devices.reshape(n_row, n_col // cores, cores), ("row", "z", "core"))
    child = P(("row", "z", "core"), None, None)
    parent = P(("z", "core"), None, None)
    return jax.shard_map(
        on_device,
        mesh=split,
        in_specs=(child, parent, child, child, child, child, parent, parent, P(("row", "z", "core"))),
        out_specs=(child, parent),
        check_vma=False,
    )
```

```python
import functools
import math
import jax
import jax.numpy as jnp
from jax import lax
from jax.experimental import pallas as pl
from jax.experimental.pallas import tpu as pltpu
from jax.sharding import Mesh, PartitionSpec as P

F32 = jnp.float32
BF16 = jnp.bfloat16
VMEM = pl.BlockSpec(memory_space=pltpu.VMEM)
ANY = pl.BlockSpec(memory_space=pl.ANY)
MIB = 1 << 20
VMEM_BYTES = 64 * MIB
WAIT = pl.CostEstimate(flops=8 * 10**9, bytes_accessed=MIB, transcendentals=0)


def ranges(count, shares):
    ends = [count * sum(shares[: i + 1]) // sum(shares) for i in range(len(shares))]
    pairs = zip([0] + ends[:-1], ends)
    return [(lo, hi) for lo, hi in pairs if hi > lo]


def params(mib):
    return pltpu.CompilerParams(vmem_limit_bytes=mib * MIB)


def dot(a, b):
    return jnp.dot(a, b, preferred_element_type=F32)


def dot_t(a, b):
    return lax.dot_general(a, b, (((1,), (1,)), ((), ())), preferred_element_type=F32)


def forward_kernel(cores, chunk, owner_hbm, rhs_hbm, inv_hbm, off_hbm, fwd, *rest):
    mine, theirs, scratch = rest[0], rest[1:cores], rest[cores:]
    rhs, inv, off, owner, even, odd, in_sem, owner_sem = scratch
    n_row, _, half, _ = mine.shape
    groups = fwd.shape[0] // chunk
    arrays = ((rhs_hbm, rhs), (inv_hbm, inv), (off_hbm, off))

    def loads(g):
        part = pl.ds(g * chunk, chunk)
        return [
            pltpu.make_async_copy(h.at[part], v.at[part], in_sem.at[s, g])
            for s, (h, v) in enumerate(arrays)
        ]

    names = pltpu.make_async_copy(owner_hbm, owner, owner_sem)
    names.start()

    @pl.loop(0, groups)
    def _(g):
        for copy in loads(g):
            copy.start()

    even[...] = jnp.zeros_like(even)
    odd[...] = jnp.zeros_like(odd)

    def solve(c):
        fwd[c] = dot(inv[c], rhs[c]).astype(BF16)

    def add(c, acc):
        acc[owner[c]] += dot(off[c], fwd[c])

    for copy in loads(0):
        copy.wait()
    for n in range(chunk):
        solve(n)
    names.wait()

    def step(g):
        for copy in loads(g):
            copy.wait()
        for n in range(chunk):
            solve(g * chunk + n)
            add((g - 1) * chunk + n, odd if n % 2 else even)

    pl.loop(1, groups - 1)(step)
    if groups > 1:
        step(groups - 1)
    for n in range(chunk):
        add((groups - 1) * chunk + n, odd if n % 2 else even)
    me = lax.axis_index("core")
    for p in range(even.shape[0]):
        turned = (even[p] + odd[p]).astype(BF16).T
        for r in range(n_row):
            halves = [turned[n * half : (n + 1) * half] for n in range(r * cores, (r + 1) * cores)]
            for k in range(cores):
                out = theirs[k - 1] if k else mine
                value = halves[0]
                for n in range(1, cores):
                    value = jnp.where(lax.rem(me + k, cores) == n, halves[n], value)
                out[r, p] = value


def forward(parent_of, rhs, inv, off, n_row, n_chip, cores, per_col):
    count, width, sides = rhs.shape
    chunk = max(c for c in range(1, 13) if count % c == 0)
    parents = n_chip * cores * per_col
    piece = (n_row, parents, sides // (n_row * cores), width)
    kept = 2 * rhs.size + 2 * cores * math.prod(piece)
    room = (VMEM_BYTES - kept - MIB) // MIB
    return pl.pallas_call(
        functools.partial(forward_kernel, cores, chunk),
        out_shape=[pltpu.VMEM(rhs.shape, BF16)] + [pltpu.VMEM(piece, BF16)] * cores,
        in_specs=[ANY] * 4,
        out_specs=[VMEM] * (1 + cores),
        scratch_shapes=[
            pltpu.VMEM(rhs.shape, BF16),
            pltpu.VMEM(inv.shape, BF16),
            pltpu.VMEM(off.shape, BF16),
            pltpu.SMEM(parent_of.shape, jnp.int32),
            pltpu.VMEM((parents, width, sides), F32),
            pltpu.VMEM((parents, width, sides), F32),
            pltpu.SemaphoreType.DMA((3, count // chunk)),
            pltpu.SemaphoreType.DMA,
        ],
        compiler_params=params(room),
        name="forward",
    )(*(pltpu.with_memory_space_constraint(x, pltpu.HBM) for x in (parent_of, rhs, inv, off)))


def couple_kernel(inv, off, _, out):
    for c in range(out.shape[0]):
        out[c] = (-dot(inv[c], off[c])).astype(BF16)


def couple(inv, off, after):
    count, width, _ = inv.shape
    return pl.pallas_call(
        couple_kernel,
        out_shape=pltpu.VMEM(off.shape, BF16),
        in_specs=[VMEM, VMEM, ANY],
        out_specs=VMEM,
        compiler_params=params(16),
        cost_estimate=pl.CostEstimate(
            flops=2 * count * width**3, bytes_accessed=6 * count * width**2, transcendentals=0
        ),
        name="couple",
    )(inv, off, after)


def core_sum_kernel(*refs):
    total = refs[0][...].astype(F32)
    for part in refs[1:-2]:
        total = total + part[...].astype(F32)
    refs[-1][...] = total.astype(BF16)


def core_sum(parts, after):
    return pl.pallas_call(
        core_sum_kernel,
        out_shape=jax.ShapeDtypeStruct(parts[0].shape, BF16),
        in_specs=[VMEM] * len(parts) + [ANY],
        out_specs=VMEM,
        compiler_params=params(16),
        cost_estimate=WAIT,
        name="core_sum",
    )(*parts, after)


def prepare_kernel(rhs, lower, upper, _, whole, mine, turned):
    slab = mine.shape[1]
    rows = pl.ds(pl.multiple_of(lax.axis_index("row") * slab, slab), slab)
    for p in range(mine.shape[0]):
        whole[p] = dot(upper[p], lower[p]).astype(BF16)
        turned[...] = rhs[p].astype(F32).T
        mine[p] = turned[rows, :]


def prepare(rhs, lower, upper, after, n_row):
    per_col, width, sides = rhs.shape
    return pl.pallas_call(
        prepare_kernel,
        out_shape=[
            jax.ShapeDtypeStruct(lower.shape, BF16),
            jax.ShapeDtypeStruct((per_col, sides // n_row, width), F32),
        ],
        in_specs=[VMEM] * 3 + [ANY],
        out_specs=[VMEM, VMEM],
        scratch_shapes=[pltpu.VMEM((sides, width), F32)],
        compiler_params=params(16),
        name="prepare",
    )(rhs, lower, upper, after)


def parent_kernel(cores, whole, rhs, parts, out):
    devices, per_col, half, _ = out.shape
    for p in range(per_col):
        updates = []
        for k in range(cores):
            terms = [parts[d, p].astype(F32) for d in range(k, devices, cores)]
            while len(terms) > 1:
                pairs = zip(terms[::2], terms[1::2])
                terms = [x + y for x, y in pairs] + terms[len(terms) - len(terms) % 2 :]
            updates.append(terms[0])
        residual = (rhs[p] - jnp.concatenate(updates)).astype(BF16)
        solved = dot_t(residual, whole[p]).astype(BF16)
        for d in range(devices):
            k = d % cores
            out[d, p] = solved[k * half : (k + 1) * half]


def parent_solve(whole, rhs, parts, cores):
    return pl.pallas_call(
        functools.partial(parent_kernel, cores),
        out_shape=jax.ShapeDtypeStruct(parts.shape, BF16),
        in_specs=[VMEM] * 3,
        out_specs=VMEM,
        compiler_params=params(16),
        cost_estimate=WAIT,
        name="parent_solve",
    )(whole, rhs, parts)


def backward_kernel(cores, groups, owner, fwd, inv, coupled, *rest):
    parts, scratch = rest[:cores], rest[cores:]
    out_hbm, solved_hbm, out, picked, out_sem, solved_sem = scratch
    n_row, parents, half, _ = parts[0].shape
    per_col = solved_hbm.shape[0]
    me = lax.axis_index("core")
    for p in range(parents):
        rows = []
        for r in range(n_row):
            for n in range(cores):
                value = parts[0][r, p]
                for k in range(1, cores):
                    value = jnp.where(lax.rem(me + k, cores) == n, parts[k][r, p], value)
                rows.append(value)
        picked[p] = jnp.concatenate(rows).T
    mine = (lax.axis_index("z") * cores + me) * per_col
    solved = pltpu.make_async_copy(picked.at[pl.ds(mine, per_col)], solved_hbm, solved_sem)
    solved.start()
    stores = [solved]
    for g, (lo, hi) in enumerate(groups):
        for c in range(lo, hi):
            mats = jnp.concatenate([inv[c], coupled[c]], axis=1)
            out[c] = dot(mats, jnp.concatenate([fwd[c], picked[owner[c]]])).astype(BF16)
        part = pl.ds(lo, hi - lo)
        copy = pltpu.make_async_copy(out.at[part], out_hbm.at[part], out_sem.at[g])
        copy.start()
        stores.append(copy)
    for copy in stores:
        copy.wait()


def backward(parent_of, fwd, inv, coupled, parts, per_col):
    count, width, sides = fwd.shape
    groups = ranges(count, (1, 2, 3, 4, 5, 4, 3, 2))
    parents = parts[0].shape[1]
    return pl.pallas_call(
        functools.partial(backward_kernel, len(parts), groups),
        out_shape=[
            jax.ShapeDtypeStruct(fwd.shape, BF16),
            jax.ShapeDtypeStruct((per_col, width, sides), BF16),
        ],
        in_specs=[VMEM] * (4 + len(parts)),
        out_specs=[ANY, ANY],
        scratch_shapes=[
            pltpu.VMEM(fwd.shape, BF16),
            pltpu.VMEM((parents, width, sides), BF16),
            pltpu.SemaphoreType.DMA((len(groups),)),
            pltpu.SemaphoreType.DMA,
        ],
        compiler_params=params(32),
        name="backward",
    )(parent_of, fwd, inv, coupled, *parts)


def from_core(value, k):
    cores = lax.axis_size("core")
    return lax.ppermute(value, "core", [(i, (i + k) % cores) for i in range(cores)])


def on_device(
    child_rhs,
    parent_rhs,
    child_lower_inv,
    child_lower_off,
    child_upper_inv,
    child_upper_off,
    parent_lower_inv,
    parent_upper_inv,
    parent_of,
):
    n_row, n_chip, cores = (lax.axis_size(a) for a in ("row", "z", "core"))
    per_col = parent_rhs.shape[0]
    fwd, mine, *theirs = forward(
        parent_of, child_rhs, child_lower_inv, child_lower_off, n_row, n_chip, cores, per_col
    )
    theirs = [from_core(x, k) for k, x in enumerate(theirs, 1)]
    whole, rhs = prepare(parent_rhs, parent_lower_inv, parent_upper_inv, mine, n_row)
    total = core_sum([mine] + theirs, whole)
    axes = ("row", "z", "core")
    sent = total.reshape(-1, per_col, *total.shape[2:])
    rows = lax.all_to_all(sent.reshape(-1, sent.shape[-1]), axes, 0, 0, tiled=True)
    parts = rows.reshape(sent.shape)
    solved = parent_solve(whole, rhs, parts, cores)
    rows = lax.all_to_all(solved.reshape(rows.shape), axes, 0, 0, tiled=True)
    mine = rows.reshape(total.shape)
    parts = [mine] + [from_core(mine, cores - k) for k in range(1, cores)]
    coupled = couple(child_upper_inv, child_upper_off, mine)
    return tuple(backward(parent_of, fwd, child_upper_inv, coupled, parts, per_col))


def solution(mesh):
    n_row, n_col = (mesh.shape[a] for a in ("row", "col"))
    cores = 1 if n_col % 2 else 2
    split = Mesh(mesh.devices.reshape(n_row, n_col // cores, cores), ("row", "z", "core"))
    child = P(("row", "z", "core"), None, None)
    parent = P(("z", "core"), None, None)
    return jax.shard_map(
        on_device,
        mesh=split,
        in_specs=(child, parent, child, child, child, child, parent, parent, P(("row", "z", "core"))),
        out_specs=(child, parent),
        check_vma=False,
    )
```

```python
import functools
import math
import jax
import jax.numpy as jnp
from jax import lax
from jax.experimental import pallas as pl
from jax.experimental.pallas import tpu as pltpu
from jax.sharding import Mesh, PartitionSpec as P

F32 = jnp.float32
BF16 = jnp.bfloat16
VMEM = pl.BlockSpec(memory_space=pltpu.VMEM)
ANY = pl.BlockSpec(memory_space=pl.ANY)
MIB = 1 << 20
VMEM_BYTES = 64 * MIB
WAIT = pl.CostEstimate(flops=8 * 10**9, bytes_accessed=MIB, transcendentals=0)


def ranges(count, shares):
    ends = [count * sum(shares[: i + 1]) // sum(shares) for i in range(len(shares))]
    pairs = zip([0] + ends[:-1], ends)
    return [(lo, hi) for lo, hi in pairs if hi > lo]


def params(mib):
    return pltpu.CompilerParams(vmem_limit_bytes=mib * MIB)


def dot(a, b):
    return jnp.dot(a, b, preferred_element_type=F32)


def dot_t(a, b):
    return lax.dot_general(a, b, (((1,), (1,)), ((), ())), preferred_element_type=F32)


def identity(n):
    rows = lax.broadcasted_iota(jnp.int32, (n, n), 0)
    return (rows == lax.broadcasted_iota(jnp.int32, (n, n), 1)).astype(F32).astype(BF16)


def forward_kernel(cores, chunk, owner_hbm, rhs_hbm, inv_hbm, off_hbm, fwd, *rest):
    mine, theirs, scratch = rest[0], rest[1:cores], rest[cores:]
    rhs, inv, off, owner, even, odd, in_sem, owner_sem = scratch
    n_row, _, half, _ = mine.shape
    groups = fwd.shape[0] // chunk
    arrays = ((rhs_hbm, rhs), (inv_hbm, inv), (off_hbm, off))

    def loads(g):
        part = pl.ds(g * chunk, chunk)
        return [
            pltpu.make_async_copy(h.at[part], v.at[part], in_sem.at[s, g])
            for s, (h, v) in enumerate(arrays)
        ]

    names = pltpu.make_async_copy(owner_hbm, owner, owner_sem)
    names.start()

    @pl.loop(0, groups)
    def _(g):
        for copy in loads(g):
            copy.start()

    one = identity(even.shape[2])
    even[...] = jnp.zeros_like(even)
    odd[...] = jnp.zeros_like(odd)

    def solve(c):
        fwd[c] = dot(inv[c], rhs[c]).astype(BF16)

    def add(c, acc):
        acc[owner[c]] += dot(off[c], fwd[c])

    for copy in loads(0):
        copy.wait()
    for n in range(chunk):
        solve(n)
    names.wait()

    def step(g):
        for copy in loads(g):
            copy.wait()
        for n in range(chunk):
            solve(g * chunk + n)
            add((g - 1) * chunk + n, odd if n % 2 else even)

    pl.loop(1, groups - 1)(step)
    if groups > 1:
        step(groups - 1)
    for n in range(chunk):
        add((groups - 1) * chunk + n, odd if n % 2 else even)
    me = lax.axis_index("core")
    for p in range(even.shape[0]):
        turned = dot_t(one, (even[p] + odd[p]).astype(BF16)).astype(BF16)
        for r in range(n_row):
            halves = [turned[n * half : (n + 1) * half] for n in range(r * cores, (r + 1) * cores)]
            for k in range(cores):
                out = theirs[k - 1] if k else mine
                value = halves[0]
                for n in range(1, cores):
                    value = jnp.where(lax.rem(me + k, cores) == n, halves[n], value)
                out[r, p] = value


def forward(parent_of, rhs, inv, off, n_row, n_chip, cores, per_col):
    count, width, sides = rhs.shape
    chunk = max(c for c in range(1, 13) if count % c == 0)
    parents = n_chip * cores * per_col
    piece = (n_row, parents, sides // (n_row * cores), width)
    kept = 2 * rhs.size + 2 * cores * math.prod(piece)
    room = (VMEM_BYTES - kept - MIB) // MIB
    return pl.pallas_call(
        functools.partial(forward_kernel, cores, chunk),
        out_shape=[pltpu.VMEM(rhs.shape, BF16)] + [pltpu.VMEM(piece, BF16)] * cores,
        in_specs=[ANY] * 4,
        out_specs=[VMEM] * (1 + cores),
        scratch_shapes=[
            pltpu.VMEM(rhs.shape, BF16),
            pltpu.VMEM(inv.shape, BF16),
            pltpu.VMEM(off.shape, BF16),
            pltpu.SMEM(parent_of.shape, jnp.int32),
            pltpu.VMEM((parents, width, sides), F32),
            pltpu.VMEM((parents, width, sides), F32),
            pltpu.SemaphoreType.DMA((3, count // chunk)),
            pltpu.SemaphoreType.DMA,
        ],
        compiler_params=params(room),
        name="forward",
    )(*(pltpu.with_memory_space_constraint(x, pltpu.HBM) for x in (parent_of, rhs, inv, off)))


def couple_kernel(inv, off, _, out):
    for c in range(out.shape[0]):
        out[c] = (-dot(inv[c], off[c])).astype(BF16)


def couple(inv, off, after):
    count, width, _ = inv.shape
    return pl.pallas_call(
        couple_kernel,
        out_shape=pltpu.VMEM(off.shape, BF16),
        in_specs=[VMEM, VMEM, ANY],
        out_specs=VMEM,
        compiler_params=params(16),
        cost_estimate=pl.CostEstimate(
            flops=2 * count * width**3, bytes_accessed=6 * count * width**2, transcendentals=0
        ),
        name="couple",
    )(inv, off, after)


def core_sum_kernel(*refs):
    total = refs[0][...].astype(F32)
    for part in refs[1:-2]:
        total = total + part[...].astype(F32)
    refs[-1][...] = total.astype(BF16)


def core_sum(parts, after):
    return pl.pallas_call(
        core_sum_kernel,
        out_shape=jax.ShapeDtypeStruct(parts[0].shape, BF16),
        in_specs=[VMEM] * len(parts) + [ANY],
        out_specs=VMEM,
        compiler_params=params(16),
        cost_estimate=WAIT,
        name="core_sum",
    )(*parts, after)


def prepare_kernel(rhs, lower, upper, _, whole, mine, turned):
    slab = mine.shape[1]
    rows = pl.ds(pl.multiple_of(lax.axis_index("row") * slab, slab), slab)
    for p in range(mine.shape[0]):
        whole[p] = dot(upper[p], lower[p]).astype(BF16)
        turned[...] = rhs[p].astype(F32).T
        mine[p] = turned[rows, :]


def prepare(rhs, lower, upper, after, n_row):
    per_col, width, sides = rhs.shape
    return pl.pallas_call(
        prepare_kernel,
        out_shape=[
            jax.ShapeDtypeStruct(lower.shape, BF16),
            jax.ShapeDtypeStruct((per_col, sides // n_row, width), F32),
        ],
        in_specs=[VMEM] * 3 + [ANY],
        out_specs=[VMEM, VMEM],
        scratch_shapes=[pltpu.VMEM((sides, width), F32)],
        compiler_params=params(16),
        name="prepare",
    )(rhs, lower, upper, after)


def parent_kernel(cores, whole, rhs, parts, out):
    devices, per_col, half, _ = out.shape
    for p in range(per_col):
        updates = []
        for k in range(cores):
            terms = [parts[d, p].astype(F32) for d in range(k, devices, cores)]
            while len(terms) > 1:
                pairs = zip(terms[::2], terms[1::2])
                terms = [x + y for x, y in pairs] + terms[len(terms) - len(terms) % 2 :]
            updates.append(terms[0])
        residual = (rhs[p] - jnp.concatenate(updates)).astype(BF16)
        solved = dot_t(residual, whole[p]).astype(BF16)
        for d in range(devices):
            k = d % cores
            out[d, p] = solved[k * half : (k + 1) * half]


def parent_solve(whole, rhs, parts, cores):
    return pl.pallas_call(
        functools.partial(parent_kernel, cores),
        out_shape=jax.ShapeDtypeStruct(parts.shape, BF16),
        in_specs=[VMEM] * 3,
        out_specs=VMEM,
        compiler_params=params(16),
        cost_estimate=WAIT,
        name="parent_solve",
    )(whole, rhs, parts)


def backward_kernel(cores, groups, owner, fwd, inv, coupled, *rest):
    parts, scratch = rest[:cores], rest[cores:]
    out_hbm, solved_hbm, out, picked, out_sem, solved_sem = scratch
    n_row, parents, half, _ = parts[0].shape
    per_col = solved_hbm.shape[0]
    me = lax.axis_index("core")
    one = identity(picked.shape[1])
    for p in range(parents):
        rows = []
        for r in range(n_row):
            for n in range(cores):
                value = parts[0][r, p]
                for k in range(1, cores):
                    value = jnp.where(lax.rem(me + k, cores) == n, parts[k][r, p], value)
                rows.append(value)
        picked[p] = dot_t(one, jnp.concatenate(rows)).astype(BF16)
    mine = (lax.axis_index("z") * cores + me) * per_col
    solved = pltpu.make_async_copy(picked.at[pl.ds(mine, per_col)], solved_hbm, solved_sem)
    solved.start()
    stores = [solved]
    for g, (lo, hi) in enumerate(groups):
        for c in range(lo, hi):
            mats = jnp.concatenate([inv[c], coupled[c]], axis=1)
            out[c] = dot(mats, jnp.concatenate([fwd[c], picked[owner[c]]])).astype(BF16)
        part = pl.ds(lo, hi - lo)
        copy = pltpu.make_async_copy(out.at[part], out_hbm.at[part], out_sem.at[g])
        copy.start()
        stores.append(copy)
    for copy in stores:
        copy.wait()


def backward(parent_of, fwd, inv, coupled, parts, per_col):
    count, width, sides = fwd.shape
    groups = ranges(count, (1, 2, 3, 4, 5, 4, 3, 2))
    parents = parts[0].shape[1]
    return pl.pallas_call(
        functools.partial(backward_kernel, len(parts), groups),
        out_shape=[
            jax.ShapeDtypeStruct(fwd.shape, BF16),
            jax.ShapeDtypeStruct((per_col, width, sides), BF16),
        ],
        in_specs=[VMEM] * (4 + len(parts)),
        out_specs=[ANY, ANY],
        scratch_shapes=[
            pltpu.VMEM(fwd.shape, BF16),
            pltpu.VMEM((parents, width, sides), BF16),
            pltpu.SemaphoreType.DMA((len(groups),)),
            pltpu.SemaphoreType.DMA,
        ],
        compiler_params=params(32),
        name="backward",
    )(parent_of, fwd, inv, coupled, *parts)


def from_core(value, k):
    cores = lax.axis_size("core")
    return lax.ppermute(value, "core", [(i, (i + k) % cores) for i in range(cores)])


def on_device(
    child_rhs,
    parent_rhs,
    child_lower_inv,
    child_lower_off,
    child_upper_inv,
    child_upper_off,
    parent_lower_inv,
    parent_upper_inv,
    parent_of,
):
    n_row, n_chip, cores = (lax.axis_size(a) for a in ("row", "z", "core"))
    per_col = parent_rhs.shape[0]
    fwd, mine, *theirs = forward(
        parent_of, child_rhs, child_lower_inv, child_lower_off, n_row, n_chip, cores, per_col
    )
    theirs = [from_core(x, k) for k, x in enumerate(theirs, 1)]
    whole, rhs = prepare(parent_rhs, parent_lower_inv, parent_upper_inv, mine, n_row)
    total = core_sum([mine] + theirs, whole)
    axes = ("row", "z", "core")
    sent = total.reshape(-1, per_col, *total.shape[2:])
    parts = lax.all_to_all(sent, axes, 0, 0, tiled=True)
    solved = parent_solve(whole, rhs, parts, cores)
    mine = lax.all_to_all(solved, axes, 0, 0, tiled=True).reshape(total.shape)
    parts = [mine] + [from_core(mine, cores - k) for k in range(1, cores)]
    coupled = couple(child_upper_inv, child_upper_off, mine)
    return tuple(backward(parent_of, fwd, child_upper_inv, coupled, parts, per_col))


def solution(mesh):
    n_row, n_col = (mesh.shape[a] for a in ("row", "col"))
    cores = 1 if n_col % 2 else 2
    split = Mesh(mesh.devices.reshape(n_row, n_col // cores, cores), ("row", "z", "core"))
    child = P(("row", "z", "core"), None, None)
    parent = P(("z", "core"), None, None)
    return jax.shard_map(
        on_device,
        mesh=split,
        in_specs=(child, parent, child, child, child, child, parent, parent, P(("row", "z", "core"))),
        out_specs=(child, parent),
        check_vma=False,
    )
```

```python
import functools
import math
import jax
import jax.numpy as jnp
from jax import lax
from jax.experimental import pallas as pl
from jax.experimental.pallas import tpu as pltpu
from jax.sharding import Mesh, PartitionSpec as P

F32 = jnp.float32
BF16 = jnp.bfloat16
VMEM = pl.BlockSpec(memory_space=pltpu.VMEM)
ANY = pl.BlockSpec(memory_space=pl.ANY)
MIB = 1 << 20
VMEM_BYTES = 64 * MIB
WAIT = pl.CostEstimate(flops=8 * 10**9, bytes_accessed=MIB, transcendentals=0)


def ranges(count, shares):
    ends = [count * sum(shares[: i + 1]) // sum(shares) for i in range(len(shares))]
    pairs = zip([0] + ends[:-1], ends)
    return [(lo, hi) for lo, hi in pairs if hi > lo]


def params(mib):
    return pltpu.CompilerParams(vmem_limit_bytes=mib * MIB)


def dot(a, b):
    return jnp.dot(a, b, preferred_element_type=F32)


def dot_t(a, b):
    return lax.dot_general(a, b, (((1,), (1,)), ((), ())), preferred_element_type=F32)


def forward_kernel(cores, chunk, owner_hbm, rhs_hbm, inv_hbm, off_hbm, fwd, *rest):
    mine, theirs, scratch = rest[0], rest[1:cores], rest[cores:]
    rhs, inv, off, owner, even, odd, in_sem, owner_sem = scratch
    n_row, _, half, _ = mine.shape
    groups = fwd.shape[0] // chunk
    arrays = ((rhs_hbm, rhs), (inv_hbm, inv), (off_hbm, off))

    def load(s, g):
        part = pl.ds(g * chunk, chunk)
        return pltpu.make_async_copy(arrays[s][0].at[part], arrays[s][1].at[part], in_sem.at[s, g])

    load(0, 0).start()
    load(1, 0).start()
    names = pltpu.make_async_copy(owner_hbm, owner, owner_sem)
    names.start()

    @pl.loop(1, groups)
    def _(g):
        load(0, g).start()
        load(1, g).start()
        load(2, g - 1).start()

    load(2, groups - 1).start()
    even[...] = jnp.zeros_like(even)
    odd[...] = jnp.zeros_like(odd)

    def solve(c):
        fwd[c] = dot(inv[c], rhs[c]).astype(BF16)

    def add(c, acc):
        acc[owner[c]] += dot(off[c], fwd[c])

    load(0, 0).wait()
    load(1, 0).wait()
    for n in range(chunk):
        solve(n)
    names.wait()

    def step(g):
        load(0, g).wait()
        load(1, g).wait()
        load(2, g - 1).wait()
        for n in range(chunk):
            solve(g * chunk + n)
            add((g - 1) * chunk + n, odd if n % 2 else even)

    pl.loop(1, groups - 1)(step)
    if groups > 1:
        step(groups - 1)
    load(2, groups - 1).wait()
    for n in range(chunk):
        add((groups - 1) * chunk + n, odd if n % 2 else even)
    me = lax.axis_index("core")
    for p in range(even.shape[0]):
        turned = (even[p] + odd[p]).astype(BF16).T
        for r in range(n_row):
            halves = [turned[n * half : (n + 1) * half] for n in range(r * cores, (r + 1) * cores)]
            for k in range(cores):
                out = theirs[k - 1] if k else mine
                value = halves[0]
                for n in range(1, cores):
                    value = jnp.where(lax.rem(me + k, cores) == n, halves[n], value)
                out[r, p] = value


def forward(parent_of, rhs, inv, off, n_row, n_chip, cores, per_col):
    count, width, sides = rhs.shape
    chunk = max(c for c in range(1, 13) if count % c == 0)
    parents = n_chip * cores * per_col
    piece = (n_row, parents, sides // (n_row * cores), width)
    kept = 2 * rhs.size + 2 * cores * math.prod(piece)
    room = (VMEM_BYTES - kept - MIB) // MIB
    return pl.pallas_call(
        functools.partial(forward_kernel, cores, chunk),
        out_shape=[pltpu.VMEM(rhs.shape, BF16)] + [pltpu.VMEM(piece, BF16)] * cores,
        in_specs=[ANY] * 4,
        out_specs=[VMEM] * (1 + cores),
        scratch_shapes=[
            pltpu.VMEM(rhs.shape, BF16),
            pltpu.VMEM(inv.shape, BF16),
            pltpu.VMEM(off.shape, BF16),
            pltpu.SMEM(parent_of.shape, jnp.int32),
            pltpu.VMEM((parents, width, sides), F32),
            pltpu.VMEM((parents, width, sides), F32),
            pltpu.SemaphoreType.DMA((3, count // chunk)),
            pltpu.SemaphoreType.DMA,
        ],
        compiler_params=params(room),
        name="forward",
    )(*(pltpu.with_memory_space_constraint(x, pltpu.HBM) for x in (parent_of, rhs, inv, off)))


def couple_kernel(inv, off, _, out):
    for c in range(out.shape[0]):
        out[c] = (-dot(inv[c], off[c])).astype(BF16)


def couple(inv, off, after):
    count, width, _ = inv.shape
    return pl.pallas_call(
        couple_kernel,
        out_shape=pltpu.VMEM(off.shape, BF16),
        in_specs=[VMEM, VMEM, ANY],
        out_specs=VMEM,
        compiler_params=params(16),
        cost_estimate=pl.CostEstimate(
            flops=2 * count * width**3, bytes_accessed=6 * count * width**2, transcendentals=0
        ),
        name="couple",
    )(inv, off, after)


def core_sum_kernel(*refs):
    total = refs[0][...].astype(F32)
    for part in refs[1:-2]:
        total = total + part[...].astype(F32)
    refs[-1][...] = total.astype(BF16)


def core_sum(parts, after):
    return pl.pallas_call(
        core_sum_kernel,
        out_shape=jax.ShapeDtypeStruct(parts[0].shape, BF16),
        in_specs=[VMEM] * len(parts) + [ANY],
        out_specs=VMEM,
        compiler_params=params(16),
        cost_estimate=WAIT,
        name="core_sum",
    )(*parts, after)


def prepare_kernel(rhs, lower, upper, _, whole, mine, turned):
    slab = mine.shape[1]
    rows = pl.ds(pl.multiple_of(lax.axis_index("row") * slab, slab), slab)
    for p in range(mine.shape[0]):
        whole[p] = dot(upper[p], lower[p]).astype(BF16)
        turned[...] = rhs[p].astype(F32).T
        mine[p] = turned[rows, :]


def prepare(rhs, lower, upper, after, n_row):
    per_col, width, sides = rhs.shape
    return pl.pallas_call(
        prepare_kernel,
        out_shape=[
            jax.ShapeDtypeStruct(lower.shape, BF16),
            jax.ShapeDtypeStruct((per_col, sides // n_row, width), F32),
        ],
        in_specs=[VMEM] * 3 + [ANY],
        out_specs=[VMEM, VMEM],
        scratch_shapes=[pltpu.VMEM((sides, width), F32)],
        compiler_params=params(16),
        name="prepare",
    )(rhs, lower, upper, after)


def parent_kernel(cores, whole, rhs, parts, out):
    devices, per_col, half, _ = out.shape
    for p in range(per_col):
        updates = []
        for k in range(cores):
            terms = [parts[d, p].astype(F32) for d in range(k, devices, cores)]
            while len(terms) > 1:
                pairs = zip(terms[::2], terms[1::2])
                terms = [x + y for x, y in pairs] + terms[len(terms) - len(terms) % 2 :]
            updates.append(terms[0])
        residual = (rhs[p] - jnp.concatenate(updates)).astype(BF16)
        solved = dot_t(residual, whole[p]).astype(BF16)
        for d in range(devices):
            k = d % cores
            out[d, p] = solved[k * half : (k + 1) * half]


def parent_solve(whole, rhs, parts, cores):
    return pl.pallas_call(
        functools.partial(parent_kernel, cores),
        out_shape=jax.ShapeDtypeStruct(parts.shape, BF16),
        in_specs=[VMEM] * 3,
        out_specs=VMEM,
        compiler_params=params(16),
        cost_estimate=WAIT,
        name="parent_solve",
    )(whole, rhs, parts)


def backward_kernel(cores, groups, owner, fwd, inv, coupled, *rest):
    parts, scratch = rest[:cores], rest[cores:]
    out_hbm, solved_hbm, out, picked, out_sem, solved_sem = scratch
    n_row, parents, half, _ = parts[0].shape
    per_col = solved_hbm.shape[0]
    me = lax.axis_index("core")
    for p in range(parents):
        rows = []
        for r in range(n_row):
            for n in range(cores):
                value = parts[0][r, p]
                for k in range(1, cores):
                    value = jnp.where(lax.rem(me + k, cores) == n, parts[k][r, p], value)
                rows.append(value)
        picked[p] = jnp.concatenate(rows).T
    mine = (lax.axis_index("z") * cores + me) * per_col
    solved = pltpu.make_async_copy(picked.at[pl.ds(mine, per_col)], solved_hbm, solved_sem)
    solved.start()
    stores = [solved]
    for g, (lo, hi) in enumerate(groups):
        for c in range(lo, hi):
            mats = jnp.concatenate([inv[c], coupled[c]], axis=1)
            out[c] = dot(mats, jnp.concatenate([fwd[c], picked[owner[c]]])).astype(BF16)
        part = pl.ds(lo, hi - lo)
        copy = pltpu.make_async_copy(out.at[part], out_hbm.at[part], out_sem.at[g])
        copy.start()
        stores.append(copy)
    for copy in stores:
        copy.wait()


def backward(parent_of, fwd, inv, coupled, parts, per_col):
    count, width, sides = fwd.shape
    groups = ranges(count, (1, 2, 3, 4, 5, 4, 3, 2))
    parents = parts[0].shape[1]
    return pl.pallas_call(
        functools.partial(backward_kernel, len(parts), groups),
        out_shape=[
            jax.ShapeDtypeStruct(fwd.shape, BF16),
            jax.ShapeDtypeStruct((per_col, width, sides), BF16),
        ],
        in_specs=[VMEM] * (4 + len(parts)),
        out_specs=[ANY, ANY],
        scratch_shapes=[
            pltpu.VMEM(fwd.shape, BF16),
            pltpu.VMEM((parents, width, sides), BF16),
            pltpu.SemaphoreType.DMA((len(groups),)),
            pltpu.SemaphoreType.DMA,
        ],
        compiler_params=params(32),
        name="backward",
    )(parent_of, fwd, inv, coupled, *parts)


def from_core(value, k):
    cores = lax.axis_size("core")
    return lax.ppermute(value, "core", [(i, (i + k) % cores) for i in range(cores)])


def on_device(
    child_rhs,
    parent_rhs,
    child_lower_inv,
    child_lower_off,
    child_upper_inv,
    child_upper_off,
    parent_lower_inv,
    parent_upper_inv,
    parent_of,
):
    n_row, n_chip, cores = (lax.axis_size(a) for a in ("row", "z", "core"))
    per_col = parent_rhs.shape[0]
    fwd, mine, *theirs = forward(
        parent_of, child_rhs, child_lower_inv, child_lower_off, n_row, n_chip, cores, per_col
    )
    theirs = [from_core(x, k) for k, x in enumerate(theirs, 1)]
    whole, rhs = prepare(parent_rhs, parent_lower_inv, parent_upper_inv, mine, n_row)
    total = core_sum([mine] + theirs, whole)
    axes = ("row", "z", "core")
    sent = total.reshape(-1, per_col, *total.shape[2:])
    parts = lax.all_to_all(sent, axes, 0, 0, tiled=True)
    solved = parent_solve(whole, rhs, parts, cores)
    mine = lax.all_to_all(solved, axes, 0, 0, tiled=True).reshape(total.shape)
    parts = [mine] + [from_core(mine, cores - k) for k in range(1, cores)]
    coupled = couple(child_upper_inv, child_upper_off, mine)
    return tuple(backward(parent_of, fwd, child_upper_inv, coupled, parts, per_col))


def solution(mesh):
    n_row, n_col = (mesh.shape[a] for a in ("row", "col"))
    cores = 1 if n_col % 2 else 2
    split = Mesh(mesh.devices.reshape(n_row, n_col // cores, cores), ("row", "z", "core"))
    child = P(("row", "z", "core"), None, None)
    parent = P(("z", "core"), None, None)
    return jax.shard_map(
        on_device,
        mesh=split,
        in_specs=(child, parent, child, child, child, child, parent, parent, P(("row", "z", "core"))),
        out_specs=(child, parent),
        check_vma=False,
    )
```

```python
import functools
import math
import jax
import jax.numpy as jnp
from jax import lax
from jax.experimental import pallas as pl
from jax.experimental.pallas import tpu as pltpu
from jax.sharding import Mesh, PartitionSpec as P

F32 = jnp.float32
BF16 = jnp.bfloat16
VMEM = pl.BlockSpec(memory_space=pltpu.VMEM)
ANY = pl.BlockSpec(memory_space=pl.ANY)
MIB = 1 << 20
VMEM_BYTES = 64 * MIB
WAIT = pl.CostEstimate(flops=8 * 10**9, bytes_accessed=MIB, transcendentals=0)


def ranges(count, shares):
    ends = [count * sum(shares[: i + 1]) // sum(shares) for i in range(len(shares))]
    pairs = zip([0] + ends[:-1], ends)
    return [(lo, hi) for lo, hi in pairs if hi > lo]


def params(mib):
    return pltpu.CompilerParams(vmem_limit_bytes=mib * MIB)


def dot(a, b):
    return jnp.dot(a, b, preferred_element_type=F32)


def dot_t(a, b):
    return lax.dot_general(a, b, (((1,), (1,)), ((), ())), preferred_element_type=F32)


def forward_kernel(cores, chunk, owner_hbm, rhs_hbm, inv_hbm, off_hbm, fwd, *rest):
    mine, theirs, scratch = rest[0], rest[1:cores], rest[cores:]
    rhs, inv, off, owner, even, odd, in_sem, owner_sem = scratch
    n_row, _, half, _ = mine.shape
    groups = fwd.shape[0] // chunk
    arrays = ((rhs_hbm, rhs), (inv_hbm, inv), (off_hbm, off))

    def load(s, g):
        part = pl.ds(g * chunk, chunk)
        return pltpu.make_async_copy(arrays[s][0].at[part], arrays[s][1].at[part], in_sem.at[s, g])

    load(0, 0).start()
    load(1, 0).start()
    names = pltpu.make_async_copy(owner_hbm, owner, owner_sem)
    names.start()

    @pl.loop(1, groups)
    def _(g):
        load(0, g).start()
        load(1, g).start()
        load(2, g - 1).start()

    load(2, groups - 1).start()
    even[...] = jnp.zeros_like(even)
    odd[...] = jnp.zeros_like(odd)

    def solve(c):
        fwd[c] = dot(inv[c], rhs[c]).astype(BF16)

    def add(c, acc):
        acc[owner[c]] += dot(off[c], fwd[c])

    load(0, 0).wait()
    load(1, 0).wait()
    for n in range(chunk):
        solve(n)
    names.wait()

    def step(g):
        load(0, g).wait()
        load(1, g).wait()
        load(2, g - 1).wait()
        for n in range(chunk):
            solve(g * chunk + n)
            add((g - 1) * chunk + n, odd if n % 2 else even)

    pl.loop(1, groups - 1)(step)
    if groups > 1:
        step(groups - 1)
    load(2, groups - 1).wait()
    for n in range(chunk):
        add((groups - 1) * chunk + n, odd if n % 2 else even)
    me = lax.axis_index("core")
    for p in range(even.shape[0]):
        turned = (even[p] + odd[p]).astype(BF16).T
        for r in range(n_row):
            halves = [turned[n * half : (n + 1) * half] for n in range(r * cores, (r + 1) * cores)]
            for k in range(cores):
                out = theirs[k - 1] if k else mine
                value = halves[0]
                for n in range(1, cores):
                    value = jnp.where(lax.rem(me + k, cores) == n, halves[n], value)
                out[r, p] = value


def forward(parent_of, rhs, inv, off, n_row, n_chip, cores, per_col):
    count, width, sides = rhs.shape
    chunk = max(c for c in range(1, 17) if count % c == 0)
    parents = n_chip * cores * per_col
    piece = (n_row, parents, sides // (n_row * cores), width)
    kept = 2 * rhs.size + 2 * cores * math.prod(piece)
    room = (VMEM_BYTES - kept - MIB) // MIB
    return pl.pallas_call(
        functools.partial(forward_kernel, cores, chunk),
        out_shape=[pltpu.VMEM(rhs.shape, BF16)] + [pltpu.VMEM(piece, BF16)] * cores,
        in_specs=[ANY] * 4,
        out_specs=[VMEM] * (1 + cores),
        scratch_shapes=[
            pltpu.VMEM(rhs.shape, BF16),
            pltpu.VMEM(inv.shape, BF16),
            pltpu.VMEM(off.shape, BF16),
            pltpu.SMEM(parent_of.shape, jnp.int32),
            pltpu.VMEM((parents, width, sides), F32),
            pltpu.VMEM((parents, width, sides), F32),
            pltpu.SemaphoreType.DMA((3, count // chunk)),
            pltpu.SemaphoreType.DMA,
        ],
        compiler_params=params(room),
        name="forward",
    )(*(pltpu.with_memory_space_constraint(x, pltpu.HBM) for x in (parent_of, rhs, inv, off)))


def couple_kernel(inv, off, _, out):
    for c in range(out.shape[0]):
        out[c] = (-dot(inv[c], off[c])).astype(BF16)


def couple(inv, off, after):
    count, width, _ = inv.shape
    return pl.pallas_call(
        couple_kernel,
        out_shape=pltpu.VMEM(off.shape, BF16),
        in_specs=[VMEM, VMEM, ANY],
        out_specs=VMEM,
        compiler_params=params(16),
        cost_estimate=pl.CostEstimate(
            flops=2 * count * width**3, bytes_accessed=6 * count * width**2, transcendentals=0
        ),
        name="couple",
    )(inv, off, after)


def core_sum_kernel(*refs):
    total = refs[0][...].astype(F32)
    for part in refs[1:-2]:
        total = total + part[...].astype(F32)
    refs[-1][...] = total.astype(BF16)


def core_sum(parts, after):
    return pl.pallas_call(
        core_sum_kernel,
        out_shape=jax.ShapeDtypeStruct(parts[0].shape, BF16),
        in_specs=[VMEM] * len(parts) + [ANY],
        out_specs=VMEM,
        compiler_params=params(16),
        cost_estimate=WAIT,
        name="core_sum",
    )(*parts, after)


def prepare_kernel(rhs, lower, upper, _, whole, mine, turned):
    slab = mine.shape[1]
    rows = pl.ds(pl.multiple_of(lax.axis_index("row") * slab, slab), slab)
    for p in range(mine.shape[0]):
        whole[p] = dot(upper[p], lower[p]).astype(BF16)
        turned[...] = rhs[p].astype(F32).T
        mine[p] = turned[rows, :]


def prepare(rhs, lower, upper, after, n_row):
    per_col, width, sides = rhs.shape
    return pl.pallas_call(
        prepare_kernel,
        out_shape=[
            jax.ShapeDtypeStruct(lower.shape, BF16),
            jax.ShapeDtypeStruct((per_col, sides // n_row, width), F32),
        ],
        in_specs=[VMEM] * 3 + [ANY],
        out_specs=[VMEM, VMEM],
        scratch_shapes=[pltpu.VMEM((sides, width), F32)],
        compiler_params=params(16),
        name="prepare",
    )(rhs, lower, upper, after)


def parent_kernel(cores, whole, rhs, parts, out):
    devices, per_col, half, _ = out.shape
    for p in range(per_col):
        updates = []
        for k in range(cores):
            terms = [parts[d, p].astype(F32) for d in range(k, devices, cores)]
            while len(terms) > 1:
                pairs = zip(terms[::2], terms[1::2])
                terms = [x + y for x, y in pairs] + terms[len(terms) - len(terms) % 2 :]
            updates.append(terms[0])
        residual = (rhs[p] - jnp.concatenate(updates)).astype(BF16)
        solved = dot_t(residual, whole[p]).astype(BF16)
        for d in range(devices):
            k = d % cores
            out[d, p] = solved[k * half : (k + 1) * half]


def parent_solve(whole, rhs, parts, cores):
    return pl.pallas_call(
        functools.partial(parent_kernel, cores),
        out_shape=jax.ShapeDtypeStruct(parts.shape, BF16),
        in_specs=[VMEM] * 3,
        out_specs=VMEM,
        compiler_params=params(16),
        cost_estimate=WAIT,
        name="parent_solve",
    )(whole, rhs, parts)


def backward_kernel(cores, groups, owner, fwd, inv, coupled, *rest):
    parts, scratch = rest[:cores], rest[cores:]
    out_hbm, solved_hbm, out, picked, out_sem, solved_sem = scratch
    n_row, parents, half, _ = parts[0].shape
    per_col = solved_hbm.shape[0]
    me = lax.axis_index("core")
    for p in range(parents):
        rows = []
        for r in range(n_row):
            for n in range(cores):
                value = parts[0][r, p]
                for k in range(1, cores):
                    value = jnp.where(lax.rem(me + k, cores) == n, parts[k][r, p], value)
                rows.append(value)
        picked[p] = jnp.concatenate(rows).T
    mine = (lax.axis_index("z") * cores + me) * per_col
    solved = pltpu.make_async_copy(picked.at[pl.ds(mine, per_col)], solved_hbm, solved_sem)
    solved.start()
    stores = [solved]
    for g, (lo, hi) in enumerate(groups):
        for c in range(lo, hi):
            mats = jnp.concatenate([inv[c], coupled[c]], axis=1)
            out[c] = dot(mats, jnp.concatenate([fwd[c], picked[owner[c]]])).astype(BF16)
        part = pl.ds(lo, hi - lo)
        copy = pltpu.make_async_copy(out.at[part], out_hbm.at[part], out_sem.at[g])
        copy.start()
        stores.append(copy)
    for copy in stores:
        copy.wait()


def backward(parent_of, fwd, inv, coupled, parts, per_col):
    count, width, sides = fwd.shape
    groups = ranges(count, (1, 2, 3, 4, 5, 4, 3, 2))
    parents = parts[0].shape[1]
    return pl.pallas_call(
        functools.partial(backward_kernel, len(parts), groups),
        out_shape=[
            jax.ShapeDtypeStruct(fwd.shape, BF16),
            jax.ShapeDtypeStruct((per_col, width, sides), BF16),
        ],
        in_specs=[VMEM] * (4 + len(parts)),
        out_specs=[ANY, ANY],
        scratch_shapes=[
            pltpu.VMEM(fwd.shape, BF16),
            pltpu.VMEM((parents, width, sides), BF16),
            pltpu.SemaphoreType.DMA((len(groups),)),
            pltpu.SemaphoreType.DMA,
        ],
        compiler_params=params(32),
        name="backward",
    )(parent_of, fwd, inv, coupled, *parts)


def from_core(value, k):
    cores = lax.axis_size("core")
    return lax.ppermute(value, "core", [(i, (i + k) % cores) for i in range(cores)])


def on_device(
    child_rhs,
    parent_rhs,
    child_lower_inv,
    child_lower_off,
    child_upper_inv,
    child_upper_off,
    parent_lower_inv,
    parent_upper_inv,
    parent_of,
):
    n_row, n_chip, cores = (lax.axis_size(a) for a in ("row", "z", "core"))
    per_col = parent_rhs.shape[0]
    fwd, mine, *theirs = forward(
        parent_of, child_rhs, child_lower_inv, child_lower_off, n_row, n_chip, cores, per_col
    )
    theirs = [from_core(x, k) for k, x in enumerate(theirs, 1)]
    whole, rhs = prepare(parent_rhs, parent_lower_inv, parent_upper_inv, mine, n_row)
    total = core_sum([mine] + theirs, whole)
    axes = ("row", "z", "core")
    sent = total.reshape(-1, per_col, *total.shape[2:])
    parts = lax.all_to_all(sent, axes, 0, 0, tiled=True)
    solved = parent_solve(whole, rhs, parts, cores)
    mine = lax.all_to_all(solved, axes, 0, 0, tiled=True).reshape(total.shape)
    parts = [mine] + [from_core(mine, cores - k) for k in range(1, cores)]
    coupled = couple(child_upper_inv, child_upper_off, mine)
    return tuple(backward(parent_of, fwd, child_upper_inv, coupled, parts, per_col))


def solution(mesh):
    n_row, n_col = (mesh.shape[a] for a in ("row", "col"))
    cores = 1 if n_col % 2 else 2
    split = Mesh(mesh.devices.reshape(n_row, n_col // cores, cores), ("row", "z", "core"))
    child = P(("row", "z", "core"), None, None)
    parent = P(("z", "core"), None, None)
    return jax.shard_map(
        on_device,
        mesh=split,
        in_specs=(child, parent, child, child, child, child, parent, parent, P(("row", "z", "core"))),
        out_specs=(child, parent),
        check_vma=False,
    )
```

```python
import functools
import math
import jax
import jax.numpy as jnp
from jax import lax
from jax.experimental import pallas as pl
from jax.experimental.pallas import tpu as pltpu
from jax.sharding import Mesh, PartitionSpec as P

F32 = jnp.float32
BF16 = jnp.bfloat16
VMEM = pl.BlockSpec(memory_space=pltpu.VMEM)
ANY = pl.BlockSpec(memory_space=pl.ANY)
MIB = 1 << 20
VMEM_BYTES = 64 * MIB
WAIT = pl.CostEstimate(flops=8 * 10**9, bytes_accessed=MIB, transcendentals=0)


def ranges(count, shares):
    ends = [count * sum(shares[: i + 1]) // sum(shares) for i in range(len(shares))]
    pairs = zip([0] + ends[:-1], ends)
    return [(lo, hi) for lo, hi in pairs if hi > lo]


def params(mib):
    return pltpu.CompilerParams(vmem_limit_bytes=mib * MIB)


def dot(a, b):
    return jnp.dot(a, b, preferred_element_type=F32)


def dot_t(a, b):
    return lax.dot_general(a, b, (((1,), (1,)), ((), ())), preferred_element_type=F32)


def forward_kernel(cores, chunk, owner_hbm, rhs_hbm, inv_hbm, off_hbm, fwd, *rest):
    mine, theirs, scratch = rest[0], rest[1:cores], rest[cores:]
    rhs, inv, off, owner, even, odd, in_sem, owner_sem = scratch
    n_row, _, half, _ = mine.shape
    groups = fwd.shape[0] // chunk
    arrays = ((rhs_hbm, rhs), (inv_hbm, inv), (off_hbm, off))

    def load(s, g):
        part = pl.ds(g * chunk, chunk)
        return pltpu.make_async_copy(arrays[s][0].at[part], arrays[s][1].at[part], in_sem.at[s, g])

    load(0, 0).start()
    load(1, 0).start()
    names = pltpu.make_async_copy(owner_hbm, owner, owner_sem)
    names.start()

    @pl.loop(1, groups)
    def _(g):
        load(0, g).start()
        load(1, g).start()
        load(2, g - 1).start()

    load(2, groups - 1).start()
    even[...] = jnp.zeros_like(even)
    odd[...] = jnp.zeros_like(odd)

    def solve(c):
        fwd[c] = dot(inv[c], rhs[c]).astype(BF16)

    def add(c, acc):
        acc[owner[c]] += dot(off[c], fwd[c])

    load(0, 0).wait()
    load(1, 0).wait()
    for n in range(chunk):
        solve(n)
    names.wait()

    def step(g):
        load(0, g).wait()
        load(1, g).wait()
        load(2, g - 1).wait()
        for n in range(chunk):
            solve(g * chunk + n)
            add((g - 1) * chunk + n, odd if n % 2 else even)

    pl.loop(1, groups - 1)(step)
    load(2, groups - 1).wait()
    if groups > 1:
        step(groups - 1)
    for n in range(chunk):
        add((groups - 1) * chunk + n, odd if n % 2 else even)
    me = lax.axis_index("core")
    for p in range(even.shape[0]):
        turned = (even[p] + odd[p]).astype(BF16).T
        for r in range(n_row):
            halves = [turned[n * half : (n + 1) * half] for n in range(r * cores, (r + 1) * cores)]
            for k in range(cores):
                out = theirs[k - 1] if k else mine
                value = halves[0]
                for n in range(1, cores):
                    value = jnp.where(lax.rem(me + k, cores) == n, halves[n], value)
                out[r, p] = value


def forward(parent_of, rhs, inv, off, n_row, n_chip, cores, per_col):
    count, width, sides = rhs.shape
    chunk = max(c for c in range(1, 13) if count % c == 0)
    parents = n_chip * cores * per_col
    piece = (n_row, parents, sides // (n_row * cores), width)
    kept = 2 * rhs.size + 2 * cores * math.prod(piece)
    room = (VMEM_BYTES - kept - MIB) // MIB
    return pl.pallas_call(
        functools.partial(forward_kernel, cores, chunk),
        out_shape=[pltpu.VMEM(rhs.shape, BF16)] + [pltpu.VMEM(piece, BF16)] * cores,
        in_specs=[ANY] * 4,
        out_specs=[VMEM] * (1 + cores),
        scratch_shapes=[
            pltpu.VMEM(rhs.shape, BF16),
            pltpu.VMEM(inv.shape, BF16),
            pltpu.VMEM(off.shape, BF16),
            pltpu.SMEM(parent_of.shape, jnp.int32),
            pltpu.VMEM((parents, width, sides), F32),
            pltpu.VMEM((parents, width, sides), F32),
            pltpu.SemaphoreType.DMA((3, count // chunk)),
            pltpu.SemaphoreType.DMA,
        ],
        compiler_params=params(room),
        name="forward",
    )(*(pltpu.with_memory_space_constraint(x, pltpu.HBM) for x in (parent_of, rhs, inv, off)))


def couple_kernel(inv, off, _, out):
    for c in range(out.shape[0]):
        out[c] = (-dot(inv[c], off[c])).astype(BF16)


def couple(inv, off, after):
    count, width, _ = inv.shape
    return pl.pallas_call(
        couple_kernel,
        out_shape=pltpu.VMEM(off.shape, BF16),
        in_specs=[VMEM, VMEM, ANY],
        out_specs=VMEM,
        compiler_params=params(16),
        cost_estimate=pl.CostEstimate(
            flops=2 * count * width**3, bytes_accessed=6 * count * width**2, transcendentals=0
        ),
        name="couple",
    )(inv, off, after)


def core_sum_kernel(*refs):
    total = refs[0][...].astype(F32)
    for part in refs[1:-2]:
        total = total + part[...].astype(F32)
    refs[-1][...] = total.astype(BF16)


def core_sum(parts, after):
    return pl.pallas_call(
        core_sum_kernel,
        out_shape=jax.ShapeDtypeStruct(parts[0].shape, BF16),
        in_specs=[VMEM] * len(parts) + [ANY],
        out_specs=VMEM,
        compiler_params=params(16),
        cost_estimate=WAIT,
        name="core_sum",
    )(*parts, after)


def prepare_kernel(rhs, lower, upper, _, whole, mine, turned):
    slab = mine.shape[1]
    rows = pl.ds(pl.multiple_of(lax.axis_index("row") * slab, slab), slab)
    for p in range(mine.shape[0]):
        whole[p] = dot(upper[p], lower[p]).astype(BF16)
        turned[...] = rhs[p].astype(F32).T
        mine[p] = turned[rows, :]


def prepare(rhs, lower, upper, after, n_row):
    per_col, width, sides = rhs.shape
    return pl.pallas_call(
        prepare_kernel,
        out_shape=[
            jax.ShapeDtypeStruct(lower.shape, BF16),
            jax.ShapeDtypeStruct((per_col, sides // n_row, width), F32),
        ],
        in_specs=[VMEM] * 3 + [ANY],
        out_specs=[VMEM, VMEM],
        scratch_shapes=[pltpu.VMEM((sides, width), F32)],
        compiler_params=params(16),
        name="prepare",
    )(rhs, lower, upper, after)


def parent_kernel(cores, whole, rhs, parts, out):
    devices, per_col, half, _ = out.shape
    for p in range(per_col):
        updates = []
        for k in range(cores):
            terms = [parts[d, p].astype(F32) for d in range(k, devices, cores)]
            while len(terms) > 1:
                pairs = zip(terms[::2], terms[1::2])
                terms = [x + y for x, y in pairs] + terms[len(terms) - len(terms) % 2 :]
            updates.append(terms[0])
        residual = (rhs[p] - jnp.concatenate(updates)).astype(BF16)
        solved = dot_t(residual, whole[p]).astype(BF16)
        for d in range(devices):
            k = d % cores
            out[d, p] = solved[k * half : (k + 1) * half]


def parent_solve(whole, rhs, parts, cores):
    return pl.pallas_call(
        functools.partial(parent_kernel, cores),
        out_shape=jax.ShapeDtypeStruct(parts.shape, BF16),
        in_specs=[VMEM] * 3,
        out_specs=VMEM,
        compiler_params=params(16),
        cost_estimate=WAIT,
        name="parent_solve",
    )(whole, rhs, parts)


def backward_kernel(cores, groups, owner, fwd, inv, coupled, *rest):
    parts, scratch = rest[:cores], rest[cores:]
    out_hbm, solved_hbm, out, picked, out_sem, solved_sem = scratch
    n_row, parents, half, _ = parts[0].shape
    per_col = solved_hbm.shape[0]
    me = lax.axis_index("core")
    for p in range(parents):
        rows = []
        for r in range(n_row):
            for n in range(cores):
                value = parts[0][r, p]
                for k in range(1, cores):
                    value = jnp.where(lax.rem(me + k, cores) == n, parts[k][r, p], value)
                rows.append(value)
        picked[p] = jnp.concatenate(rows).T
    mine = (lax.axis_index("z") * cores + me) * per_col
    solved = pltpu.make_async_copy(picked.at[pl.ds(mine, per_col)], solved_hbm, solved_sem)
    solved.start()
    stores = [solved]
    for g, (lo, hi) in enumerate(groups):
        for c in range(lo, hi):
            mats = jnp.concatenate([inv[c], coupled[c]], axis=1)
            out[c] = dot(mats, jnp.concatenate([fwd[c], picked[owner[c]]])).astype(BF16)
        part = pl.ds(lo, hi - lo)
        copy = pltpu.make_async_copy(out.at[part], out_hbm.at[part], out_sem.at[g])
        copy.start()
        stores.append(copy)
    for copy in stores:
        copy.wait()


def backward(parent_of, fwd, inv, coupled, parts, per_col):
    count, width, sides = fwd.shape
    groups = ranges(count, (1, 2, 3, 4, 5, 4, 3, 2))
    parents = parts[0].shape[1]
    return pl.pallas_call(
        functools.partial(backward_kernel, len(parts), groups),
        out_shape=[
            jax.ShapeDtypeStruct(fwd.shape, BF16),
            jax.ShapeDtypeStruct((per_col, width, sides), BF16),
        ],
        in_specs=[VMEM] * (4 + len(parts)),
        out_specs=[ANY, ANY],
        scratch_shapes=[
            pltpu.VMEM(fwd.shape, BF16),
            pltpu.VMEM((parents, width, sides), BF16),
            pltpu.SemaphoreType.DMA((len(groups),)),
            pltpu.SemaphoreType.DMA,
        ],
        compiler_params=params(32),
        name="backward",
    )(parent_of, fwd, inv, coupled, *parts)


def from_core(value, k):
    cores = lax.axis_size("core")
    return lax.ppermute(value, "core", [(i, (i + k) % cores) for i in range(cores)])


def on_device(
    child_rhs,
    parent_rhs,
    child_lower_inv,
    child_lower_off,
    child_upper_inv,
    child_upper_off,
    parent_lower_inv,
    parent_upper_inv,
    parent_of,
):
    n_row, n_chip, cores = (lax.axis_size(a) for a in ("row", "z", "core"))
    per_col = parent_rhs.shape[0]
    fwd, mine, *theirs = forward(
        parent_of, child_rhs, child_lower_inv, child_lower_off, n_row, n_chip, cores, per_col
    )
    theirs = [from_core(x, k) for k, x in enumerate(theirs, 1)]
    whole, rhs = prepare(parent_rhs, parent_lower_inv, parent_upper_inv, mine, n_row)
    total = core_sum([mine] + theirs, whole)
    axes = ("row", "z", "core")
    sent = total.reshape(-1, per_col, *total.shape[2:])
    parts = lax.all_to_all(sent, axes, 0, 0, tiled=True)
    solved = parent_solve(whole, rhs, parts, cores)
    mine = lax.all_to_all(solved, axes, 0, 0, tiled=True).reshape(total.shape)
    parts = [mine] + [from_core(mine, cores - k) for k in range(1, cores)]
    coupled = couple(child_upper_inv, child_upper_off, mine)
    return tuple(backward(parent_of, fwd, child_upper_inv, coupled, parts, per_col))


def solution(mesh):
    n_row, n_col = (mesh.shape[a] for a in ("row", "col"))
    cores = 1 if n_col % 2 else 2
    split = Mesh(mesh.devices.reshape(n_row, n_col // cores, cores), ("row", "z", "core"))
    child = P(("row", "z", "core"), None, None)
    parent = P(("z", "core"), None, None)
    return jax.shard_map(
        on_device,
        mesh=split,
        in_specs=(child, parent, child, child, child, child, parent, parent, P(("row", "z", "core"))),
        out_specs=(child, parent),
        check_vma=False,
    )
```

```python
import functools
import math
import jax
import jax.numpy as jnp
from jax import lax
from jax.experimental import pallas as pl
from jax.experimental.pallas import tpu as pltpu
from jax.sharding import Mesh, PartitionSpec as P

F32 = jnp.float32
BF16 = jnp.bfloat16
VMEM = pl.BlockSpec(memory_space=pltpu.VMEM)
ANY = pl.BlockSpec(memory_space=pl.ANY)
MIB = 1 << 20
VMEM_BYTES = 64 * MIB
WAIT = pl.CostEstimate(flops=8 * 10**9, bytes_accessed=MIB, transcendentals=0)


def ranges(count, shares):
    ends = [count * sum(shares[: i + 1]) // sum(shares) for i in range(len(shares))]
    pairs = zip([0] + ends[:-1], ends)
    return [(lo, hi) for lo, hi in pairs if hi > lo]


def params(mib):
    return pltpu.CompilerParams(vmem_limit_bytes=mib * MIB)


def dot(a, b):
    return jnp.dot(a, b, preferred_element_type=F32)


def dot_t(a, b):
    return lax.dot_general(a, b, (((1,), (1,)), ((), ())), preferred_element_type=F32)


def forward_kernel(cores, chunk, owner_hbm, rhs_hbm, inv_hbm, off_hbm, fwd, *rest):
    mine, theirs, scratch = rest[0], rest[1:cores], rest[cores:]
    rhs, inv, off, owner, acc, in_sem, owner_sem = scratch
    n_row, _, half, _ = mine.shape
    groups = fwd.shape[0] // chunk
    arrays = ((rhs_hbm, rhs), (inv_hbm, inv), (off_hbm, off))

    def load(s, g):
        part = pl.ds(g * chunk, chunk)
        return pltpu.make_async_copy(arrays[s][0].at[part], arrays[s][1].at[part], in_sem.at[s, g])

    load(0, 0).start()
    load(1, 0).start()
    names = pltpu.make_async_copy(owner_hbm, owner, owner_sem)
    names.start()

    @pl.loop(1, groups)
    def _(g):
        load(0, g).start()
        load(1, g).start()
        load(2, g - 1).start()

    load(2, groups - 1).start()
    acc[...] = jnp.zeros_like(acc)

    def solve(c):
        fwd[c] = dot(inv[c], rhs[c]).astype(BF16)

    def add(c):
        acc[owner[c]] += dot(off[c], fwd[c])

    load(0, 0).wait()
    load(1, 0).wait()
    for n in range(chunk):
        solve(n)
    names.wait()

    def step(g):
        load(0, g).wait()
        load(1, g).wait()
        load(2, g - 1).wait()
        for n in range(chunk):
            solve(g * chunk + n)
            add((g - 1) * chunk + n)

    pl.loop(1, groups - 1)(step)
    if groups > 1:
        step(groups - 1)
    load(2, groups - 1).wait()
    for n in range(chunk):
        add((groups - 1) * chunk + n)
    me = lax.axis_index("core")
    for p in range(acc.shape[0]):
        turned = acc[p].astype(BF16).T
        for r in range(n_row):
            halves = [turned[n * half : (n + 1) * half] for n in range(r * cores, (r + 1) * cores)]
            for k in range(cores):
                out = theirs[k - 1] if k else mine
                value = halves[0]
                for n in range(1, cores):
                    value = jnp.where(lax.rem(me + k, cores) == n, halves[n], value)
                out[r, p] = value


def forward(parent_of, rhs, inv, off, n_row, n_chip, cores, per_col):
    count, width, sides = rhs.shape
    chunk = max(c for c in range(1, 13) if count % c == 0)
    parents = n_chip * cores * per_col
    piece = (n_row, parents, sides // (n_row * cores), width)
    kept = 2 * rhs.size + 2 * cores * math.prod(piece)
    room = (VMEM_BYTES - kept - MIB) // MIB
    return pl.pallas_call(
        functools.partial(forward_kernel, cores, chunk),
        out_shape=[pltpu.VMEM(rhs.shape, BF16)] + [pltpu.VMEM(piece, BF16)] * cores,
        in_specs=[ANY] * 4,
        out_specs=[VMEM] * (1 + cores),
        scratch_shapes=[
            pltpu.VMEM(rhs.shape, BF16),
            pltpu.VMEM(inv.shape, BF16),
            pltpu.VMEM(off.shape, BF16),
            pltpu.SMEM(parent_of.shape, jnp.int32),
            pltpu.VMEM((parents, width, sides), F32),
            pltpu.SemaphoreType.DMA((3, count // chunk)),
            pltpu.SemaphoreType.DMA,
        ],
        compiler_params=params(room),
        name="forward",
    )(*(pltpu.with_memory_space_constraint(x, pltpu.HBM) for x in (parent_of, rhs, inv, off)))


def couple_kernel(inv, off, _, out):
    for c in range(out.shape[0]):
        out[c] = (-dot(inv[c], off[c])).astype(BF16)


def couple(inv, off, after):
    count, width, _ = inv.shape
    return pl.pallas_call(
        couple_kernel,
        out_shape=pltpu.VMEM(off.shape, BF16),
        in_specs=[VMEM, VMEM, ANY],
        out_specs=VMEM,
        compiler_params=params(16),
        cost_estimate=pl.CostEstimate(
            flops=2 * count * width**3, bytes_accessed=6 * count * width**2, transcendentals=0
        ),
        name="couple",
    )(inv, off, after)


def core_sum_kernel(*refs):
    total = refs[0][...].astype(F32)
    for part in refs[1:-2]:
        total = total + part[...].astype(F32)
    refs[-1][...] = total.astype(BF16)


def core_sum(parts, after):
    return pl.pallas_call(
        core_sum_kernel,
        out_shape=jax.ShapeDtypeStruct(parts[0].shape, BF16),
        in_specs=[VMEM] * len(parts) + [ANY],
        out_specs=VMEM,
        compiler_params=params(16),
        cost_estimate=WAIT,
        name="core_sum",
    )(*parts, after)


def prepare_kernel(rhs, lower, upper, _, whole, mine, turned):
    slab = mine.shape[1]
    rows = pl.ds(pl.multiple_of(lax.axis_index("row") * slab, slab), slab)
    for p in range(mine.shape[0]):
        whole[p] = dot(upper[p], lower[p]).astype(BF16)
        turned[...] = rhs[p].astype(F32).T
        mine[p] = turned[rows, :]


def prepare(rhs, lower, upper, after, n_row):
    per_col, width, sides = rhs.shape
    return pl.pallas_call(
        prepare_kernel,
        out_shape=[
            jax.ShapeDtypeStruct(lower.shape, BF16),
            jax.ShapeDtypeStruct((per_col, sides // n_row, width), F32),
        ],
        in_specs=[VMEM] * 3 + [ANY],
        out_specs=[VMEM, VMEM],
        scratch_shapes=[pltpu.VMEM((sides, width), F32)],
        compiler_params=params(16),
        name="prepare",
    )(rhs, lower, upper, after)


def parent_kernel(cores, whole, rhs, parts, out):
    devices, per_col, half, _ = out.shape
    for p in range(per_col):
        updates = []
        for k in range(cores):
            terms = [parts[d, p].astype(F32) for d in range(k, devices, cores)]
            while len(terms) > 1:
                pairs = zip(terms[::2], terms[1::2])
                terms = [x + y for x, y in pairs] + terms[len(terms) - len(terms) % 2 :]
            updates.append(terms[0])
        residual = (rhs[p] - jnp.concatenate(updates)).astype(BF16)
        solved = dot_t(residual, whole[p]).astype(BF16)
        for d in range(devices):
            k = d % cores
            out[d, p] = solved[k * half : (k + 1) * half]


def parent_solve(whole, rhs, parts, cores):
    return pl.pallas_call(
        functools.partial(parent_kernel, cores),
        out_shape=jax.ShapeDtypeStruct(parts.shape, BF16),
        in_specs=[VMEM] * 3,
        out_specs=VMEM,
        compiler_params=params(16),
        cost_estimate=WAIT,
        name="parent_solve",
    )(whole, rhs, parts)


def backward_kernel(cores, groups, owner, fwd, inv, coupled, *rest):
    parts, scratch = rest[:cores], rest[cores:]
    out_hbm, solved_hbm, out, picked, out_sem, solved_sem = scratch
    n_row, parents, half, _ = parts[0].shape
    per_col = solved_hbm.shape[0]
    me = lax.axis_index("core")
    for p in range(parents):
        rows = []
        for r in range(n_row):
            for n in range(cores):
                value = parts[0][r, p]
                for k in range(1, cores):
                    value = jnp.where(lax.rem(me + k, cores) == n, parts[k][r, p], value)
                rows.append(value)
        picked[p] = jnp.concatenate(rows).T
    mine = (lax.axis_index("z") * cores + me) * per_col
    solved = pltpu.make_async_copy(picked.at[pl.ds(mine, per_col)], solved_hbm, solved_sem)
    solved.start()
    stores = [solved]
    for g, (lo, hi) in enumerate(groups):
        for c in range(lo, hi):
            mats = jnp.concatenate([inv[c], coupled[c]], axis=1)
            out[c] = dot(mats, jnp.concatenate([fwd[c], picked[owner[c]]])).astype(BF16)
        part = pl.ds(lo, hi - lo)
        copy = pltpu.make_async_copy(out.at[part], out_hbm.at[part], out_sem.at[g])
        copy.start()
        stores.append(copy)
    for copy in stores:
        copy.wait()


def backward(parent_of, fwd, inv, coupled, parts, per_col):
    count, width, sides = fwd.shape
    groups = ranges(count, (1, 2, 3, 4, 5, 4, 3, 2))
    parents = parts[0].shape[1]
    return pl.pallas_call(
        functools.partial(backward_kernel, len(parts), groups),
        out_shape=[
            jax.ShapeDtypeStruct(fwd.shape, BF16),
            jax.ShapeDtypeStruct((per_col, width, sides), BF16),
        ],
        in_specs=[VMEM] * (4 + len(parts)),
        out_specs=[ANY, ANY],
        scratch_shapes=[
            pltpu.VMEM(fwd.shape, BF16),
            pltpu.VMEM((parents, width, sides), BF16),
            pltpu.SemaphoreType.DMA((len(groups),)),
            pltpu.SemaphoreType.DMA,
        ],
        compiler_params=params(32),
        name="backward",
    )(parent_of, fwd, inv, coupled, *parts)


def from_core(value, k):
    cores = lax.axis_size("core")
    return lax.ppermute(value, "core", [(i, (i + k) % cores) for i in range(cores)])


def on_device(
    child_rhs,
    parent_rhs,
    child_lower_inv,
    child_lower_off,
    child_upper_inv,
    child_upper_off,
    parent_lower_inv,
    parent_upper_inv,
    parent_of,
):
    n_row, n_chip, cores = (lax.axis_size(a) for a in ("row", "z", "core"))
    per_col = parent_rhs.shape[0]
    fwd, mine, *theirs = forward(
        parent_of, child_rhs, child_lower_inv, child_lower_off, n_row, n_chip, cores, per_col
    )
    theirs = [from_core(x, k) for k, x in enumerate(theirs, 1)]
    whole, rhs = prepare(parent_rhs, parent_lower_inv, parent_upper_inv, mine, n_row)
    total = core_sum([mine] + theirs, whole)
    axes = ("row", "z", "core")
    sent = total.reshape(-1, per_col, *total.shape[2:])
    parts = lax.all_to_all(sent, axes, 0, 0, tiled=True)
    solved = parent_solve(whole, rhs, parts, cores)
    mine = lax.all_to_all(solved, axes, 0, 0, tiled=True).reshape(total.shape)
    parts = [mine] + [from_core(mine, cores - k) for k in range(1, cores)]
    coupled = couple(child_upper_inv, child_upper_off, mine)
    return tuple(backward(parent_of, fwd, child_upper_inv, coupled, parts, per_col))


def solution(mesh):
    n_row, n_col = (mesh.shape[a] for a in ("row", "col"))
    cores = 1 if n_col % 2 else 2
    split = Mesh(mesh.devices.reshape(n_row, n_col // cores, cores), ("row", "z", "core"))
    child = P(("row", "z", "core"), None, None)
    parent = P(("z", "core"), None, None)
    return jax.shard_map(
        on_device,
        mesh=split,
        in_specs=(child, parent, child, child, child, child, parent, parent, P(("row", "z", "core"))),
        out_specs=(child, parent),
        check_vma=False,
    )
```
